32 devices in a mesh: gx: 2 (over x), gy: 4 (over y, core), dp: 4 (over z).
Axes of the slice: x: 2, y: 2, z: 4, core: 2. Of those that a mesh axis runs over, the one named last changes fastest.
Arguments:
- features: bfloat16 [4, 32, 1024, 128], P('dp', 'gx', 'gy'), may hold values from -6 to 6
- kernel: bfloat16 [3, 3, 3, 64, 64], replicated, may hold values from -0.15625 to 0.15625
- offsets: float32 [64], replicated, may hold values from -3 to 3
- upstream: bfloat16 [4, 32, 1024, 128], P('dp', 'gx', 'gy'), may hold values from -6 to 6
- grad_exponents: int32 [3, 3, 3], replicated, may hold values from -2 to 2
Outputs:
- activation: bfloat16 [4, 32, 1024, 128], P('dp', 'gx', 'gy')
- input_grad: bfloat16 [4, 32, 1024, 128], P('dp', 'gx', 'gy')
- kernel_grad: bfloat16 [3, 3, 3, 64, 64], P(None, None, None, None, 'dp')
- bias_grad: float32 [64], P('dp')
The draws below stay inside these ranges and needn't reach their ends.
All inputs are finite; a program needn't handle non-finite values.
Results may differ from the reference program's by a relative error of at most 0.007.
Values may be sent and summed in bfloat16 or wider, within the bound.
No kernel may reach another device: no remote copies, remote signals or barrier semaphores. Data moves between devices by JAX's collectives and lax.ppermute only.
A program may use at most 128 MiB of HBM per device.

```python
import jax
import jax.numpy as jnp
from jax import lax

C = 64
PLANES = 2
SAMPLES = 4
NX = 32
NY = 1024


def with_ends(array, key, low, high):
    longest = array.shape.index(max(array.shape))
    spots = []
    for shift in (0, 1):
        where = [jax.random.randint(jax.random.fold_in(key, axis), (), 0, length) for axis, length in enumerate(array.shape)]
        where[longest] = (where[longest] + shift) % array.shape[longest]
        spots.append(tuple(where))
    return array.at[spots[0]].set(low).at[spots[1]].set(high)


def shard_levels(stream_key, dims, shards, low, largest):
    loudness, own = 1.0, jax.random.fold_in(stream_key, 6)
    for position, blocks in shards:
        steps = jnp.exp(jax.random.uniform(jax.random.fold_in(own, position), (blocks,), jnp.float32, low / len(shards), largest / len(shards)))
        loudness = loudness * jnp.repeat(steps, dims[position] // blocks).reshape([-1 if axis == position else 1 for axis in range(len(dims))])
    return loudness


def scatter_about(rng, shape, spread, bound, shards=(), dtype=jnp.bfloat16):
    array = spread * jax.random.normal(rng, shape, jnp.float32)
    if shards:
        array = array * shard_levels(rng, shape, shards, -0.22, 0.18)
    return jnp.clip(array, -bound, bound).astype(dtype)


def setup_inputs(seed: int = 0) -> dict:
    key_list = jax.random.split(jax.random.key(seed), 6)
    features = scatter_about(key_list[0], (SAMPLES, NX, NY, PLANES * C), 1.0, 6.0, ((0, 4), (1, 2), (2, 4)))
    kernel = scatter_about(key_list[1], (3, 3, 3, C, C), (27 * C) ** -0.5, 0.15625)
    offsets = scatter_about(key_list[2], (C,), 0.5, 3.0, (), jnp.float32)
    upstream = scatter_about(key_list[3], (SAMPLES, NX, NY, PLANES * C), 1.0, 6.0, ((0, 4), (1, 2), (2, 4)))
    grad_exponents = with_ends(jax.random.randint(key_list[4], (3, 3, 3), -2, 3), jax.random.fold_in(key_list[4], 1), -2, 2).astype(jnp.int32)
    return dict(features=features, kernel=kernel, offsets=offsets, upstream=upstream, grad_exponents=grad_exponents)


def build_matrices(kernel):
    upper = jnp.concatenate([kernel[:, :, 1], kernel[:, :, 0]], axis=-1)
    lower = jnp.concatenate([kernel[:, :, 2], kernel[:, :, 1]], axis=-1)
    return jnp.concatenate([upper, lower], axis=2)

def reference(features, kernel, offsets, upstream, grad_exponents):
    matrices = build_matrices(kernel)
    width = features.shape[3]
    chans = width // 2
    bias_full = jnp.concatenate([offsets, offsets]).astype(jnp.float32)

    def one_sample(pair):
        sample, cotangent = pair
        size_x, size_y = (sample.shape[0], sample.shape[1])
        padded = jnp.pad(sample, ((1, 1), (1, 1), (0, 0)))
        preact = jnp.zeros((size_x * size_y, width), jnp.float32) + bias_full
        for shift_x in range(3):
            for shift_y in range(3):
                window = padded[shift_x:shift_x + size_x, shift_y:shift_y + size_y].reshape(-1, width)
                preact = preact + jnp.dot(window, matrices[shift_x, shift_y], preferred_element_type=jnp.float32)
        sigma = jax.nn.sigmoid(preact)
        activation = (preact * sigma).astype(jnp.bfloat16)
        pre_grad = (cotangent.reshape(-1, width).astype(jnp.float32) * sigma * (1.0 + preact * (1.0 - sigma))).astype(jnp.bfloat16)
        grad_pad = jnp.pad(pre_grad.reshape(size_x, size_y, width), ((1, 1), (1, 1), (0, 0)))
        input_grad = jnp.zeros((size_x * size_y, width), jnp.float32)
        blocks = []
        for shift_x in range(3):
            for shift_y in range(3):
                window = grad_pad[2 - shift_x:2 - shift_x + size_x, 2 - shift_y:2 - shift_y + size_y].reshape(-1, width)
                input_grad = input_grad + jnp.dot(window, matrices[shift_x, shift_y].T, preferred_element_type=jnp.float32)
                source = padded[shift_x:shift_x + size_x, shift_y:shift_y + size_y].reshape(-1, width)
                blocks.append(jnp.dot(source.T, pre_grad, preferred_element_type=jnp.float32))
        matrix_grad = jnp.stack(blocks).reshape(3, 3, width, width)
        bias_sum = lax.optimization_barrier(jnp.sum(pre_grad.astype(jnp.float32), axis=0))
        return (activation.reshape(size_x, size_y, width), input_grad.astype(jnp.bfloat16).reshape(size_x, size_y, width), matrix_grad, bias_sum)
    activation, input_grad, matrix_grads, bias_sums = lax.map(one_sample, (features, upstream))
    matrix_grad = lax.optimization_barrier(jnp.sum(matrix_grads, axis=0))
    bias_sum = lax.optimization_barrier(jnp.sum(bias_sums, axis=0))
    tap_low = matrix_grad[:, :, :chans, chans:]
    tap_mid = matrix_grad[:, :, :chans, :chans] + matrix_grad[:, :, chans:, chans:]
    tap_high = matrix_grad[:, :, chans:, :chans]
    tap_grad = jnp.stack([tap_low, tap_mid, tap_high], axis=2)
    count = features.shape[0] * features.shape[1] * features.shape[2] * 2
    inverse = 1.0 / jnp.sqrt(jnp.float32(count))
    scales = jnp.exp2(grad_exponents.astype(jnp.float32))[:, :, :, None, None]
    kernel_grad = (tap_grad * scales * inverse).astype(jnp.bfloat16)
    bias_grad = (bias_sum[:chans] + bias_sum[chans:]) * inverse
    return (activation, input_grad, kernel_grad, bias_grad)
```

```python
import math

import jax
import jax.numpy as jnp
from jax import lax
from jax.experimental import pallas as pl
from jax.experimental.pallas import tpu as pltpu
from jax.sharding import PartitionSpec as P

PAD = 16
RIM = 8
VMEM = pl.BlockSpec(memory_space=pltpu.VMEM)
HBM = pl.BlockSpec(memory_space=pl.ANY)


def swap(value, axis, first):
    count = lax.axis_size(axis)
    links = []
    for low in range(first, count - 1, 2):
        links += [(low, low + 1), (low + 1, low)]
    if not links:
        return jnp.zeros_like(value)
    return lax.ppermute(value, axis, links)


def exchange(value, axis, step):
    return lax.ppermute(value, axis, [(i, i ^ step) for i in range(lax.axis_size(axis))])


def build_matrices(kernel):
    upper = jnp.concatenate([kernel[:, :, 1], kernel[:, :, 0]], axis=-1)
    lower = jnp.concatenate([kernel[:, :, 2], kernel[:, :, 1]], axis=-1)
    return jnp.concatenate([upper, lower], axis=2)


def conv_rows(planes, x, weights):
    rows, width = planes.shape[1], planes.shape[2]
    stacked = jnp.concatenate([planes[x], planes[x + 1], planes[x + 2]], axis=1)
    taps = jnp.dot(stacked, weights, preferred_element_type=jnp.float32)
    return (
        pltpu.roll(taps[:, :width], 1, 0)
        + taps[:, width : 2 * width]
        + pltpu.roll(taps[:, 2 * width :], rows - 1, 0)
    )


def clear_margins(planes):
    count, rows, width = planes.shape
    blank = jnp.zeros((count, RIM, width), planes.dtype)
    planes[:, :RIM, :] = blank
    planes[:, rows - RIM :, :] = blank


def place_rims(position, near, far, place):
    @pl.when(position == 0)
    def _():
        place(far, near)

    @pl.when(position == 1)
    def _():
        place(near, far)


def main_kernel(
    f_hbm, u_hbm, y_near, y_far, x_near, x_far, w_ref, bias_ref,
    act_hbm, grad_hbm, edge_near, edge_far, keep_ref, send_ref,
    fp, up, act, grad, turned, acc, in_sem, out_sem,
):
    size_x, size_y, width = f_hbm.shape
    half = width // 2
    parts = keep_ref.shape[0]
    share = keep_ref.shape[2]
    inner = pl.ds(PAD, size_y)
    loads = []
    for x in range(size_x):
        loads.append((
            pltpu.make_async_copy(f_hbm.at[x], fp.at[x + 1, inner], in_sem.at[0, x]),
            pltpu.make_async_copy(u_hbm.at[x], up.at[x, inner], in_sem.at[1, x]),
        ))
        for copy in loads[-1]:
            copy.start()
    y_side = lax.axis_index("gy") % 2
    x_side = lax.axis_index("gx") % 2
    clear_margins(fp)
    clear_margins(up)

    def place_y(left, right):
        fp[1 : size_x + 1, PAD - RIM : PAD, :] = left[:, :RIM, :]
        fp[1 : size_x + 1, PAD + size_y : PAD + size_y + RIM, :] = right[:, :RIM, :]
        up[:, PAD - RIM : PAD, :] = left[:, RIM:, :]
        up[:, PAD + size_y : PAD + size_y + RIM, :] = right[:, RIM:, :]

    def place_x(below, above):
        fp[0] = below[...]
        fp[size_x + 1] = above[...]

    place_rims(y_side, y_near, y_far, place_y)
    place_rims(x_side, x_near, x_far, place_x)

    weights = w_ref[...]
    bias = bias_ref[...]
    bias_sum = jnp.zeros((8, width), jnp.float32)

    def turn(x):
        turned[x] = fp[x, PAD : PAD + size_y, :].T

    turn(0)
    loads[0][0].wait()
    turn(1)
    stores = []
    for x in range(size_x):
        if x + 1 < size_x:
            loads[x + 1][0].wait()
        turn(x + 2)
        preact = conv_rows(fp, x, weights) + bias
        sigma = 0.5 * jnp.tanh(0.5 * preact) + 0.5
        act[x] = (preact * sigma)[PAD : PAD + size_y].astype(jnp.bfloat16)
        loads[x][1].wait()
        cotangent = up[x].astype(jnp.float32)
        rounded = (cotangent * sigma * (1.0 + preact * (1.0 - sigma))).astype(jnp.bfloat16)
        grad[x] = rounded
        wide = rounded.astype(jnp.float32)
        rows = wide.shape[0]
        ahead = pltpu.roll(wide, rows - 1, 0)[PAD : PAD + size_y]
        behind = pltpu.roll(wide, 1, 0)[PAD : PAD + size_y]
        middle = wide[PAD : PAD + size_y]
        bias_sum = bias_sum + jnp.sum(middle.reshape(size_y // 8, 8, width), axis=0)
        shifted = jnp.concatenate([ahead, middle, behind], axis=1).astype(jnp.bfloat16)
        source = turned[x : x + 3].reshape(3 * width, size_y)
        term = jnp.dot(source, shifted, preferred_element_type=jnp.float32)
        if x == 0:
            acc[...] = term
        else:
            acc[...] += term
        stores.append(pltpu.make_async_copy(act.at[x], act_hbm.at[x], out_sem.at[0, x]))
        stores.append(pltpu.make_async_copy(grad.at[x], grad_hbm.at[x], out_sem.at[1, x]))
        stores[-2].start()
        stores[-1].start()

    def place_edges(first, second):
        second[...] = grad[size_x - 1]
        first[...] = grad[0]

    place_rims(x_side, edge_near, edge_far, place_edges)

    lane = lax.broadcasted_iota(jnp.int32, (half, width), 1)
    lower = lane < half
    column = jnp.broadcast_to(jnp.sum(bias_sum, axis=0, keepdims=True), (width, width)).T
    column = column[:half] + column[half:]
    slots, tails = [], []
    for a in range(3):
        for b in range(3):
            block = acc[a * width : (a + 1) * width, b * width : (b + 1) * width].T
            top, bottom = block[:half], block[half:]
            rolled = pltpu.roll(bottom, half, 1)
            slots.append(top + jnp.where(lower, rolled, 0.0))
            tails.append((bottom, rolled))
    for t in range(0, 9, 2):
        second = tails[t + 1][1] if t + 1 < 9 else column
        slots.append(jnp.where(lower, tails[t][0], second))
    count = len(slots) // 2

    def emit(first, second):
        for s in range(count):
            for d in range(parts):
                first[d, s] = slots[s][d * share : (d + 1) * share]
                second[d, s] = slots[count + s][d * share : (d + 1) * share]

    @pl.when(y_side == 0)
    def _():
        emit(keep_ref, send_ref)

    @pl.when(y_side == 1)
    def _():
        emit(send_ref, keep_ref)

    for copy in stores:
        copy.wait()


def back_kernel(grad_hbm, x_near, x_far, w_ref, out_hbm, gp, out, in_sem, out_sem):
    size_x = grad_hbm.shape[0]
    size_y = out.shape[1]
    loads = []
    for x in range(size_x):
        loads.append(pltpu.make_async_copy(grad_hbm.at[x], gp.at[x + 1], in_sem.at[x]))
        loads[-1].start()

    def place_x(below, above):
        gp[0] = below[...]
        gp[size_x + 1] = above[...]

    place_rims(lax.axis_index("gx") % 2, x_near, x_far, place_x)
    weights = w_ref[...]
    loads[0].wait()
    stores = []
    for x in range(size_x):
        if x + 1 < size_x:
            loads[x + 1].wait()
        out[x] = conv_rows(gp, x, weights)[PAD : PAD + size_y].astype(jnp.bfloat16)
        stores.append(pltpu.make_async_copy(out.at[x], out_hbm.at[x], out_sem.at[x]))
        stores[-1].start()
    for copy in stores:
        copy.wait()


def finish_kernel(own, other, scale_ref, grad_ref, bias_ref, both):
    side = lax.axis_index("gy") % 2
    half_slots = own.shape[0]
    both[side] = own[...]
    both[1 - side] = other[...]
    half = own.shape[2] // 2
    for s in range(2 * half_slots):
        block = both[s // half_slots, s % half_slots].T * scale_ref[s]
        rounded = block.astype(jnp.bfloat16)
        if s < 9:
            grad_ref[3 * s + 1] = rounded[:half]
            grad_ref[3 * s + 2] = rounded[half:]
        else:
            t = 2 * (s - 9)
            grad_ref[3 * t] = rounded[:half]
            if t + 1 < 9:
                grad_ref[3 * (t + 1)] = rounded[half:]
            else:
                bias_ref[...] = block[half : half + 8]


def local(features, kernel, offsets, upstream, grad_exponents):
    cells, cotangent = features[0], upstream[0]
    size_x, size_y, width = cells.shape
    half = width // 2
    rows = size_y + 2 * PAD
    parts = lax.axis_size("dp")
    share = half // parts
    y_side = lax.axis_index("gy") % 2
    x_side = lax.axis_index("gx") % 2

    def rim(start):
        return jnp.concatenate(
            [
                lax.dynamic_slice_in_dim(cells, start, RIM, axis=1),
                lax.dynamic_slice_in_dim(cotangent, start, RIM, axis=1),
            ],
            axis=1,
        )

    last = size_y - RIM
    y_near = swap(rim((1 - y_side) * last), "gy", 0)
    y_far = swap(rim(y_side * last), "gy", 1)

    def plane(index):
        near = lax.dynamic_slice_in_dim(y_near, index, 1, axis=0)[0, :RIM]
        far = lax.dynamic_slice_in_dim(y_far, index, 1, axis=0)[0, :RIM]
        body = lax.dynamic_slice_in_dim(cells, index, 1, axis=0)[0]
        blank = jnp.zeros((PAD - RIM, width), cells.dtype)
        left = jnp.where(y_side == 0, far, near)
        right = jnp.where(y_side == 0, near, far)
        return jnp.concatenate([blank, left, body, right, blank], axis=0)

    x_near = swap(plane((1 - x_side) * (size_x - 1)), "gx", 0)
    x_far = swap(plane(x_side * (size_x - 1)), "gx", 1)

    matrices = build_matrices(kernel)
    forward_weights = matrices.transpose(0, 2, 1, 3).reshape(3 * width, 3 * width)
    backward_weights = matrices[::-1, ::-1].transpose(0, 3, 1, 2).reshape(3 * width, 3 * width)
    bias = jnp.concatenate([offsets, offsets])[None, :]

    bf16, f32 = jnp.bfloat16, jnp.float32
    activation, grad, edge_near, edge_far, keep, send = pl.pallas_call(
        main_kernel,
        out_shape=(
            jax.ShapeDtypeStruct((size_x, size_y, width), bf16),
            jax.ShapeDtypeStruct((size_x, rows, width), bf16),
            jax.ShapeDtypeStruct((rows, width), bf16),
            jax.ShapeDtypeStruct((rows, width), bf16),
            jax.ShapeDtypeStruct((parts, 7, share, width), f32),
            jax.ShapeDtypeStruct((parts, 7, share, width), f32),
        ),
        in_specs=[HBM, HBM] + [VMEM] * 6,
        out_specs=(HBM, HBM) + (VMEM,) * 4,
        scratch_shapes=[
            pltpu.VMEM((size_x + 2, rows, width), bf16),
            pltpu.VMEM((size_x, rows, width), bf16),
            pltpu.VMEM((size_x, size_y, width), bf16),
            pltpu.VMEM((size_x, rows, width), bf16),
            pltpu.VMEM((size_x + 2, width, size_y), bf16),
            pltpu.VMEM((3 * width, 3 * width), f32),
            pltpu.SemaphoreType.DMA((2, size_x)),
            pltpu.SemaphoreType.DMA((2, size_x)),
        ],
        compiler_params=pltpu.CompilerParams(vmem_limit_bytes=32 * 2**20),
        name="forward_and_weight_grad",
    )(cells, cotangent, y_near, y_far, x_near, x_far, forward_weights, bias)

    back_near = swap(edge_near, "gx", 0)
    back_far = swap(edge_far, "gx", 1)
    input_grad = pl.pallas_call(
        back_kernel,
        out_shape=jax.ShapeDtypeStruct((size_x, size_y, width), bf16),
        in_specs=[HBM] + [VMEM] * 3,
        out_specs=HBM,
        scratch_shapes=[
            pltpu.VMEM((size_x + 2, rows, width), bf16),
            pltpu.VMEM((size_x, size_y, width), bf16),
            pltpu.SemaphoreType.DMA((size_x,)),
            pltpu.SemaphoreType.DMA((size_x,)),
        ],
        compiler_params=pltpu.CompilerParams(vmem_limit_bytes=32 * 2**20),
        cost_estimate=pl.CostEstimate(
            flops=2 * 9 * size_x * size_y * width * width,
            bytes_accessed=4 * size_x * size_y * width,
            transcendentals=0,
        ),
        name="input_grad",
    )(grad, back_near, back_far, backward_weights)

    total = keep + swap(send, "gy", 0)
    me = lax.axis_index("dp")
    step = 1
    while step < parts:
        paired = total.reshape(total.shape[0] // 2, 2, 7, share, width)
        bit = (me // step) % 2
        mine = lax.dynamic_index_in_dim(paired, bit, 1, keepdims=False)
        theirs = lax.dynamic_index_in_dim(paired, 1 - bit, 1, keepdims=False)
        total = mine + exchange(theirs, "dp", step)
        step *= 2
    total = total[0]
    step = 2
    while step < lax.axis_size("gy"):
        total = total + exchange(total, "gy", step)
        step *= 2
    step = 1
    while step < lax.axis_size("gx"):
        total = total + exchange(total, "gx", step)
        step *= 2
    other = swap(total, "gy", 0)

    voxels = (
        features.shape[0] * parts * size_x * lax.axis_size("gx") * size_y * lax.axis_size("gy") * 2
    )
    inverse = 1.0 / math.sqrt(voxels)
    scales = jnp.exp2(grad_exponents.astype(f32)).reshape(9, 3) * inverse
    pairs = jnp.concatenate([scales[:, 0], jnp.full((1,), inverse, f32)]).reshape(5, 2)
    scales = jnp.concatenate([scales[:, 1:], pairs])
    scales = jnp.broadcast_to(jnp.repeat(scales, half, axis=1)[:, :, None], (14, width, share))
    kernel_grad, bias_grad = pl.pallas_call(
        finish_kernel,
        out_shape=(
            jax.ShapeDtypeStruct((27, half, share), bf16),
            jax.ShapeDtypeStruct((8, share), f32),
        ),
        in_specs=[VMEM] * 3,
        out_specs=(VMEM, VMEM),
        scratch_shapes=[pltpu.VMEM((2, 7, share, width), f32)],
        name="scale_weight_grad",
    )(total, other, scales)
    return (
        activation[None],
        input_grad[None],
        kernel_grad.reshape(3, 3, 3, half, share),
        bias_grad[0],
    )


def solution(mesh):
    placed = (P("dp", "gx", "gy", None), P(), P(), P("dp", "gx", "gy", None), P())
    return jax.shard_map(
        local,
        mesh=mesh,
        in_specs=placed,
        out_specs=(
            P("dp", "gx", "gy", None),
            P("dp", "gx", "gy", None),
            P(None, None, None, None, "dp"),
            P("dp"),
        ),
        check_vma=False,
    )
```

```python
import math

import jax
import jax.numpy as jnp
from jax import lax
from jax.experimental import pallas as pl
from jax.experimental.pallas import tpu as pltpu
from jax.sharding import PartitionSpec as P

RIM = 8
PAD = 16
CHUNK = 64
SLOTS = 14
VMEM = pl.BlockSpec(memory_space=pltpu.VMEM)
SMEM = pl.BlockSpec(memory_space=pltpu.SMEM)
ANY = pl.BlockSpec(memory_space=pl.ANY)
PARAMS = pltpu.CompilerParams(vmem_limit_bytes=32 * 2**20)
BF16, F32 = jnp.bfloat16, jnp.float32


def swap(value, axis, first):
    count = lax.axis_size(axis)
    links = []
    for low in range(first, count - 1, 2):
        links += [(low, low + 1), (low + 1, low)]
    if not links:
        return jnp.zeros_like(value)
    return lax.ppermute(value, axis, links)


def exchange(value, axis, step):
    return lax.ppermute(value, axis, [(i, i ^ step) for i in range(lax.axis_size(axis))])


def weights_kernel(taps, ahead, back):
    half = taps.shape[3]
    width = 2 * half
    for out in (ahead, back):
        out[...] = jnp.zeros(out.shape, BF16)
    for a in range(3):
        for b in range(3):
            low, mid, high = taps[a, b, 0], taps[a, b, 1], taps[a, b, 2]
            block = jnp.concatenate(
                [jnp.concatenate([mid, low], axis=1), jnp.concatenate([high, mid], axis=1)], axis=0
            )
            turned = block.T
            for k in range(2):
                row, col = (a + k) * width, (3 * k + b) * width
                ahead[row : row + width, col : col + width] = block
                row, col = (2 - a + k) * width, (3 * k + 2 - b) * width
                back[row : row + width, col : col + width] = turned


def plane_taps(taps, slots, bodies, weights):
    size_y, width = bodies[0].shape
    result = jnp.dot(
        jnp.concatenate(bodies, axis=1), weights, preferred_element_type=F32
    )
    for k, p in enumerate(slots):
        for b in range(3):
            col = (3 * k + b) * width
            taps[b, p, PAD : PAD + size_y, :] = result[:, col : col + width]


def rim_taps(taps, slots, triples, weights):
    width = triples[0][0].shape[1]
    rows = 2 * RIM
    last = taps.shape[2] - PAD
    stacked = jnp.concatenate(
        [jnp.concatenate([triple[j] for triple in triples], axis=0) for j in range(3)], axis=1
    )
    result = jnp.dot(stacked, weights, preferred_element_type=F32)
    for k, p in enumerate(slots):
        for b in range(3):
            block = result[k * rows : (k + 1) * rows, b * width : (b + 1) * width]
            taps[b, p, PAD - RIM : PAD, :] = block[:RIM]
            taps[b, p, last : last + RIM, :] = block[RIM:]


def shifted_sum(taps, p, start, rows):
    return (
        taps[0, p, start - 1 : start - 1 + rows, :]
        + taps[1, p, start : start + rows, :]
        + taps[2, p, start + 1 : start + 1 + rows, :]
    )


def activate(taps, wide, p, bias, sums, u_body, u_rim, act, grad_body, grad_rim):
    size_y = taps.shape[2] - 2 * PAD
    spans = [(PAD - RIM, RIM)]
    spans += [(PAD + y, CHUNK) for y in range(0, size_y, CHUNK)]
    spans += [(PAD + size_y, RIM)]
    for start, rows in spans:
        body = rows == CHUNK
        y = start - PAD if body else (0 if start < PAD else RIM)
        preact = shifted_sum(taps, p, start, rows) + bias
        sigma = 0.5 * jnp.tanh(0.5 * preact) + 0.5
        cotangent = (u_body if body else u_rim)[y : y + rows, :].astype(F32)
        rounded = (cotangent * sigma * (1.0 + preact * (1.0 - sigma))).astype(BF16)
        exact = rounded.astype(F32)
        wide[p, start : start + rows, :] = exact
        if body:
            act[y : y + rows, :] = (preact * sigma).astype(BF16)
            grad_body[y : y + rows, :] = rounded
            sums = sums + jnp.sum(exact.reshape(rows // 8, 8, exact.shape[1]), axis=0)
        else:
            grad_rim[y : y + rows, :] = rounded
    return sums


def shifted_grads(wide, p):
    size_y = wide.shape[1] - 2 * PAD
    return jnp.concatenate(
        [wide[p, PAD + 1 - b : PAD + 1 - b + size_y, :].astype(BF16) for b in range(3)], axis=1
    )


def outer(sources, grads):
    return jnp.dot(
        jnp.concatenate([jnp.concatenate(three, axis=0) for three in sources], axis=1),
        jnp.concatenate(grads, axis=0),
        preferred_element_type=F32,
    )


def oriented(near, far, side, place):
    @pl.when(side == 0)
    def _():
        place(far, near)

    @pl.when(side == 1)
    def _():
        place(near, far)


def place_rims(y_near, y_far, f_rim, u_rim):
    def place(left, right):
        f_rim[:, :RIM, :] = left[:, :RIM, :]
        f_rim[:, RIM:, :] = right[:, :RIM, :]
        u_rim[:, :RIM, :] = left[:, RIM:, :]
        u_rim[:, RIM:, :] = right[:, RIM:, :]

    oriented(y_near, y_far, lax.axis_index("gy") % 2, place)


def inner_kernel(
    f_ref, u_ref, y_near, y_far, w_ref, bias_ref,
    act_hbm, grad_ref, rim_ref, acc_ref, sums_ref,
    f_rim, u_rim, act, taps, wide, turned, sems,
):
    size_x, size_y, width = f_ref.shape
    inner = size_x - 2
    place_rims(y_near, y_far, f_rim, u_rim)
    bias = bias_ref[...]
    rim_taps(
        taps,
        range(inner),
        [[f_rim[x + j] for j in range(3)] for x in range(inner)],
        w_ref[: 3 * width, : 3 * width],
    )
    sums = jnp.zeros((8, width), F32)
    stores = []
    pairs = range(0, inner, 2)

    def multiply(p):
        plane_taps(taps, (p, p + 1), [f_ref[p + j] for j in range(4)], w_ref[...])
        for x in range(0 if p == 0 else p + 2, p + 4):
            turned[x] = f_ref[x].T

    multiply(0)
    for p in pairs:
        if p + 2 < inner:
            multiply(p + 2)
        for q in (p, p + 1):
            sums = activate(
                taps, wide, q, bias, sums, u_ref.at[q + 1], u_rim.at[q + 1],
                act.at[q], grad_ref.at[q], rim_ref.at[q],
            )
        stores.append(
            pltpu.make_async_copy(
                act.at[pl.ds(p, 2)], act_hbm.at[pl.ds(p + 1, 2)], sems.at[p // 2]
            )
        )
        stores[-1].start()
        term = outer(
            [[turned[q + j] for j in range(3)] for q in (p, p + 1)],
            [shifted_grads(wide, q) for q in (p, p + 1)],
        )
        if p == 0:
            acc_ref[...] = term
        else:
            acc_ref[...] += term
    sums_ref[...] = sums
    for copy in stores:
        copy.wait()


def edge_kernel(
    f_ref, u_ref, y_near, y_far, x_near, x_far, w_ref, bias_ref, acc_ref, sums_ref, act_in,
    act_hbm, first_ref, last_ref, near_ref, far_ref, keep_ref, send_ref,
    f_rim, u_rim, around, act, taps, wide, acc, sems,
):
    size_x, size_y, width = f_ref.shape
    half = width // 2
    parts, _, share, _ = keep_ref.shape
    y_side = lax.axis_index("gy") % 2
    x_side = lax.axis_index("gx") % 2
    place_rims(y_near, y_far, f_rim, u_rim)

    def place(below, above):
        around[0] = below[...]
        around[1] = above[...]

    oriented(x_near, x_far, x_side, place)
    bias = bias_ref[...]
    weights = w_ref[: 3 * width, : 3 * width]
    tall = size_y + 2 * RIM
    bodies = [
        [around[0, :size_y], f_ref[0], f_ref[1]],
        [f_ref[size_x - 2], f_ref[size_x - 1], around[1, :size_y]],
    ]
    rims = [
        [around[0, size_y:tall], f_rim[0], f_rim[1]],
        [f_rim[size_x - 2], f_rim[size_x - 1], around[1, size_y:tall]],
    ]
    rim_taps(taps, (0, 1), rims, weights)
    for p in range(2):
        plane_taps(taps, (p,), bodies[p], weights)
    sums = sums_ref[...]
    outs = (first_ref, last_ref)
    places = (0, size_x - 1)
    for p in range(2):
        x = places[p]
        sums = activate(
            taps, wide, p, bias, sums, u_ref.at[x], u_rim.at[x], act.at[p],
            outs[p].at[pl.ds(0, size_y)], outs[p].at[pl.ds(size_y, 2 * RIM)],
        )
    stores = [
        pltpu.make_async_copy(act.at[p], act_hbm.at[places[p]], sems.at[p]) for p in range(2)
    ]
    for copy in stores:
        copy.start()
    acc[...] = acc_ref[...] + outer(
        [[plane.T for plane in bodies[p]] for p in range(2)],
        [shifted_grads(wide, p) for p in range(2)],
    )

    def hand(second, first):
        first[...] = first_ref[...]
        second[...] = last_ref[...]

    oriented(far_ref, near_ref, x_side, lambda low, high: hand(low, high))

    lane = lax.broadcasted_iota(jnp.int32, (half, width), 1)
    lower = lane < half
    slots, tails = [], []
    for a in range(3):
        for b in range(3):
            block = acc[a * width : (a + 1) * width, b * width : (b + 1) * width].T
            top, bottom = block[:half], block[half:]
            rolled = pltpu.roll(bottom, half, 1)
            slots.append(top + jnp.where(lower, rolled, 0.0))
            tails.append((bottom, rolled))
    for t in range(0, 8, 2):
        slots.append(jnp.where(lower, tails[t][0], tails[t + 1][1]))
    both = jnp.sum(sums, axis=0, keepdims=True)
    both = jnp.broadcast_to(both + pltpu.roll(both, half, 1), (share, width))
    spare = [
        jnp.where(
            lower[:share],
            tails[8][0][d * share : (d + 1) * share],
            pltpu.roll(both, (half - d * share) % width, 1),
        )
        for d in range(parts)
    ]

    def emit(first, second):
        for s in range(SLOTS):
            out = first if s < SLOTS // 2 else second
            for d in range(parts):
                part = spare[d] if s == SLOTS - 1 else slots[s][d * share : (d + 1) * share]
                out[d, s % (SLOTS // 2)] = part

    @pl.when(y_side == 0)
    def _():
        emit(keep_ref, send_ref)

    @pl.when(y_side == 1)
    def _():
        emit(send_ref, keep_ref)

    for copy in stores:
        copy.wait()


def back_kernel(pairs, edges, grad_ref, rim_ref, first_ref, last_ref, *refs):
    x_near, x_far = refs[:2] if edges else (None, None)
    w_ref = refs[2 * edges]
    out_hbm, out, taps, around, sems = refs[-5:]
    size_y, width = grad_ref.shape[1:]
    size_x = grad_ref.shape[0] + 2
    tall = size_y + 2 * RIM

    def body(x):
        if x == 0:
            return first_ref[:size_y]
        if x == size_x - 1:
            return last_ref[:size_y]
        if x < 0 or x >= size_x:
            return around[int(x > 0), :size_y]
        return grad_ref[x - 1]

    def rim(x):
        if x == 0:
            return first_ref[size_y:tall]
        if x == size_x - 1:
            return last_ref[size_y:tall]
        if x < 0 or x >= size_x:
            return around[int(x > 0), size_y:tall]
        return rim_ref[x - 1]

    if edges:

        def place(below, above):
            around[0] = below[...]
            around[1] = above[...]

        oriented(x_near, x_far, lax.axis_index("gx") % 2, place)
    narrow = w_ref[: 3 * width, : 3 * width]
    planes = [0, size_x - 1] if edges else [x for first in pairs for x in (first, first + 1)]
    rim_taps(taps, range(len(planes)), [[rim(x + j) for j in (-1, 0, 1)] for x in planes], narrow)
    stores = []

    def multiply(k):
        x = planes[k]
        if edges:
            for i in range(2):
                plane_taps(taps, (i,), [body(planes[i] + j) for j in (-1, 0, 1)], narrow)
        else:
            plane_taps(taps, (k, k + 1), [body(x + j) for j in (-1, 0, 1, 2)], w_ref[...])

    multiply(0)
    for k in range(0, len(planes), 2):
        if k + 2 < len(planes):
            multiply(k + 2)
        for i in (k, k + 1):
            for y in range(0, size_y, CHUNK):
                out[i, y : y + CHUNK, :] = shifted_sum(taps, i, PAD + y, CHUNK).astype(BF16)
            stores.append(
                pltpu.make_async_copy(out.at[i], out_hbm.at[planes[i]], sems.at[i])
            )
            stores[-1].start()
    for copy in stores:
        copy.wait()


def finish_kernel(inverse, own, other, exponents, grad_ref, bias_ref):
    half = own.shape[2] // 2

    def emit(first, second):
        def scaled(block, a, b, c):
            power = lax.shift_left(jnp.int32(1), exponents[a, b, c] + 2).astype(F32)
            return (block * (power * (0.25 * inverse))).astype(BF16)

        for s in range(SLOTS):
            block = (first if s < SLOTS // 2 else second)[s % (SLOTS // 2)]
            low, high = block[:, :half], pltpu.roll(block, half, 1)[:, :half]
            if s < 9:
                a, b = s // 3, s % 3
                grad_ref[3 * s + 1] = scaled(low, a, b, 1)
                grad_ref[3 * s + 2] = scaled(high, a, b, 2)
            else:
                t = 2 * (s - 9)
                grad_ref[3 * t] = scaled(low, t // 3, t % 3, 0)
                if t + 1 < 9:
                    grad_ref[3 * t + 3] = scaled(high, (t + 1) // 3, (t + 1) % 3, 0)
                else:
                    bias_ref[...] = high[:1, : bias_ref.shape[1]] * inverse

    @pl.when(lax.axis_index("gy") % 2 == 0)
    def _():
        emit(own, other)

    @pl.when(lax.axis_index("gy") % 2 == 1)
    def _():
        emit(other, own)


def shape(*dims, dtype=BF16):
    return jax.ShapeDtypeStruct(dims, dtype)


def local(features, kernel, offsets, upstream, grad_exponents):
    cells, cotangent = features[0], upstream[0]
    size_x, size_y, width = cells.shape
    half = width // 2
    tall, rows = size_y + 2 * RIM, size_y + 2 * PAD
    parts = lax.axis_size("dp")
    share = half // parts
    y_side = lax.axis_index("gy") % 2
    x_side = lax.axis_index("gx") % 2

    def rim(start):
        return jnp.concatenate(
            [
                lax.dynamic_slice_in_dim(cells, start, RIM, axis=1),
                lax.dynamic_slice_in_dim(cotangent, start, RIM, axis=1),
            ],
            axis=1,
        )

    last = size_y - RIM
    y_near = swap(rim((1 - y_side) * last), "gy", 0)
    y_far = swap(rim(y_side * last), "gy", 1)

    forward_weights, backward_weights = pl.pallas_call(
        weights_kernel,
        out_shape=(shape(4 * width, 6 * width), shape(4 * width, 6 * width)),
        in_specs=[VMEM],
        out_specs=(VMEM, VMEM),
        name="tap_matrices",
    )(kernel)
    bias = jnp.concatenate([offsets, offsets])[None, :]

    def plane(index):
        near = lax.dynamic_slice_in_dim(y_near, index, 1, axis=0)[0, :RIM]
        far = lax.dynamic_slice_in_dim(y_far, index, 1, axis=0)[0, :RIM]
        body = lax.dynamic_slice_in_dim(cells, index, 1, axis=0)[0]
        left = jnp.where(y_side == 0, far, near)
        right = jnp.where(y_side == 0, near, far)
        return jnp.concatenate([body, left, right], axis=0)

    x_near = swap(plane((1 - x_side) * (size_x - 1)), "gx", 0)
    x_far = swap(plane(x_side * (size_x - 1)), "gx", 1)

    inner = size_x - 2
    rims = [
        pltpu.VMEM((size_x, 2 * RIM, width), BF16),
        pltpu.VMEM((size_x, 2 * RIM, width), BF16),
    ]
    activation, grad, grad_rim, acc, sums = pl.pallas_call(
        inner_kernel,
        out_shape=(
            shape(size_x, size_y, width),
            shape(inner, size_y, width),
            shape(inner, 2 * RIM, width),
            shape(3 * width, 3 * width, dtype=F32),
            shape(8, width, dtype=F32),
        ),
        in_specs=[VMEM] * 6,
        out_specs=(ANY, VMEM, VMEM, VMEM, VMEM),
        scratch_shapes=rims + [
            pltpu.VMEM((inner, size_y, width), BF16),
            pltpu.VMEM((3, inner, rows, width), F32),
            pltpu.VMEM((inner, rows, width), F32),
            pltpu.VMEM((size_x, width, size_y), BF16),
            pltpu.SemaphoreType.DMA((inner // 2,)),
        ],
        compiler_params=PARAMS,
        cost_estimate=pl.CostEstimate(
            flops=2 * 18 * inner * size_y * width * width, bytes_accessed=0, transcendentals=0
        ),
        name="inner_planes",
    )(cells, cotangent, y_near, y_far, forward_weights, bias)

    activation, first, final, near, far, keep, send = pl.pallas_call(
        edge_kernel,
        out_shape=(
            shape(size_x, size_y, width),
            shape(tall, width),
            shape(tall, width),
            shape(tall, width),
            shape(tall, width),
            shape(parts, SLOTS // 2, share, width, dtype=F32),
            shape(parts, SLOTS // 2, share, width, dtype=F32),
        ),
        in_specs=[VMEM] * 10 + [ANY],
        out_specs=(ANY,) + (VMEM,) * 6,
        scratch_shapes=rims + [
            pltpu.VMEM((2, tall, width), BF16),
            pltpu.VMEM((2, size_y, width), BF16),
            pltpu.VMEM((3, 2, rows, width), F32),
            pltpu.VMEM((2, rows, width), F32),
            pltpu.VMEM((3 * width, 3 * width), F32),
            pltpu.SemaphoreType.DMA((2,)),
        ],
        input_output_aliases={10: 0},
        compiler_params=PARAMS,
        name="edge_planes",
    )(
        cells, cotangent, y_near, y_far, x_near, x_far, forward_weights, bias, acc, sums,
        activation,
    )

    back_near = swap(near, "gx", 0)
    back_far = swap(far, "gx", 1)

    def back(pairs, edges, previous, after):
        operands = [grad, grad_rim, first, final]
        operands += [back_near, back_far] if edges else []
        operands += [backward_weights]
        specs = [VMEM] * len(operands)
        aliases = {}
        if previous is not None:
            aliases = {len(operands): 0}
            operands.append(previous)
            specs.append(ANY)
        operands.append(after)
        specs.append(ANY)
        planes = 2 if edges else 2 * len(pairs)
        return pl.pallas_call(
            lambda *refs: back_kernel(pairs, edges, *refs),
            out_shape=shape(size_x, size_y, width),
            in_specs=specs,
            out_specs=ANY,
            scratch_shapes=[
                pltpu.VMEM((planes, size_y, width), BF16),
                pltpu.VMEM((3, planes, rows, width), F32),
                pltpu.VMEM((2, tall, width), BF16),
                pltpu.SemaphoreType.DMA((planes,)),
            ],
            input_output_aliases=aliases,
            compiler_params=PARAMS,
            cost_estimate=pl.CostEstimate(
                flops=2 * 9 * planes * size_y * width * width,
                bytes_accessed=0,
                transcendentals=0,
            ),
            name="input_grad",
        )(*operands)

    total = keep + swap(send, "gy", 0)
    me = lax.axis_index("dp")
    step = 1
    while step < parts:
        paired = total.reshape(total.shape[0] // 2, 2, SLOTS // 2, share, width)
        bit = (me // step) % 2
        mine = lax.dynamic_index_in_dim(paired, bit, 1, keepdims=False)
        theirs = lax.dynamic_index_in_dim(paired, 1 - bit, 1, keepdims=False)
        total = mine + exchange(theirs, "dp", step)
        step *= 2
    total = total[0]
    rounds = [("gy", 1 << i) for i in range(1, lax.axis_size("gy").bit_length() - 1)]
    rounds += [("gx", 1 << i) for i in range(lax.axis_size("gx").bit_length() - 1)]
    for axis, step in rounds:
        total = total + exchange(total, axis, step)
    other = swap(total, "gy", 0)

    starts = list(range(1, size_x - 1, 2))
    cut = (len(starts) + 1) // 2
    input_grad = back(starts[:cut], False, None, send)
    input_grad = back(starts[cut:], False, input_grad, send)
    input_grad = back([], True, input_grad, send)

    voxels = (
        features.shape[0] * parts * size_x * lax.axis_size("gx") * size_y * lax.axis_size("gy") * 2
    )
    kernel_grad, bias_grad = pl.pallas_call(
        lambda *refs: finish_kernel(1.0 / math.sqrt(voxels), *refs),
        out_shape=(shape(27, share, half), shape(1, share, dtype=F32)),
        in_specs=[VMEM, VMEM, SMEM],
        out_specs=(VMEM, VMEM),
        name="scale_weight_grad",
    )(total, other, grad_exponents)
    return (
        activation[None],
        input_grad[None],
        jnp.swapaxes(kernel_grad.reshape(3, 3, 3, share, half), 3, 4),
        bias_grad.reshape(share),
    )


def solution(mesh):
    placed = (P("dp", "gx", "gy", None), P(), P(), P("dp", "gx", "gy", None), P())
    return jax.shard_map(
        local,
        mesh=mesh,
        in_specs=placed,
        out_specs=(
            P("dp", "gx", "gy", None),
            P("dp", "gx", "gy", None),
            P(None, None, None, None, "dp"),
            P("dp"),
        ),
        check_vma=False,
    )
```

```python
import math

import jax
import jax.numpy as jnp
from jax import lax
from jax.experimental import pallas as pl
from jax.experimental.pallas import tpu as pltpu
from jax.sharding import PartitionSpec as P

RIM = 8
THIN = 2
PAD = 16
CHUNK = 64
SLOTS = 14
VMEM = pl.BlockSpec(memory_space=pltpu.VMEM)
SMEM = pl.BlockSpec(memory_space=pltpu.SMEM)
ANY = pl.BlockSpec(memory_space=pl.ANY)
BF16, F32 = jnp.bfloat16, jnp.float32


def swap(value, axis, first):
    count = lax.axis_size(axis)
    links = []
    for low in range(first, count - 1, 2):
        links += [(low, low + 1), (low + 1, low)]
    if not links:
        return jnp.zeros_like(value)
    return lax.ppermute(value, axis, links)


def exchange(value, axis, step):
    return lax.ppermute(value, axis, [(i, i ^ step) for i in range(lax.axis_size(axis))])


def tap_block(taps, a, b):
    low, mid, high = taps[a, b, 0], taps[a, b, 1], taps[a, b, 2]
    return jnp.concatenate(
        [jnp.concatenate([mid, low], axis=1), jnp.concatenate([high, mid], axis=1)], axis=0
    )


def clear_corners(out, width):
    blank = jnp.zeros((width, 3 * width), BF16)
    out[3 * width :, : 3 * width] = blank
    out[:width, 3 * width :] = blank


def bias_kernel(offsets, rim_in, bias_ref):
    bias = offsets[...].reshape(1, bias_ref.shape[1] // 2)
    bias_ref[...] = jnp.concatenate([bias, bias], axis=1)


def build_front(taps, w_ref, narrow_ref):
    width = 2 * taps.shape[3]
    clear_corners(w_ref, width)
    for a in range(3):
        for b in range(3):
            block = tap_block(taps, a, b)
            for k in range(2):
                row, col = (a + k) * width, (3 * k + b) * width
                w_ref[row : row + width, col : col + width] = block
            row, col = a * width, b * width
            narrow_ref[row : row + width, col : col + width] = block


def back_weights_kernel(inverse, taps, exponents, w_ref, scale_ref):
    half = taps.shape[3]
    width = 2 * half
    clear_corners(w_ref, width)
    for a in range(3):
        for b in range(3):
            turned = tap_block(taps, a, b).T
            for k in range(2):
                row, col = (2 - a + k) * width, (3 * k + 2 - b) * width
                w_ref[row : row + width, col : col + width] = turned
    lower = lax.broadcasted_iota(jnp.int32, (8, width), 1) < half

    def scale(t, c):
        power = lax.shift_left(jnp.int32(1), exponents[t // 3, t % 3, c] + 2)
        return power.astype(F32) * (0.25 * inverse)

    for s in range(SLOTS):
        t = 2 * (s - 9)
        if s < 9:
            low, high = scale(s, 1), scale(s, 2)
        else:
            low, high = scale(t, 0), scale(t + 1, 0) if t + 1 < 9 else inverse
        scale_ref[s] = jnp.where(lower, low, high)


def plane_taps(taps, slots, bodies, weights):
    size_y, width = bodies[0].shape
    result = jnp.dot(
        jnp.concatenate(bodies, axis=1), weights, preferred_element_type=F32
    )
    for k, p in enumerate(slots):
        for b in range(3):
            col = (3 * k + b) * width
            taps[b, p, PAD : PAD + size_y, :] = result[:, col : col + width]


def rim_taps(taps, slots, triples, weights):
    width = triples[0][0].shape[1]
    rows = 2 * RIM
    last = taps.shape[2] - PAD
    stacked = jnp.concatenate(
        [jnp.concatenate([triple[j] for triple in triples], axis=0) for j in range(3)], axis=1
    )
    result = jnp.dot(stacked, weights, preferred_element_type=F32)
    for k, p in enumerate(slots):
        for b in range(3):
            block = result[k * rows : (k + 1) * rows, b * width : (b + 1) * width]
            taps[b, p, PAD - RIM : PAD, :] = block[:RIM]
            taps[b, p, last : last + RIM, :] = block[RIM:]


def shifted_sum(taps, p, start, rows):
    return (
        taps[0, p, start - 1 : start - 1 + rows, :]
        + taps[1, p, start : start + rows, :]
        + taps[2, p, start + 1 : start + 1 + rows, :]
    )


def activate(taps, wide, p, bias, sums, u_body, u_rim, act, grad_body, grad_rim):
    size_y = taps.shape[2] - 2 * PAD
    spans = [(PAD - RIM, RIM)]
    spans += [(PAD + y, CHUNK) for y in range(0, size_y, CHUNK)]
    spans += [(PAD + size_y, RIM)]
    for start, rows in spans:
        body = rows == CHUNK
        y = start - PAD if body else (0 if start < PAD else RIM)
        preact = shifted_sum(taps, p, start, rows) + bias
        sigma = 0.5 * jnp.tanh(0.5 * preact) + 0.5
        cotangent = (u_body if body else u_rim)[y : y + rows, :].astype(F32)
        rounded = (cotangent * sigma * (1.0 + preact * (1.0 - sigma))).astype(BF16)
        exact = rounded.astype(F32)
        wide[p, start : start + rows, :] = exact
        if body:
            act[y : y + rows, :] = (preact * sigma).astype(BF16)
            grad_body[y : y + rows, :] = rounded
            sums = sums + jnp.sum(exact.reshape(rows // 8, 8, exact.shape[1]), axis=0)
        else:
            grad_rim[y : y + rows, :] = rounded
    return sums


def shifted_grads(wide, p):
    size_y = wide.shape[1] - 2 * PAD
    return jnp.concatenate(
        [wide[p, PAD + 1 - b : PAD + 1 - b + size_y, :].astype(BF16) for b in range(3)], axis=1
    )


def outer(sources, grads):
    return jnp.dot(
        jnp.concatenate([jnp.concatenate(three, axis=0) for three in sources], axis=1),
        jnp.concatenate(grads, axis=0),
        preferred_element_type=F32,
    )


def oriented(near, far, side, place):
    @pl.when(side == 0)
    def _():
        place(far, near)

    @pl.when(side == 1)
    def _():
        place(near, far)


def place_rims(y_near, y_far, f_rim, u_rim):
    for ref in (f_rim, u_rim):
        ref[...] = jnp.zeros(ref.shape, BF16)

    def place(left, right):
        f_rim[:, RIM - THIN : RIM, :] = left[:, :THIN, :]
        f_rim[:, RIM : RIM + THIN, :] = right[:, :THIN, :]
        u_rim[:, RIM - THIN : RIM, :] = left[:, THIN:, :]
        u_rim[:, RIM : RIM + THIN, :] = right[:, THIN:, :]

    oriented(y_near, y_far, lax.axis_index("gy") % 2, place)


def inner_kernel(
    f_ref, u_ref, y_near, y_far, kernel_ref, bias_ref,
    act_hbm, grad_ref, rim_ref, acc_ref, sums_ref, narrow_ref,
    f_rim, u_rim, act, taps, wide, turned, w_ref, sems,
):
    size_x, size_y, width = f_ref.shape
    build_front(kernel_ref, w_ref, narrow_ref)
    inner = size_x - 2
    place_rims(y_near, y_far, f_rim, u_rim)
    bias = bias_ref[...]
    rim_taps(
        taps,
        range(inner),
        [[f_rim[x + j] for j in range(3)] for x in range(inner)],
        w_ref[: 3 * width, : 3 * width],
    )
    sums = jnp.zeros((8, width), F32)
    stores = []
    pairs = range(0, inner, 2)

    def multiply(p):
        plane_taps(taps, (p, p + 1), [f_ref[p + j] for j in range(4)], w_ref[...])
        for x in range(0 if p == 0 else p + 2, p + 4):
            turned[x] = f_ref[x].T

    multiply(0)
    for p in pairs:
        if p + 2 < inner:
            multiply(p + 2)
        for q in (p, p + 1):
            sums = activate(
                taps, wide, q, bias, sums, u_ref.at[q + 1], u_rim.at[q + 1],
                act.at[q], grad_ref.at[q], rim_ref.at[q],
            )
        stores.append(
            pltpu.make_async_copy(
                act.at[pl.ds(p, 2)], act_hbm.at[pl.ds(p + 1, 2)], sems.at[p // 2]
            )
        )
        stores[-1].start()
        term = outer(
            [[turned[q + j] for j in range(3)] for q in (p, p + 1)],
            [shifted_grads(wide, q) for q in (p, p + 1)],
        )
        if p == 0:
            acc_ref[...] = term
        else:
            acc_ref[...] += term
    sums_ref[...] = sums
    for copy in stores:
        copy.wait()


def edge_kernel(
    f_ref, u_ref, y_near, y_far, x_near, x_far, w_ref, bias_ref, acc_ref, sums_ref, act_in,
    act_hbm, first_ref, last_ref, near_ref, far_ref, keep_ref, send_ref,
    f_rim, u_rim, around, act, taps, wide, acc, sems,
):
    size_x, size_y, width = f_ref.shape
    half = width // 2
    parts, _, share, _ = keep_ref.shape
    y_side = lax.axis_index("gy") % 2
    x_side = lax.axis_index("gx") % 2
    place_rims(y_near, y_far, f_rim, u_rim)

    def place(below, above):
        around[0] = below[...]
        around[1] = above[...]

    oriented(x_near, x_far, x_side, place)
    bias = bias_ref[...]
    weights = w_ref[...]
    tall = size_y + 2 * RIM
    bodies = [
        [around[0, :size_y], f_ref[0], f_ref[1]],
        [f_ref[size_x - 2], f_ref[size_x - 1], around[1, :size_y]],
    ]
    rims = [
        [around[0, size_y:tall], f_rim[0], f_rim[1]],
        [f_rim[size_x - 2], f_rim[size_x - 1], around[1, size_y:tall]],
    ]
    rim_taps(taps, (0, 1), rims, weights)
    for p in range(2):
        plane_taps(taps, (p,), bodies[p], weights)
    sums = sums_ref[...]
    outs = (first_ref, last_ref)
    places = (0, size_x - 1)
    for p in range(2):
        x = places[p]
        sums = activate(
            taps, wide, p, bias, sums, u_ref.at[x], u_rim.at[x], act.at[p],
            outs[p].at[pl.ds(0, size_y)], outs[p].at[pl.ds(size_y, 2 * RIM)],
        )
    stores = [
        pltpu.make_async_copy(act.at[p], act_hbm.at[places[p]], sems.at[p]) for p in range(2)
    ]
    for copy in stores:
        copy.start()
    acc[...] = acc_ref[...] + outer(
        [[plane.T for plane in bodies[p]] for p in range(2)],
        [shifted_grads(wide, p) for p in range(2)],
    )

    def hand(second, first):
        first[...] = first_ref[...]
        second[...] = last_ref[...]

    oriented(far_ref, near_ref, x_side, lambda low, high: hand(low, high))

    lane = lax.broadcasted_iota(jnp.int32, (half, width), 1)
    lower = lane < half
    slots, tails = [], []
    for a in range(3):
        for b in range(3):
            block = acc[a * width : (a + 1) * width, b * width : (b + 1) * width].T
            top, bottom = block[:half], block[half:]
            rolled = pltpu.roll(bottom, half, 1)
            slots.append(top + jnp.where(lower, rolled, 0.0))
            tails.append((bottom, rolled))
    for t in range(0, 8, 2):
        slots.append(jnp.where(lower, tails[t][0], tails[t + 1][1]))
    both = jnp.sum(sums, axis=0, keepdims=True)
    both = jnp.broadcast_to(both + pltpu.roll(both, half, 1), (share, width))
    spare = [
        jnp.where(
            lower[:share],
            tails[8][0][d * share : (d + 1) * share],
            pltpu.roll(both, (half - d * share) % width, 1),
        )
        for d in range(parts)
    ]

    def emit(first, second):
        for s in range(SLOTS):
            out = first if s < SLOTS // 2 else second
            for d in range(parts):
                part = spare[d] if s == SLOTS - 1 else slots[s][d * share : (d + 1) * share]
                out[d, s % (SLOTS // 2)] = part

    @pl.when(y_side == 0)
    def _():
        emit(keep_ref, send_ref)

    @pl.when(y_side == 1)
    def _():
        emit(send_ref, keep_ref)

    for copy in stores:
        copy.wait()


def back_kernel(pairs, edges, grad_ref, rim_ref, first_ref, last_ref, *refs):
    x_near, x_far = refs[:2] if edges else (None, None)
    w_ref = refs[2 * edges]
    out_hbm, out, taps, around, sems = refs[-5:]
    size_y, width = grad_ref.shape[1:]
    size_x = grad_ref.shape[0] + 2
    tall = size_y + 2 * RIM

    def body(x):
        if x == 0:
            return first_ref[:size_y]
        if x == size_x - 1:
            return last_ref[:size_y]
        if x < 0 or x >= size_x:
            return around[int(x > 0), :size_y]
        return grad_ref[x - 1]

    def rim(x):
        if x == 0:
            return first_ref[size_y:tall]
        if x == size_x - 1:
            return last_ref[size_y:tall]
        if x < 0 or x >= size_x:
            return around[int(x > 0), size_y:tall]
        return rim_ref[x - 1]

    if edges:

        def place(below, above):
            around[0] = below[...]
            around[1] = above[...]

        oriented(x_near, x_far, lax.axis_index("gx") % 2, place)
    narrow = w_ref[: 3 * width, : 3 * width]
    planes = [0, size_x - 1] if edges else [x for first in pairs for x in (first, first + 1)]
    rim_taps(taps, range(len(planes)), [[rim(x + j) for j in (-1, 0, 1)] for x in planes], narrow)
    stores = []

    def multiply(k):
        x = planes[k]
        if edges:
            for i in range(2):
                plane_taps(taps, (i,), [body(planes[i] + j) for j in (-1, 0, 1)], narrow)
        else:
            plane_taps(taps, (k, k + 1), [body(x + j) for j in (-1, 0, 1, 2)], w_ref[...])

    multiply(0)
    for k in range(0, len(planes), 2):
        if k + 2 < len(planes):
            multiply(k + 2)
        for i in (k, k + 1):
            for y in range(0, size_y, CHUNK):
                out[i, y : y + CHUNK, :] = shifted_sum(taps, i, PAD + y, CHUNK).astype(BF16)
            stores.append(
                pltpu.make_async_copy(out.at[i], out_hbm.at[planes[i]], sems.at[i])
            )
            stores[-1].start()
    for copy in stores:
        copy.wait()


def finish_kernel(own, other, scale_ref, grad_ref, bias_ref):
    share, half = grad_ref.shape[1:]

    def emit(first, second):
        for s in range(SLOTS):
            block = (first if s < SLOTS // 2 else second)[s % (SLOTS // 2)] * scale_ref[s, :1]
            low, high = block[:, :half], pltpu.roll(block, half, 1)[:, :half]
            t = 2 * (s - 9)
            grad_ref[3 * s + 1 if s < 9 else 3 * t] = low.astype(BF16)
            if s < SLOTS - 1:
                grad_ref[3 * s + 2 if s < 9 else 3 * t + 3] = high.astype(BF16)
            else:
                bias_ref[...] = high[:1, :share]

    @pl.when(lax.axis_index("gy") % 2 == 0)
    def _():
        emit(own, other)

    @pl.when(lax.axis_index("gy") % 2 == 1)
    def _():
        emit(other, own)


def shape(*dims, dtype=BF16):
    return jax.ShapeDtypeStruct(dims, dtype)


def grant(mebibytes):
    return pltpu.CompilerParams(vmem_limit_bytes=mebibytes * 2**20)


def cost(microseconds):
    return pl.CostEstimate(
        flops=int(1.1e9 * microseconds), bytes_accessed=0, transcendentals=0
    )


def local(features, kernel, offsets, upstream, grad_exponents):
    cells, cotangent = features[0], upstream[0]
    size_x, size_y, width = cells.shape
    half = width // 2
    tall, rows = size_y + 2 * RIM, size_y + 2 * PAD
    parts = lax.axis_size("dp")
    share = half // parts
    y_side = lax.axis_index("gy") % 2
    x_side = lax.axis_index("gx") % 2

    def rim(start):
        return jnp.concatenate(
            [
                lax.dynamic_slice_in_dim(cells, start, THIN, axis=1),
                lax.dynamic_slice_in_dim(cotangent, start, THIN, axis=1),
            ],
            axis=1,
        )

    last = size_y - THIN
    rim_near, rim_far = rim((1 - y_side) * last), rim(y_side * last)
    y_near = swap(rim_near, "gy", 0)
    y_far = swap(rim_far, "gy", 1)

    voxels = (
        features.shape[0] * parts * size_x * lax.axis_size("gx") * size_y * lax.axis_size("gy") * 2
    )
    backward_weights, scales = pl.pallas_call(
        lambda *refs: back_weights_kernel(1.0 / math.sqrt(voxels), *refs),
        out_shape=(shape(4 * width, 6 * width), shape(SLOTS, 8, width, dtype=F32)),
        in_specs=[VMEM, SMEM],
        out_specs=(VMEM, VMEM),
        compiler_params=grant(4),
        cost_estimate=cost(2.0),
        name="back_weights",
    )(kernel, grad_exponents)
    bias = pl.pallas_call(
        bias_kernel,
        out_shape=shape(1, width, dtype=F32),
        in_specs=[VMEM, ANY],
        out_specs=VMEM,
        compiler_params=grant(2),
        cost_estimate=cost(3.0),
        name="bias",
    )(offsets, rim_far)

    def plane(index):
        near = lax.dynamic_slice_in_dim(y_near, index, 1, axis=0)[0, :THIN]
        far = lax.dynamic_slice_in_dim(y_far, index, 1, axis=0)[0, :THIN]
        body = lax.dynamic_slice_in_dim(cells, index, 1, axis=0)[0]
        left = jnp.where(y_side == 0, far, near)
        right = jnp.where(y_side == 0, near, far)
        blank = jnp.zeros((RIM - THIN, width), body.dtype)
        return jnp.concatenate([body, blank, left, right, blank], axis=0)

    x_near = swap(plane((1 - x_side) * (size_x - 1)), "gx", 0)
    x_far = swap(plane(x_side * (size_x - 1)), "gx", 1)

    inner = size_x - 2
    rims = [
        pltpu.VMEM((size_x, 2 * RIM, width), BF16),
        pltpu.VMEM((size_x, 2 * RIM, width), BF16),
    ]
    activation, grad, grad_rim, acc, sums, forward_weights = pl.pallas_call(
        inner_kernel,
        out_shape=(
            shape(size_x, size_y, width),
            shape(inner, size_y, width),
            shape(inner, 2 * RIM, width),
            shape(3 * width, 3 * width, dtype=F32),
            shape(8, width, dtype=F32),
            shape(3 * width, 3 * width),
        ),
        in_specs=[VMEM] * 6,
        out_specs=(ANY,) + (VMEM,) * 5,
        scratch_shapes=rims + [
            pltpu.VMEM((inner, size_y, width), BF16),
            pltpu.VMEM((3, inner, rows, width), F32),
            pltpu.VMEM((inner, rows, width), F32),
            pltpu.VMEM((size_x, width, size_y), BF16),
            pltpu.VMEM((4 * width, 6 * width), BF16),
            pltpu.SemaphoreType.DMA((inner // 2,)),
        ],
        compiler_params=grant(24),
        cost_estimate=cost(4.0),
        name="inner_planes",
    )(cells, cotangent, y_near, y_far, kernel, bias)

    activation, first, final, near, far, keep, send = pl.pallas_call(
        edge_kernel,
        out_shape=(
            shape(size_x, size_y, width),
            shape(tall, width),
            shape(tall, width),
            shape(tall, width),
            shape(tall, width),
            shape(parts, SLOTS // 2, share, width, dtype=F32),
            shape(parts, SLOTS // 2, share, width, dtype=F32),
        ),
        in_specs=[VMEM] * 10 + [ANY],
        out_specs=(ANY,) + (VMEM,) * 6,
        scratch_shapes=rims + [
            pltpu.VMEM((2, tall, width), BF16),
            pltpu.VMEM((2, size_y, width), BF16),
            pltpu.VMEM((3, 2, rows, width), F32),
            pltpu.VMEM((2, rows, width), F32),
            pltpu.VMEM((3 * width, 3 * width), F32),
            pltpu.SemaphoreType.DMA((2,)),
        ],
        input_output_aliases={10: 0},
        compiler_params=grant(12),
        cost_estimate=cost(2.0),
        name="edge_planes",
    )(
        cells, cotangent, y_near, y_far, x_near, x_far, forward_weights, bias, acc, sums,
        activation,
    )

    back_near = swap(near, "gx", 0)
    back_far = swap(far, "gx", 1)

    def back(pairs, edges, previous, after):
        operands = [grad, grad_rim, first, final]
        operands += [back_near, back_far] if edges else []
        operands += [backward_weights]
        specs = [VMEM] * len(operands)
        aliases = {}
        if previous is not None:
            aliases = {len(operands): 0}
            operands.append(previous)
            specs.append(ANY)
        operands.append(after)
        specs.append(ANY)
        planes = 2 if edges else 2 * len(pairs)
        return pl.pallas_call(
            lambda *refs: back_kernel(pairs, edges, *refs),
            out_shape=shape(size_x, size_y, width),
            in_specs=specs,
            out_specs=ANY,
            scratch_shapes=[
                pltpu.VMEM((planes, size_y, width), BF16),
                pltpu.VMEM((3, planes, rows, width), F32),
                pltpu.VMEM((2, tall, width), BF16),
                pltpu.SemaphoreType.DMA((planes,)),
            ],
            input_output_aliases=aliases,
            compiler_params=grant(12),
            cost_estimate=cost(2.5),
            name="input_grad",
        )(*operands)

    total = keep + swap(send, "gy", 0)
    me = lax.axis_index("dp")
    step = 1
    while step < parts:
        paired = total.reshape(total.shape[0] // 2, 2, SLOTS // 2, share, width)
        bit = (me // step) % 2
        mine = lax.dynamic_index_in_dim(paired, bit, 1, keepdims=False)
        theirs = lax.dynamic_index_in_dim(paired, 1 - bit, 1, keepdims=False)
        total = mine + exchange(theirs, "dp", step)
        step *= 2
    total = total[0]
    rounds = [("gy", 1 << i) for i in range(1, lax.axis_size("gy").bit_length() - 1)]
    rounds += [("gx", 1 << i) for i in range(lax.axis_size("gx").bit_length() - 1)]
    for axis, step in rounds:
        total = total + exchange(total, axis, step)
    other = swap(total, "gy", 0)

    starts = list(range(1, size_x - 1, 2))
    cut = (len(starts) + 1) // 2
    input_grad = back(starts[:cut], False, None, send)
    input_grad = back(starts[cut:], False, input_grad, send)
    input_grad = back([], True, input_grad, send)

    kernel_grad, bias_grad = pl.pallas_call(
        finish_kernel,
        out_shape=(shape(27, share, half), shape(1, share, dtype=F32)),
        in_specs=[VMEM] * 3,
        out_specs=(VMEM, VMEM),
        compiler_params=grant(4),
        name="scale_weight_grad",
    )(total, other, scales)
    return (
        activation[None],
        input_grad[None],
        jnp.swapaxes(kernel_grad.reshape(3, 3, 3, share, half), 3, 4),
        bias_grad.reshape(share),
    )


def solution(mesh):
    placed = (P("dp", "gx", "gy", None), P(), P(), P("dp", "gx", "gy", None), P())
    return jax.shard_map(
        local,
        mesh=mesh,
        in_specs=placed,
        out_specs=(
            P("dp", "gx", "gy", None),
            P("dp", "gx", "gy", None),
            P(None, None, None, None, "dp"),
            P("dp"),
        ),
        check_vma=False,
    )
```

```python
import math

import jax
import jax.numpy as jnp
from jax import lax
from jax.experimental import pallas as pl
from jax.experimental.pallas import tpu as pltpu
from jax.sharding import PartitionSpec as P

RIM = 8
THIN = 2
PAD = 16
CHUNK = 64
SLOTS = 14
VMEM = pl.BlockSpec(memory_space=pltpu.VMEM)
SMEM = pl.BlockSpec(memory_space=pltpu.SMEM)
ANY = pl.BlockSpec(memory_space=pl.ANY)
BF16, F32 = jnp.bfloat16, jnp.float32


def swap(value, axis, first):
    count = lax.axis_size(axis)
    links = []
    for low in range(first, count, 2):
        high = (low + 1) % count
        links += [(low, high), (high, low)]
    return lax.ppermute(value, axis, links)


def exchange(value, axis, step):
    axes = ("gx", "gy", "dp")
    sizes = [lax.axis_size(name) for name in axes]
    stride = {name: math.prod(sizes[i + 1 :]) for i, name in enumerate(axes)}
    flip = (step * stride[axis]) ^ stride["gy"]
    return lax.ppermute(value, axes, [(i, i ^ flip) for i in range(math.prod(sizes))])


def half_kept():
    side = lax.axis_index("gy") % 2
    for axis, first in (("gx", 1), ("gy", 2), ("dp", 1)):
        step = first
        while step < lax.axis_size(axis):
            side = side + lax.axis_index(axis) // step
            step *= 2
    return side % 2


def tap_block(taps, a, b):
    low, mid, high = taps[a, b, 0], taps[a, b, 1], taps[a, b, 2]
    return jnp.concatenate(
        [jnp.concatenate([mid, low], axis=1), jnp.concatenate([high, mid], axis=1)], axis=0
    )


def clear_corners(out, width):
    blank = jnp.zeros((width, 3 * width), BF16)
    out[3 * width :, : 3 * width] = blank
    out[:width, 3 * width :] = blank


def build_front(taps, w_ref, narrow_ref):
    width = 2 * taps.shape[3]
    clear_corners(w_ref, width)
    for a in range(3):
        for b in range(3):
            block = tap_block(taps, a, b)
            for k in range(2):
                row, col = (a + k) * width, (3 * k + b) * width
                w_ref[row : row + width, col : col + width] = block
            row, col = a * width, b * width
            narrow_ref[row : row + width, col : col + width] = block


def back_weights_kernel(inverse, taps, exponents, w_ref, scale_ref):
    half = taps.shape[3]
    width = 2 * half
    clear_corners(w_ref, width)
    for a in range(3):
        for b in range(3):
            turned = tap_block(taps, a, b).T
            for k in range(2):
                row, col = (2 - a + k) * width, (3 * k + 2 - b) * width
                w_ref[row : row + width, col : col + width] = turned
    lower = lax.broadcasted_iota(jnp.int32, (8, width), 1) < half

    def scale(t, c):
        power = lax.shift_left(jnp.int32(1), exponents[t // 3, t % 3, c] + 2)
        return power.astype(F32) * (0.25 * inverse)

    for s in range(SLOTS):
        t = 2 * (s - 9)
        if s < 9:
            low, high = scale(s, 1), scale(s, 2)
        else:
            low, high = scale(t, 0), scale(t + 1, 0) if t + 1 < 9 else inverse
        scale_ref[s] = jnp.where(lower, low, high)


def plane_taps(taps, slots, bodies, weights):
    size_y, width = bodies[0].shape
    result = jnp.dot(
        jnp.concatenate(bodies, axis=1), weights, preferred_element_type=F32
    )
    for k, p in enumerate(slots):
        for b in range(3):
            col = (3 * k + b) * width
            taps[b, p, PAD : PAD + size_y, :] = result[:, col : col + width]


def rim_taps(taps, slots, triples, weights):
    width = triples[0][0].shape[1]
    rows = 2 * RIM
    last = taps.shape[2] - PAD
    stacked = jnp.concatenate(
        [jnp.concatenate([triple[j] for triple in triples], axis=0) for j in range(3)], axis=1
    )
    result = jnp.dot(stacked, weights, preferred_element_type=F32)
    for k, p in enumerate(slots):
        for b in range(3):
            block = result[k * rows : (k + 1) * rows, b * width : (b + 1) * width]
            taps[b, p, PAD - RIM : PAD, :] = block[:RIM]
            taps[b, p, last : last + RIM, :] = block[RIM:]


def shifted_sum(taps, p, start, rows):
    return (
        taps[0, p, start - 1 : start - 1 + rows, :]
        + taps[1, p, start : start + rows, :]
        + taps[2, p, start + 1 : start + 1 + rows, :]
    )


def activate(taps, wide, p, bias, sums, u_body, u_rim, act, grad_body, grad_rim):
    size_y = taps.shape[2] - 2 * PAD
    spans = [(PAD - RIM, RIM)]
    spans += [(PAD + y, CHUNK) for y in range(0, size_y, CHUNK)]
    spans += [(PAD + size_y, RIM)]
    for start, rows in spans:
        body = rows == CHUNK
        y = start - PAD if body else (0 if start < PAD else RIM)
        preact = shifted_sum(taps, p, start, rows) + bias
        sigma = 0.5 * jnp.tanh(0.5 * preact) + 0.5
        cotangent = (u_body if body else u_rim)[y : y + rows, :].astype(F32)
        rounded = (cotangent * sigma * (1.0 + preact * (1.0 - sigma))).astype(BF16)
        exact = rounded.astype(F32)
        wide[p, start : start + rows, :] = exact
        if body:
            act[y : y + rows, :] = (preact * sigma).astype(BF16)
            grad_body[y : y + rows, :] = rounded
            sums = sums + jnp.sum(exact.reshape(rows // 8, 8, exact.shape[1]), axis=0)
        else:
            grad_rim[y : y + rows, :] = rounded
    return sums


def shifted_grads(wide, p):
    size_y = wide.shape[1] - 2 * PAD
    return jnp.concatenate(
        [wide[p, PAD + 1 - b : PAD + 1 - b + size_y, :].astype(BF16) for b in range(3)], axis=1
    )


def outer(sources, grads):
    return jnp.dot(
        jnp.concatenate([jnp.concatenate(three, axis=0) for three in sources], axis=1),
        jnp.concatenate(grads, axis=0),
        preferred_element_type=F32,
    )


def oriented(near, far, side, place):
    @pl.when(side == 0)
    def _():
        place(far, near)

    @pl.when(side == 1)
    def _():
        place(near, far)


def beside(axis, near, far, place, clear_low, clear_high):
    index = lax.axis_index(axis)
    oriented(near, far, index % 2, place)
    pl.when(index == 0)(clear_low)
    pl.when(index == lax.axis_size(axis) - 1)(clear_high)


def place_rims(y_near, y_far, f_rim, u_rim, gap):
    low = slice(gap, gap + THIN)
    high = slice(2 * RIM - gap - THIN, 2 * RIM - gap)

    def place(left, right):
        f_rim[:, low, :] = left[:, :THIN, :]
        u_rim[:, low, :] = left[:, THIN:, :]
        f_rim[:, high, :] = right[:, :THIN, :]
        u_rim[:, high, :] = right[:, THIN:, :]

    def clear(rows):
        blank = jnp.zeros((f_rim.shape[0], THIN, f_rim.shape[2]), BF16)
        f_rim[:, rows, :] = blank
        u_rim[:, rows, :] = blank

    for ref in (f_rim, u_rim):
        ref[...] = jnp.zeros(ref.shape, BF16)
    beside("gy", y_near, y_far, place, lambda: clear(low), lambda: clear(high))


def place_planes(x_near, x_far, around):
    def place(below, above):
        around[0] = below[...]
        around[1] = above[...]

    def clear(k):
        around[k] = jnp.zeros(around.shape[1:], BF16)

    beside("gx", x_near, x_far, place, lambda: clear(0), lambda: clear(1))


def rims_kernel(ends, near_ref, far_ref):
    rows = ends.shape[1] // 2

    def hand(tail, head):
        tail[...] = ends[:, rows:, :]
        head[...] = ends[:, :rows, :]

    oriented(far_ref, near_ref, lax.axis_index("gy") % 2, hand)


def planes_kernel(f_ref, y_near, y_far, near_ref, far_ref=None):
    size_x, size_y, width = f_ref.shape
    low = slice(size_y + RIM - THIN, size_y + RIM)
    high = slice(size_y + RIM, size_y + RIM + THIN)

    def fill(out, x):
        out[:size_y] = f_ref[x]
        out[size_y:] = jnp.zeros((2 * RIM, width), BF16)

        def place(left, right):
            out[low] = left[x, :THIN]
            out[high] = right[x, :THIN]

        def clear(rows):
            out[rows] = jnp.zeros((THIN, width), BF16)

        beside("gy", y_near, y_far, place, lambda: clear(low), lambda: clear(high))

    def hand(last, first):
        if last is not None:
            fill(last, size_x - 1)
        if first is not None:
            fill(first, 0)

    oriented(far_ref, near_ref, lax.axis_index("gx") % 2, hand)


def front_kernel(
    f_ref, kernel_ref, offsets, pre_ref, turned, narrow_ref, bias_ref, w_ref, taps
):
    size_x, size_y, width = f_ref.shape
    inner = size_x - 2
    build_front(kernel_ref, w_ref, narrow_ref)
    bias = offsets[...].reshape(1, width // 2)
    bias = jnp.concatenate([bias, bias], axis=1)
    bias_ref[...] = bias
    blank = jnp.zeros((3, inner, RIM, width), F32)
    taps[:, :, PAD - RIM : PAD, :] = blank
    taps[:, :, PAD + size_y : PAD + size_y + RIM, :] = blank
    for p in range(0, inner, 2):
        plane_taps(taps, (p, p + 1), [f_ref[p + j] for j in range(4)], w_ref[...])
        for x in range(0 if p == 0 else p + 2, p + 4):
            turned[x] = f_ref[x].T
        for q in (p, p + 1):
            for y in range(0, size_y, CHUNK):
                pre_ref[q, y : y + CHUNK, :] = shifted_sum(taps, q, PAD + y, CHUNK) + bias


def gradient(preact, cotangent):
    sigma = 0.5 * jnp.tanh(0.5 * preact) + 0.5
    rounded = (
        cotangent.astype(F32) * sigma * (1.0 + preact * (1.0 - sigma))
    ).astype(BF16)
    return preact * sigma, rounded, rounded.astype(F32)


def inner_kernel(
    f_ref, u_ref, y_near, y_far, pre_ref, turned, w_ref, bias_ref,
    act_hbm, grad_ref, rim_ref, acc_ref, sums_ref,
    f_rim, u_rim, act, wide, sems,
):
    size_x, size_y, width = f_ref.shape
    inner = size_x - 2
    gap = RIM - 2 * THIN

    place_rims(y_near, y_far, f_rim, u_rim, gap)
    f_rim[:, gap + THIN : RIM, :] = f_ref[:, :THIN, :]
    f_rim[:, RIM : RIM + THIN, :] = f_ref[:, size_y - THIN :, :]
    bias = bias_ref[...]
    rows = 2 * RIM
    tall = [
        jnp.concatenate([f_rim[x + j] for x in range(inner)], axis=0) for j in range(3)
    ]
    strips = jnp.dot(
        jnp.concatenate(tall, axis=1), w_ref[...], preferred_element_type=F32
    )
    row = lax.broadcasted_iota(jnp.int32, (RIM, width), 0)
    sums = jnp.zeros((8, width), F32)
    stores = []
    for p in range(0, inner, 2):
        for q in (p, p + 1):
            strip = [
                strips[q * rows : (q + 1) * rows, b * width : (b + 1) * width] for b in range(3)
            ]
            for side in range(2):
                part = [tap[side * RIM : (side + 1) * RIM] for tap in strip]
                preact = (
                    pltpu.roll(part[0], 1, 0) + part[1] + pltpu.roll(part[2], RIM - 1, 0) + bias
                )
                _, rounded, exact = gradient(
                    preact, u_rim[q + 1, side * RIM : (side + 1) * RIM, :]
                )
                turn = THIN if side == 0 else RIM - THIN
                exact = pltpu.roll(exact, turn, 0)
                start = PAD - RIM if side == 0 else PAD + size_y
                wide[q, start : start + RIM, :] = exact
                rim_ref[q, side * RIM : (side + 1) * RIM, :] = exact.astype(BF16)
            low = jnp.where(row == 0, pltpu.roll(strip[0][:RIM], RIM - gap - THIN + 1, 0), 0.0)
            high = jnp.where(
                row == RIM - 1, pltpu.roll(strip[2][RIM:], RIM - 1 - THIN, 0), 0.0
            )
            for y in range(0, size_y, CHUNK):
                preact = pre_ref[q, y : y + CHUNK, :]
                if y == 0:
                    preact = jnp.concatenate([preact[:RIM] + low, preact[RIM:]], axis=0)
                if y + CHUNK == size_y:
                    preact = jnp.concatenate([preact[:-RIM], preact[-RIM:] + high], axis=0)
                value, rounded, exact = gradient(preact, u_ref[q + 1, y : y + CHUNK, :])
                wide[q, PAD + y : PAD + y + CHUNK, :] = exact
                act[q, y : y + CHUNK, :] = value.astype(BF16)
                grad_ref[q, y : y + CHUNK, :] = rounded
                sums = sums + jnp.sum(exact.reshape(CHUNK // 8, 8, width), axis=0)
        stores.append(
            pltpu.make_async_copy(
                act.at[pl.ds(p, 2)], act_hbm.at[pl.ds(p + 1, 2)], sems.at[p // 2]
            )
        )
        stores[-1].start()
        term = outer(
            [[turned[q + j] for j in range(3)] for q in (p, p + 1)],
            [shifted_grads(wide, q) for q in (p, p + 1)],
        )
        if p == 0:
            acc_ref[...] = term
        else:
            acc_ref[...] += term
    sums_ref[...] = sums
    for copy in stores:
        copy.wait()


def emit_half(acc, sums, out, which):
    parts, count, share, width = out.shape
    half = width // 2

    def block(t):
        a, b = t // 3, t % 3
        return acc[a * width : (a + 1) * width, b * width : (b + 1) * width].T

    def lower(rows):
        return lax.broadcasted_iota(jnp.int32, (rows, width), 1) < half

    def middle(t):
        whole = block(t)
        rolled = pltpu.roll(whole[half:], half, 1)
        return whole[:half] + jnp.where(lower(half), rolled, 0.0)

    def put(s, value):
        for d in range(parts):
            out[d, s] = value[d * share : (d + 1) * share]

    @pl.when(which == 0)
    def _():
        for s in range(count):
            put(s, middle(s))

    @pl.when(which == 1)
    def _():
        for t in range(count, 9):
            put(t - count, middle(t))
        for t in range(0, 9, 2):
            low = block(t)[half:]
            if t + 1 < 9:
                high = pltpu.roll(block(t + 1)[half:], half, 1)
                put(9 + t // 2 - count, jnp.where(lower(half), low, high))
                continue
            both = jnp.sum(sums, axis=0, keepdims=True)
            both = jnp.broadcast_to(both + pltpu.roll(both, half, 1), (share, width))
            for d in range(parts):
                turned = pltpu.roll(both, (half - d * share) % width, 1)
                mine = low[d * share : (d + 1) * share]
                out[d, count - 1] = jnp.where(lower(share), mine, turned)


def keep_kernel(acc, sums, keep_ref):
    emit_half(acc, sums[...], keep_ref, half_kept())


def edge_kernel(
    f_ref, u_ref, y_near, y_far, x_near, x_far, w_ref, bias_ref, acc_ref, sums_ref, act_in,
    act_hbm, first_ref, last_ref, near_ref, far_ref, acc, bias_sums, send_ref,
    f_rim, u_rim, around, act, taps, wide, sems,
):
    size_x, size_y, width = f_ref.shape
    x_side = lax.axis_index("gx") % 2
    place_rims(y_near, y_far, f_rim, u_rim, RIM - THIN)
    place_planes(x_near, x_far, around)
    bias = bias_ref[...]
    weights = w_ref[...]
    tall = size_y + 2 * RIM
    bodies = [
        [around[0, :size_y], f_ref[0], f_ref[1]],
        [f_ref[size_x - 2], f_ref[size_x - 1], around[1, :size_y]],
    ]
    rims = [
        [around[0, size_y:tall], f_rim[0], f_rim[1]],
        [f_rim[size_x - 2], f_rim[size_x - 1], around[1, size_y:tall]],
    ]
    rim_taps(taps, (0, 1), rims, weights)
    for p in range(2):
        plane_taps(taps, (p,), bodies[p], weights)
    sums = sums_ref[...]
    outs = (first_ref, last_ref)
    places = (0, size_x - 1)
    for p in range(2):
        x = places[p]
        sums = activate(
            taps, wide, p, bias, sums, u_ref.at[x], u_rim.at[x], act.at[p],
            outs[p].at[pl.ds(0, size_y)], outs[p].at[pl.ds(size_y, 2 * RIM)],
        )
    stores = [
        pltpu.make_async_copy(act.at[p], act_hbm.at[places[p]], sems.at[p]) for p in range(2)
    ]
    for copy in stores:
        copy.start()
    acc[...] = acc_ref[...] + outer(
        [[plane.T for plane in bodies[p]] for p in range(2)],
        [shifted_grads(wide, p) for p in range(2)],
    )

    def hand(second, first):
        first[...] = first_ref[...]
        second[...] = last_ref[...]

    oriented(far_ref, near_ref, x_side, lambda low, high: hand(low, high))

    bias_sums[...] = sums
    emit_half(acc, sums, send_ref, 1 - half_kept())
    for copy in stores:
        copy.wait()


def back_kernel(pairs, edges, grad_ref, rim_ref, first_ref, last_ref, *refs):
    x_near, x_far = refs[:2] if edges else (None, None)
    w_ref = refs[2 * edges]
    out_hbm, out, taps, around, sems = refs[-5:]
    size_y, width = grad_ref.shape[1:]
    size_x = grad_ref.shape[0] + 2
    tall = size_y + 2 * RIM

    def body(x):
        if x == 0:
            return first_ref[:size_y]
        if x == size_x - 1:
            return last_ref[:size_y]
        if x < 0 or x >= size_x:
            return around[int(x > 0), :size_y]
        return grad_ref[x - 1]

    def rim(x):
        if x == 0:
            return first_ref[size_y:tall]
        if x == size_x - 1:
            return last_ref[size_y:tall]
        if x < 0 or x >= size_x:
            return around[int(x > 0), size_y:tall]
        return rim_ref[x - 1]

    if edges:
        place_planes(x_near, x_far, around)
    narrow = w_ref[: 3 * width, : 3 * width]
    planes = [x for first in pairs for x in (first, first + 1)]
    planes += [0, size_x - 1] if edges else []
    rim_taps(taps, range(len(planes)), [[rim(x + j) for j in (-1, 0, 1)] for x in planes], narrow)
    stores = []

    def multiply(k):
        x = planes[k]
        if planes[k + 1] == x + 1:
            plane_taps(taps, (k, k + 1), [body(x + j) for j in (-1, 0, 1, 2)], w_ref[...])
        else:
            for i in (k, k + 1):
                plane_taps(taps, (i,), [body(planes[i] + j) for j in (-1, 0, 1)], narrow)

    multiply(0)
    for k in range(0, len(planes), 2):
        if k + 2 < len(planes):
            multiply(k + 2)
        for i in (k, k + 1):
            for y in range(0, size_y, CHUNK):
                out[i, y : y + CHUNK, :] = shifted_sum(taps, i, PAD + y, CHUNK).astype(BF16)
            stores.append(
                pltpu.make_async_copy(out.at[i], out_hbm.at[planes[i]], sems.at[i])
            )
            stores[-1].start()
    for copy in stores:
        copy.wait()


def split_kernel(step, mine, received, keep_ref, send_ref):
    total = mine[...] + received[...].astype(F32)
    bit = (lax.axis_index("dp") // step) % 2

    def place(first, second):
        for k in range(keep_ref.shape[0]):
            keep_ref[k] = total[2 * k + first]
            send_ref[k] = total[2 * k + second].astype(BF16)

    pl.when(bit == 0)(lambda: place(0, 1))
    pl.when(bit == 1)(lambda: place(1, 0))


def add_kernel(mine, received, total_ref):
    total_ref[...] = mine[...] + received[...].astype(F32)


def finish_kernel(own, other, scale_ref, grad_ref, bias_ref):
    share, half = grad_ref.shape[1:]

    def emit(first, second):
        for s in range(SLOTS):
            block = (first if s < SLOTS // 2 else second)[s % (SLOTS // 2)] * scale_ref[s, :1]
            low, high = block[:, :half], pltpu.roll(block, half, 1)[:, :half]
            t = 2 * (s - 9)
            grad_ref[3 * s + 1 if s < 9 else 3 * t] = low.astype(BF16)
            if s < SLOTS - 1:
                grad_ref[3 * s + 2 if s < 9 else 3 * t + 3] = high.astype(BF16)
            else:
                bias_ref[...] = high[:1, :share]

    kept = half_kept()

    @pl.when(kept == 0)
    def _():
        emit(own, other)

    @pl.when(kept == 1)
    def _():
        emit(other, own)


def shape(*dims, dtype=BF16):
    return jax.ShapeDtypeStruct(dims, dtype)


def grant(mebibytes):
    return pltpu.CompilerParams(vmem_limit_bytes=mebibytes * 2**20)


def cost(microseconds):
    return pl.CostEstimate(
        flops=int(1.1e9 * microseconds), bytes_accessed=0, transcendentals=0
    )


def local(features, kernel, offsets, upstream, grad_exponents):
    cells, cotangent = features[0], upstream[0]
    size_x, size_y, width = cells.shape
    half = width // 2
    tall, rows = size_y + 2 * RIM, size_y + 2 * PAD
    parts = lax.axis_size("dp")
    share = half // parts
    sources = (cells, cotangent)
    ends = jnp.concatenate(
        [source[:, :THIN] for source in sources] + [source[:, size_y - THIN :] for source in sources],
        axis=1,
    )
    rim_near, rim_far = pl.pallas_call(
        rims_kernel,
        out_shape=(shape(size_x, 2 * THIN, width),) * 2,
        in_specs=[VMEM],
        out_specs=(VMEM, VMEM),
        compiler_params=grant(1),
        cost_estimate=cost(3.0),
        name="pack_rims",
    )(ends)
    y_near = swap(rim_near, "gy", 0)
    y_far = swap(rim_far, "gy", 1)

    voxels = (
        features.shape[0] * parts * size_x * lax.axis_size("gx") * size_y * lax.axis_size("gy") * 2
    )
    def back_weights(taps):
        return pl.pallas_call(
            lambda *refs: back_weights_kernel(1.0 / math.sqrt(voxels), *refs),
            out_shape=(shape(4 * width, 6 * width), shape(SLOTS, 8, width, dtype=F32)),
            in_specs=[VMEM, SMEM],
            out_specs=(VMEM, VMEM),
            compiler_params=grant(4),
            cost_estimate=cost(1.0),
            name="back_weights",
        )(taps, grad_exponents)

    inner = size_x - 2
    preact, turned, forward_weights, bias = pl.pallas_call(
        front_kernel,
        out_shape=(
            shape(inner, size_y, width, dtype=F32),
            shape(size_x, width, size_y),
            shape(3 * width, 3 * width),
            shape(1, width, dtype=F32),
        ),
        in_specs=[VMEM] * 3,
        out_specs=(VMEM,) * 4,
        scratch_shapes=[
            pltpu.VMEM((4 * width, 6 * width), BF16),
            pltpu.VMEM((3, inner, rows, width), F32),
        ],
        compiler_params=grant(16),
        cost_estimate=cost(2.0),
        name="front_planes",
    )(cells, kernel, offsets)

    many = lax.axis_size("gx") > 2
    plane_sends = pl.pallas_call(
        planes_kernel,
        out_shape=(shape(tall, width),) * (1 + many),
        in_specs=[VMEM] * 3,
        out_specs=(VMEM,) * (1 + many),
        compiler_params=grant(1),
        cost_estimate=cost(0.1),
        name="pack_planes",
    )(cells, y_near, y_far)
    x_near = swap(plane_sends[0], "gx", 0)
    x_far = swap(plane_sends[1], "gx", 1) if many else x_near

    rims = [
        pltpu.VMEM((size_x, 2 * RIM, width), BF16),
        pltpu.VMEM((size_x, 2 * RIM, width), BF16),
    ]
    activation, grad, grad_rim, acc, sums = pl.pallas_call(
        inner_kernel,
        out_shape=(
            shape(size_x, size_y, width),
            shape(inner, size_y, width),
            shape(inner, 2 * RIM, width),
            shape(3 * width, 3 * width, dtype=F32),
            shape(8, width, dtype=F32),
        ),
        in_specs=[VMEM] * 8,
        out_specs=(ANY,) + (VMEM,) * 4,
        scratch_shapes=rims + [
            pltpu.VMEM((inner, size_y, width), BF16),
            pltpu.VMEM((inner, rows, width), F32),
            pltpu.SemaphoreType.DMA((inner // 2,)),
        ],
        compiler_params=grant(12),
        cost_estimate=cost(3.0),
        name="inner_planes",
    )(cells, cotangent, y_near, y_far, preact, turned, forward_weights, bias)

    activation, first, final, near, far, acc, sums, send = pl.pallas_call(
        edge_kernel,
        out_shape=(
            shape(size_x, size_y, width),
            shape(tall, width),
            shape(tall, width),
            shape(tall, width),
            shape(tall, width),
            shape(3 * width, 3 * width, dtype=F32),
            shape(8, width, dtype=F32),
            shape(parts, SLOTS // 2, share, width, dtype=F32),
        ),
        in_specs=[VMEM] * 10 + [ANY],
        out_specs=(ANY,) + (VMEM,) * 7,
        scratch_shapes=rims + [
            pltpu.VMEM((2, tall, width), BF16),
            pltpu.VMEM((2, size_y, width), BF16),
            pltpu.VMEM((3, 2, rows, width), F32),
            pltpu.VMEM((2, rows, width), F32),
            pltpu.SemaphoreType.DMA((2,)),
        ],
        input_output_aliases={10: 0},
        compiler_params=grant(12),
        cost_estimate=cost(2.0),
        name="edge_planes",
    )(
        cells, cotangent, y_near, y_far, x_near, x_far, forward_weights, bias, acc, sums,
        activation,
    )

    def back(pairs, edges, previous, after, back_near=None):
        operands = [grad, grad_rim, first, final]
        operands += [back_near, back_far] if edges else []
        operands += [backward_weights]
        specs = [VMEM] * len(operands)
        aliases = {}
        if previous is not None:
            aliases = {len(operands): 0}
            operands.append(previous)
            specs.append(ANY)
        operands.append(after)
        specs.append(ANY)
        planes = 2 * len(pairs) + 2 * edges
        return pl.pallas_call(
            lambda *refs: back_kernel(pairs, edges, *refs),
            out_shape=shape(size_x, size_y, width),
            in_specs=specs,
            out_specs=ANY,
            scratch_shapes=[
                pltpu.VMEM((planes, size_y, width), BF16),
                pltpu.VMEM((3, planes, rows, width), F32),
                pltpu.VMEM((2, tall, width), BF16),
                pltpu.SemaphoreType.DMA((planes,)),
            ],
            input_output_aliases=aliases,
            compiler_params=grant(12),
            cost_estimate=cost(2.5),
            name="input_grad",
        )(*operands)

    starts = list(range(1, size_x - 1, 2))
    cut = (len(starts) + 1) // 2
    def add(mine, received):
        return pl.pallas_call(
            add_kernel,
            out_shape=shape(*mine.shape, dtype=F32),
            in_specs=[VMEM, VMEM],
            out_specs=VMEM,
            compiler_params=grant(2),
            cost_estimate=cost(0.1),
            name="add_sums",
        )(mine, received)

    def split(mine, received, step):
        dims = (mine.shape[0] // 2,) + mine.shape[1:]
        return pl.pallas_call(
            lambda *refs: split_kernel(step, *refs),
            out_shape=(shape(*dims, dtype=F32), shape(*dims)),
            in_specs=[VMEM, VMEM],
            out_specs=(VMEM, VMEM),
            compiler_params=grant(2),
            cost_estimate=cost(0.1),
            name="split_sums",
        )(mine, received)

    rounds = [("dp", 1 << i) for i in range(parts.bit_length() - 1)]
    rounds += [("gy", 1 << i) for i in range(1, lax.axis_size("gy").bit_length() - 1)]
    rounds += [("gx", 1 << i) for i in range(lax.axis_size("gx").bit_length() - 1)]
    received = swap(send, "gy", 0)
    total = pl.pallas_call(
        keep_kernel,
        out_shape=shape(parts, SLOTS // 2, share, width, dtype=F32),
        in_specs=[VMEM, VMEM],
        out_specs=VMEM,
        compiler_params=grant(4),
        cost_estimate=cost(0.7),
        name="kept_half",
    )(acc, sums)
    input_grad = None
    for index, (axis, step) in enumerate(rounds):
        if axis == "dp":
            total, send = split(total, received, step)
        else:
            total = send = add(total, received)
        if index == 0:
            later, send = lax.optimization_barrier((kernel, send))
            backward_weights, scales = back_weights(later)
        received = exchange(send, axis, step)
        if index == 0:
            received, backward_weights = lax.optimization_barrier((received, backward_weights))
            near, far, backward_weights = lax.optimization_barrier((near, far, backward_weights))
            back_near = swap(near, "gx", 0)
            back_far = swap(far, "gx", 1) if many else back_near
        if index == len(rounds) - 2:
            input_grad = back(starts[:cut], False, None, send)
            received, input_grad = lax.optimization_barrier((received, input_grad))
        if index == len(rounds) - 1:
            input_grad = back(starts[cut:], True, input_grad, send, back_near)
            received, input_grad = lax.optimization_barrier((received, input_grad))
    total = add(total, received).reshape(SLOTS // 2, share, width)
    other = swap(total, "gy", 0)

    kernel_grad, bias_grad = pl.pallas_call(
        finish_kernel,
        out_shape=(shape(27, share, half), shape(1, share, dtype=F32)),
        in_specs=[VMEM] * 3,
        out_specs=(VMEM, VMEM),
        compiler_params=grant(4),
        name="scale_weight_grad",
    )(total, other, scales)
    return (
        activation[None],
        input_grad[None],
        jnp.swapaxes(kernel_grad.reshape(3, 3, 3, share, half), 3, 4),
        bias_grad.reshape(share),
    )


def solution(mesh):
    placed = (P("dp", "gx", "gy", None), P(), P(), P("dp", "gx", "gy", None), P())
    return jax.shard_map(
        local,
        mesh=mesh,
        in_specs=placed,
        out_specs=(
            P("dp", "gx", "gy", None),
            P("dp", "gx", "gy", None),
            P(None, None, None, None, "dp"),
            P("dp"),
        ),
        check_vma=False,
    )
```

```python
import math

import jax
import jax.numpy as jnp
from jax import lax
from jax.experimental import pallas as pl
from jax.experimental.pallas import tpu as pltpu
from jax.sharding import PartitionSpec as P

RIM = 8
THIN = 2
PAD = 16
CHUNK = 64
SLOTS = 14
VMEM = pl.BlockSpec(memory_space=pltpu.VMEM)
SMEM = pl.BlockSpec(memory_space=pltpu.SMEM)
ANY = pl.BlockSpec(memory_space=pl.ANY)
BF16, F32 = jnp.bfloat16, jnp.float32


def swap(value, axis, first):
    count = lax.axis_size(axis)
    links = []
    for low in range(first, count, 2):
        high = (low + 1) % count
        links += [(low, high), (high, low)]
    return lax.ppermute(value, axis, links)


def exchange(value, axis, step):
    axes = ("gx", "gy", "dp")
    sizes = [lax.axis_size(name) for name in axes]
    stride = {name: math.prod(sizes[i + 1 :]) for i, name in enumerate(axes)}
    flip = (step * stride[axis]) ^ stride["gy"]
    return lax.ppermute(value, axes, [(i, i ^ flip) for i in range(math.prod(sizes))])


def half_kept():
    side = lax.axis_index("gy") % 2
    for axis, first in (("gx", 1), ("gy", 2), ("dp", 1)):
        step = first
        while step < lax.axis_size(axis):
            side = side + lax.axis_index(axis) // step
            step *= 2
    return side % 2


def tap_block(taps, a, b):
    low, mid, high = taps[a, b, 0], taps[a, b, 1], taps[a, b, 2]
    return jnp.concatenate(
        [jnp.concatenate([mid, low], axis=1), jnp.concatenate([high, mid], axis=1)], axis=0
    )


def clear_corners(out, width):
    blank = jnp.zeros((width, 3 * width), BF16)
    out[3 * width :, : 3 * width] = blank
    out[:width, 3 * width :] = blank


def build_front(taps, w_ref, narrow_ref):
    width = 2 * taps.shape[3]
    clear_corners(w_ref, width)
    for a in range(3):
        for b in range(3):
            block = tap_block(taps, a, b)
            for k in range(2):
                row, col = (a + k) * width, (3 * k + b) * width
                w_ref[row : row + width, col : col + width] = block
            row, col = a * width, b * width
            narrow_ref[row : row + width, col : col + width] = block


def back_weights_kernel(inverse, taps, exponents, w_ref, scale_ref):
    half = taps.shape[3]
    width = 2 * half
    clear_corners(w_ref, width)
    for a in range(3):
        for b in range(3):
            turned = tap_block(taps, a, b).T
            for k in range(2):
                row, col = (2 - a + k) * width, (3 * k + 2 - b) * width
                w_ref[row : row + width, col : col + width] = turned
    lower = lax.broadcasted_iota(jnp.int32, (8, width), 1) < half

    def scale(t, c):
        power = lax.shift_left(jnp.int32(1), exponents[t // 3, t % 3, c] + 2)
        return power.astype(F32) * (0.25 * inverse)

    for s in range(SLOTS):
        t = 2 * (s - 9)
        if s < 9:
            low, high = scale(s, 1), scale(s, 2)
        else:
            low, high = scale(t, 0), scale(t + 1, 0) if t + 1 < 9 else inverse
        scale_ref[s] = jnp.where(lower, low, high)


def plane_taps(taps, slots, bodies, weights):
    size_y, width = bodies[0].shape
    result = jnp.dot(
        jnp.concatenate(bodies, axis=1), weights, preferred_element_type=F32
    )
    for k, p in enumerate(slots):
        for b in range(3):
            col = (3 * k + b) * width
            taps[b, p, PAD : PAD + size_y, :] = result[:, col : col + width]


def rim_taps(taps, slots, triples, weights):
    width = triples[0][0].shape[1]
    rows = 2 * RIM
    last = taps.shape[2] - PAD
    stacked = jnp.concatenate(
        [jnp.concatenate([triple[j] for triple in triples], axis=0) for j in range(3)], axis=1
    )
    result = jnp.dot(stacked, weights, preferred_element_type=F32)
    for k, p in enumerate(slots):
        for b in range(3):
            block = result[k * rows : (k + 1) * rows, b * width : (b + 1) * width]
            taps[b, p, PAD - RIM : PAD, :] = block[:RIM]
            taps[b, p, last : last + RIM, :] = block[RIM:]


def shifted_sum(taps, p, start, rows):
    return (
        taps[0, p, start - 1 : start - 1 + rows, :]
        + taps[1, p, start : start + rows, :]
        + taps[2, p, start + 1 : start + 1 + rows, :]
    )


def activate(taps, wide, p, bias, sums, u_body, u_rim, act, grad_body, grad_rim):
    size_y = taps.shape[2] - 2 * PAD
    spans = [(PAD - RIM, RIM)]
    spans += [(PAD + y, CHUNK) for y in range(0, size_y, CHUNK)]
    spans += [(PAD + size_y, RIM)]
    for start, rows in spans:
        body = rows == CHUNK
        y = start - PAD if body else (0 if start < PAD else RIM)
        preact = shifted_sum(taps, p, start, rows) + bias
        sigma = 0.5 * jnp.tanh(0.5 * preact) + 0.5
        cotangent = (u_body if body else u_rim)[y : y + rows, :].astype(F32)
        rounded = (cotangent * sigma * (1.0 + preact * (1.0 - sigma))).astype(BF16)
        exact = rounded.astype(F32)
        wide[p, start : start + rows, :] = exact
        if body:
            act[y : y + rows, :] = (preact * sigma).astype(BF16)
            grad_body[y : y + rows, :] = rounded
            sums = sums + jnp.sum(exact.reshape(rows // 8, 8, exact.shape[1]), axis=0)
        else:
            grad_rim[y : y + rows, :] = rounded
    return sums


def shifted_grads(wide, p):
    size_y = wide.shape[1] - 2 * PAD
    return jnp.concatenate(
        [wide[p, PAD + 1 - b : PAD + 1 - b + size_y, :].astype(BF16) for b in range(3)], axis=1
    )


def outer(sources, grads):
    return jnp.dot(
        jnp.concatenate([jnp.concatenate(three, axis=0) for three in sources], axis=1),
        jnp.concatenate(grads, axis=0),
        preferred_element_type=F32,
    )


def oriented(near, far, side, place):
    @pl.when(side == 0)
    def _():
        place(far, near)

    @pl.when(side == 1)
    def _():
        place(near, far)


def beside(axis, near, far, place, clear_low, clear_high):
    index = lax.axis_index(axis)
    oriented(near, far, index % 2, place)
    pl.when(index == 0)(clear_low)
    pl.when(index == lax.axis_size(axis) - 1)(clear_high)


def place_rims(y_near, y_far, f_rim, u_rim, gap):
    low = slice(gap, gap + THIN)
    high = slice(2 * RIM - gap - THIN, 2 * RIM - gap)

    def place(left, right):
        f_rim[:, low, :] = left[:, :THIN, :]
        u_rim[:, low, :] = left[:, THIN:, :]
        f_rim[:, high, :] = right[:, :THIN, :]
        u_rim[:, high, :] = right[:, THIN:, :]

    def clear(rows):
        blank = jnp.zeros((f_rim.shape[0], THIN, f_rim.shape[2]), BF16)
        f_rim[:, rows, :] = blank
        u_rim[:, rows, :] = blank

    for ref in (f_rim, u_rim):
        ref[...] = jnp.zeros(ref.shape, BF16)
    beside("gy", y_near, y_far, place, lambda: clear(low), lambda: clear(high))


def place_planes(x_near, x_far, around):
    def place(below, above):
        around[0] = below[...]
        around[1] = above[...]

    def clear(k):
        around[k] = jnp.zeros(around.shape[1:], BF16)

    beside("gx", x_near, x_far, place, lambda: clear(0), lambda: clear(1))


def rims_kernel(ends, near_ref, far_ref):
    rows = ends.shape[1] // 2

    def hand(tail, head):
        tail[...] = ends[:, rows:, :]
        head[...] = ends[:, :rows, :]

    oriented(far_ref, near_ref, lax.axis_index("gy") % 2, hand)


def planes_kernel(f_ref, y_near, y_far, near_ref, far_ref=None):
    size_x, size_y, width = f_ref.shape
    low = slice(size_y + RIM - THIN, size_y + RIM)
    high = slice(size_y + RIM, size_y + RIM + THIN)

    def fill(out, x):
        out[:size_y] = f_ref[x]
        out[size_y:] = jnp.zeros((2 * RIM, width), BF16)

        def place(left, right):
            out[low] = left[x, :THIN]
            out[high] = right[x, :THIN]

        def clear(rows):
            out[rows] = jnp.zeros((THIN, width), BF16)

        beside("gy", y_near, y_far, place, lambda: clear(low), lambda: clear(high))

    def hand(last, first):
        if last is not None:
            fill(last, size_x - 1)
        if first is not None:
            fill(first, 0)

    oriented(far_ref, near_ref, lax.axis_index("gx") % 2, hand)


def front_kernel(
    f_ref, kernel_ref, offsets, pre_ref, turned, narrow_ref, bias_ref, w_ref, taps
):
    size_x, size_y, width = f_ref.shape
    inner = size_x - 2
    build_front(kernel_ref, w_ref, narrow_ref)
    bias = offsets[...].reshape(1, width // 2)
    bias = jnp.concatenate([bias, bias], axis=1)
    bias_ref[...] = bias
    blank = jnp.zeros((3, inner, RIM, width), F32)
    taps[:, :, PAD - RIM : PAD, :] = blank
    taps[:, :, PAD + size_y : PAD + size_y + RIM, :] = blank
    for p in range(0, inner, 2):
        plane_taps(taps, (p, p + 1), [f_ref[p + j] for j in range(4)], w_ref[...])
        for x in range(0 if p == 0 else p + 2, p + 4):
            turned[x] = f_ref[x].T
        for q in (p, p + 1):
            for y in range(0, size_y, CHUNK):
                pre_ref[q, y : y + CHUNK, :] = shifted_sum(taps, q, PAD + y, CHUNK) + bias


def gradient(preact, cotangent):
    sigma = 0.5 * jnp.tanh(0.5 * preact) + 0.5
    rounded = (
        cotangent.astype(F32) * sigma * (1.0 + preact * (1.0 - sigma))
    ).astype(BF16)
    return preact * sigma, rounded, rounded.astype(F32)


def inner_kernel(
    f_ref, u_ref, y_near, y_far, pre_ref, turned, w_ref, bias_ref,
    act, grad_ref, rim_ref, acc_ref, sums_ref,
    f_rim, u_rim, wide,
):
    size_x, size_y, width = f_ref.shape
    inner = size_x - 2
    gap = RIM - 2 * THIN

    place_rims(y_near, y_far, f_rim, u_rim, gap)
    f_rim[:, gap + THIN : RIM, :] = f_ref[:, :THIN, :]
    f_rim[:, RIM : RIM + THIN, :] = f_ref[:, size_y - THIN :, :]
    bias = bias_ref[...]
    rows = 2 * RIM
    tall = [
        jnp.concatenate([f_rim[x + j] for x in range(inner)], axis=0) for j in range(3)
    ]
    strips = jnp.dot(
        jnp.concatenate(tall, axis=1), w_ref[...], preferred_element_type=F32
    )
    row = lax.broadcasted_iota(jnp.int32, (RIM, width), 0)
    sums = jnp.zeros((8, width), F32)
    for p in range(0, inner, 2):
        for q in (p, p + 1):
            strip = [
                strips[q * rows : (q + 1) * rows, b * width : (b + 1) * width] for b in range(3)
            ]
            for side in range(2):
                part = [tap[side * RIM : (side + 1) * RIM] for tap in strip]
                preact = (
                    pltpu.roll(part[0], 1, 0) + part[1] + pltpu.roll(part[2], RIM - 1, 0) + bias
                )
                _, rounded, exact = gradient(
                    preact, u_rim[q + 1, side * RIM : (side + 1) * RIM, :]
                )
                turn = THIN if side == 0 else RIM - THIN
                exact = pltpu.roll(exact, turn, 0)
                start = PAD - RIM if side == 0 else PAD + size_y
                wide[q, start : start + RIM, :] = exact
                rim_ref[q, side * RIM : (side + 1) * RIM, :] = exact.astype(BF16)
            low = jnp.where(row == 0, pltpu.roll(strip[0][:RIM], RIM - gap - THIN + 1, 0), 0.0)
            high = jnp.where(
                row == RIM - 1, pltpu.roll(strip[2][RIM:], RIM - 1 - THIN, 0), 0.0
            )
            for y in range(0, size_y, CHUNK):
                preact = pre_ref[q, y : y + CHUNK, :]
                if y == 0:
                    preact = jnp.concatenate([preact[:RIM] + low, preact[RIM:]], axis=0)
                if y + CHUNK == size_y:
                    preact = jnp.concatenate([preact[:-RIM], preact[-RIM:] + high], axis=0)
                value, rounded, exact = gradient(preact, u_ref[q + 1, y : y + CHUNK, :])
                wide[q, PAD + y : PAD + y + CHUNK, :] = exact
                act[q, y : y + CHUNK, :] = value.astype(BF16)
                grad_ref[q, y : y + CHUNK, :] = rounded
                sums = sums + jnp.sum(exact.reshape(CHUNK // 8, 8, width), axis=0)
        term = outer(
            [[turned[q + j] for j in range(3)] for q in (p, p + 1)],
            [shifted_grads(wide, q) for q in (p, p + 1)],
        )
        if p == 0:
            acc_ref[...] = term
        else:
            acc_ref[...] += term
    sums_ref[...] = sums


def emit_half(acc, sums, which, away, stay):
    outs = [out for out in (away, stay) if out is not None]
    blocks, count, share, width = outs[0].shape
    half = width // 2

    def block(t):
        a, b = t // 3, t % 3
        return acc[a * width : (a + 1) * width, b * width : (b + 1) * width].T

    def lower(rows):
        return lax.broadcasted_iota(jnp.int32, (rows, width), 1) < half

    def middle(t):
        whole = block(t)
        rolled = pltpu.roll(whole[half:], half, 1)
        return whole[:half] + jnp.where(lower(half), rolled, 0.0)

    def low_pair(t):
        low = block(t)[half:]
        if t + 1 < 9:
            return jnp.where(lower(half), low, pltpu.roll(block(t + 1)[half:], half, 1))
        both = jnp.sum(sums, axis=0, keepdims=True)
        both = jnp.broadcast_to(both + pltpu.roll(both, half, 1), (share, width))
        turned = [
            pltpu.roll(both, (half - d * share) % width, 1) for d in range(2 * blocks)
        ]
        return jnp.where(lower(half), low, jnp.concatenate(turned, axis=0))

    def write(bit):
        def put(s, value):
            for k in range(blocks):
                for out, d in ((away, 2 * k + 1 - bit), (stay, 2 * k + bit)):
                    if out is not None:
                        out[k, s] = value[d * share : (d + 1) * share]

        @pl.when(which == 0)
        def _():
            for s in range(count):
                put(s, middle(s))

        @pl.when(which == 1)
        def _():
            for t in range(count, 9):
                put(t - count, middle(t))
            for t in range(0, 9, 2):
                put(9 + t // 2 - count, low_pair(t))

    place = lax.axis_index("dp") % 2
    pl.when(place == 0)(lambda: write(0))
    pl.when(place == 1)(lambda: write(1))


def rest_kernel(acc, sums, send_stay, keep_away, keep_stay):
    kept = half_kept()
    emit_half(acc, sums[...], 1 - kept, None, send_stay)
    emit_half(acc, sums[...], kept, keep_away, keep_stay)


def edge_kernel(
    f_ref, u_ref, y_near, y_far, x_near, x_far, w_ref, bias_ref, acc_ref, sums_ref,
    act, first_ref, last_ref, acc, bias_sums, send_ref, near_ref, *refs
):
    far_ref = refs[0] if len(refs) > 5 else None
    f_rim, u_rim, around, taps, wide = refs[-5:]
    size_x, size_y, width = f_ref.shape
    x_side = lax.axis_index("gx") % 2
    place_rims(y_near, y_far, f_rim, u_rim, RIM - THIN)
    place_planes(x_near, x_far, around)
    bias = bias_ref[...]
    weights = w_ref[...]
    tall = size_y + 2 * RIM
    bodies = [
        [around[0, :size_y], f_ref[0], f_ref[1]],
        [f_ref[size_x - 2], f_ref[size_x - 1], around[1, :size_y]],
    ]
    rims = [
        [around[0, size_y:tall], f_rim[0], f_rim[1]],
        [f_rim[size_x - 2], f_rim[size_x - 1], around[1, size_y:tall]],
    ]
    rim_taps(taps, (0, 1), rims, weights)
    for p in range(2):
        plane_taps(taps, (p,), bodies[p], weights)
    sums = sums_ref[...]
    outs = (first_ref, last_ref)
    places = (0, size_x - 1)
    for p in range(2):
        x = places[p]
        sums = activate(
            taps, wide, p, bias, sums, u_ref.at[x], u_rim.at[x], act.at[p],
            outs[p].at[pl.ds(0, size_y)], outs[p].at[pl.ds(size_y, 2 * RIM)],
        )
    acc[...] = acc_ref[...] + outer(
        [[plane.T for plane in bodies[p]] for p in range(2)],
        [shifted_grads(wide, p) for p in range(2)],
    )

    def hand(last, first):
        if last is not None:
            last[...] = last_ref[...]
        if first is not None:
            first[...] = first_ref[...]

    oriented(far_ref, near_ref, x_side, hand)

    bias_sums[...] = sums
    emit_half(acc, sums, 1 - half_kept(), send_ref, None)


def store_activation(act_inner, act_edges, act_hbm, sems):
    size_x = act_hbm.shape[0]
    copies = [
        pltpu.make_async_copy(act_edges.at[0], act_hbm.at[0], sems.at[0]),
        pltpu.make_async_copy(act_edges.at[1], act_hbm.at[size_x - 1], sems.at[1]),
        pltpu.make_async_copy(act_inner, act_hbm.at[pl.ds(1, size_x - 2)], sems.at[2]),
    ]
    for copy in copies:
        copy.start()
    return copies


def back_kernel(pairs, edges, stored, grad_ref, rim_ref, first_ref, last_ref, *refs):
    x_near, x_far = refs[:2] if edges else (None, None)
    w_ref = refs[2 * edges]
    out_hbm, *act_hbm, out, taps, around, sems = refs[-5 - stored :]
    copies = []
    if stored:
        copies = store_activation(*refs[1:3], act_hbm[0], sems.at[pl.ds(out.shape[0], 3)])
    size_y, width = grad_ref.shape[1:]
    size_x = grad_ref.shape[0] + 2
    tall = size_y + 2 * RIM

    def body(x):
        if x == 0:
            return first_ref[:size_y]
        if x == size_x - 1:
            return last_ref[:size_y]
        if x < 0 or x >= size_x:
            return around[int(x > 0), :size_y]
        return grad_ref[x - 1]

    def rim(x):
        if x == 0:
            return first_ref[size_y:tall]
        if x == size_x - 1:
            return last_ref[size_y:tall]
        if x < 0 or x >= size_x:
            return around[int(x > 0), size_y:tall]
        return rim_ref[x - 1]

    if edges:
        place_planes(x_near, x_far, around)
    narrow = w_ref[: 3 * width, : 3 * width]
    planes = [x for first in pairs for x in (first, first + 1)]
    planes += [0, size_x - 1] if edges else []
    rim_taps(taps, range(len(planes)), [[rim(x + j) for j in (-1, 0, 1)] for x in planes], narrow)
    stores = []

    def multiply(k):
        x = planes[k]
        if planes[k + 1] == x + 1:
            plane_taps(taps, (k, k + 1), [body(x + j) for j in (-1, 0, 1, 2)], w_ref[...])
        else:
            for i in (k, k + 1):
                plane_taps(taps, (i,), [body(planes[i] + j) for j in (-1, 0, 1)], narrow)

    multiply(0)
    for k in range(0, len(planes), 2):
        if k + 2 < len(planes):
            multiply(k + 2)
        for i in (k, k + 1):
            for y in range(0, size_y, CHUNK):
                out[i, y : y + CHUNK, :] = shifted_sum(taps, i, PAD + y, CHUNK).astype(BF16)
            stores.append(
                pltpu.make_async_copy(out.at[i], out_hbm.at[planes[i]], sems.at[i])
            )
            stores[-1].start()
    for copy in stores + copies:
        copy.wait()


def split_kernel(step, *refs):
    *terms, keep_ref, send_ref = refs
    total = sum_refs(terms)
    bit = (lax.axis_index("dp") // step) % 2

    def place(first, second):
        for k in range(keep_ref.shape[0]):
            keep_ref[k] = total[2 * k + first]
            send_ref[k] = total[2 * k + second].astype(BF16)

    pl.when(bit == 0)(lambda: place(0, 1))
    pl.when(bit == 1)(lambda: place(1, 0))


def sum_refs(terms):
    total = terms[0][...].astype(F32)
    for term in terms[1:]:
        total = total + term[...].astype(F32)
    return total


def add_kernel(*refs):
    *terms, total_ref = refs
    total_ref[...] = sum_refs(terms).astype(total_ref.dtype)


def finish_kernel(own, other, scale_ref, grad_ref, bias_ref):
    share, half = grad_ref.shape[1:]

    def emit(first, second):
        for s in range(SLOTS):
            block = (first if s < SLOTS // 2 else second)[s % (SLOTS // 2)] * scale_ref[s, :1]
            low, high = block[:, :half], pltpu.roll(block, half, 1)[:, :half]
            t = 2 * (s - 9)
            grad_ref[3 * s + 1 if s < 9 else 3 * t] = low.astype(BF16)
            if s < SLOTS - 1:
                grad_ref[3 * s + 2 if s < 9 else 3 * t + 3] = high.astype(BF16)
            else:
                bias_ref[...] = high[:1, :share]

    kept = half_kept()

    @pl.when(kept == 0)
    def _():
        emit(own, other)

    @pl.when(kept == 1)
    def _():
        emit(other, own)


def shape(*dims, dtype=BF16):
    return jax.ShapeDtypeStruct(dims, dtype)


def grant(mebibytes):
    return pltpu.CompilerParams(vmem_limit_bytes=mebibytes * 2**20)


def cost(microseconds):
    return pl.CostEstimate(
        flops=int(1.1e9 * microseconds), bytes_accessed=0, transcendentals=0
    )


def local(features, kernel, offsets, upstream, grad_exponents):
    cells, cotangent = features[0], upstream[0]
    size_x, size_y, width = cells.shape
    half = width // 2
    tall, rows = size_y + 2 * RIM, size_y + 2 * PAD
    parts = lax.axis_size("dp")
    share = half // parts
    sources = (cells, cotangent)
    ends = jnp.concatenate(
        [source[:, :THIN] for source in sources] + [source[:, size_y - THIN :] for source in sources],
        axis=1,
    )
    rim_near, rim_far = pl.pallas_call(
        rims_kernel,
        out_shape=(shape(size_x, 2 * THIN, width),) * 2,
        in_specs=[VMEM],
        out_specs=(VMEM, VMEM),
        compiler_params=grant(1),
        cost_estimate=cost(3.0),
        name="pack_rims",
    )(ends)
    y_near = swap(rim_near, "gy", 0)
    y_far = swap(rim_far, "gy", 1)

    voxels = (
        features.shape[0] * parts * size_x * lax.axis_size("gx") * size_y * lax.axis_size("gy") * 2
    )
    def back_weights(taps):
        return pl.pallas_call(
            lambda *refs: back_weights_kernel(1.0 / math.sqrt(voxels), *refs),
            out_shape=(shape(4 * width, 6 * width), shape(SLOTS, 8, width, dtype=F32)),
            in_specs=[VMEM, SMEM],
            out_specs=(VMEM, VMEM),
            compiler_params=grant(4),
            cost_estimate=cost(1.0),
            name="back_weights",
        )(taps, grad_exponents)

    inner = size_x - 2
    preact, turned, forward_weights, bias = pl.pallas_call(
        front_kernel,
        out_shape=(
            shape(inner, size_y, width, dtype=F32),
            shape(size_x, width, size_y),
            shape(3 * width, 3 * width),
            shape(1, width, dtype=F32),
        ),
        in_specs=[VMEM] * 3,
        out_specs=(VMEM,) * 4,
        scratch_shapes=[
            pltpu.VMEM((4 * width, 6 * width), BF16),
            pltpu.VMEM((3, inner, rows, width), F32),
        ],
        compiler_params=grant(16),
        cost_estimate=cost(2.0),
        name="front_planes",
    )(cells, kernel, offsets)

    many = lax.axis_size("gx") > 2
    plane_sends = pl.pallas_call(
        planes_kernel,
        out_shape=(shape(tall, width),) * (1 + many),
        in_specs=[VMEM] * 3,
        out_specs=(VMEM,) * (1 + many),
        compiler_params=grant(1),
        cost_estimate=cost(0.1),
        name="pack_planes",
    )(cells, y_near, y_far)
    x_near = swap(plane_sends[0], "gx", 0)
    x_far = swap(plane_sends[1], "gx", 1) if many else x_near

    rims = [
        pltpu.VMEM((size_x, 2 * RIM, width), BF16),
        pltpu.VMEM((size_x, 2 * RIM, width), BF16),
    ]
    act_inner, grad, grad_rim, acc, sums = pl.pallas_call(
        inner_kernel,
        out_shape=(
            shape(inner, size_y, width),
            shape(inner, size_y, width),
            shape(inner, 2 * RIM, width),
            shape(3 * width, 3 * width, dtype=F32),
            shape(8, width, dtype=F32),
        ),
        in_specs=[VMEM] * 8,
        out_specs=(VMEM,) * 5,
        scratch_shapes=rims + [pltpu.VMEM((inner, rows, width), F32)],
        compiler_params=grant(12),
        cost_estimate=cost(3.0),
        name="inner_planes",
    )(cells, cotangent, y_near, y_far, preact, turned, forward_weights, bias)

    blocks = (parts // 2, SLOTS // 2, share, width)
    act_edges, first, final, acc, sums, send, *edges = pl.pallas_call(
        edge_kernel,
        out_shape=(
            shape(2, size_y, width),
            shape(tall, width),
            shape(tall, width),
            shape(3 * width, 3 * width, dtype=F32),
            shape(8, width, dtype=F32),
            shape(*blocks, dtype=F32),
        )
        + (shape(tall, width),) * (1 + many),
        in_specs=[VMEM] * 10,
        out_specs=(VMEM,) * (7 + many),
        scratch_shapes=rims + [
            pltpu.VMEM((2, tall, width), BF16),
            pltpu.VMEM((3, 2, rows, width), F32),
            pltpu.VMEM((2, rows, width), F32),
        ],
        compiler_params=grant(12),
        cost_estimate=cost(2.0),
        name="edge_planes",
    )(
        cells, cotangent, y_near, y_far, x_near, x_far, forward_weights, bias, acc, sums,
    )

    def back(pairs, previous, after, beyond=(), acts=()):
        edges, stored = len(beyond) > 0, len(acts) > 0
        operands = [grad, grad_rim, first, final, *beyond, backward_weights, *acts]
        specs = [VMEM] * len(operands)
        aliases = {}
        if previous is not None:
            aliases = {len(operands): 0}
            operands.append(previous)
            specs.append(ANY)
        operands.append(after)
        specs.append(ANY)
        planes = 2 * len(pairs) + 2 * edges
        results = pl.pallas_call(
            lambda *refs: back_kernel(pairs, edges, stored, *refs),
            out_shape=(shape(size_x, size_y, width),) * (1 + stored),
            in_specs=specs,
            out_specs=(ANY,) * (1 + stored),
            scratch_shapes=[
                pltpu.VMEM((planes, size_y, width), BF16),
                pltpu.VMEM((3, planes, rows, width), F32),
                pltpu.VMEM((2, tall, width), BF16),
                pltpu.SemaphoreType.DMA((planes + 3 * stored,)),
            ],
            input_output_aliases=aliases,
            compiler_params=grant(12),
            cost_estimate=cost(2.5 if planes > 4 else 1.0),
            name="input_grad",
        )(*operands)
        return results if stored else results[0]

    starts = list(range(1, size_x - 1, 2))
    cut = len(starts) - 2
    def add(terms, dtype):
        return pl.pallas_call(
            add_kernel,
            out_shape=shape(*terms[0].shape, dtype=dtype),
            in_specs=[VMEM] * len(terms),
            out_specs=VMEM,
            compiler_params=grant(2),
            cost_estimate=cost(0.1),
            name="add_sums",
        )(*terms)

    def split(terms, step):
        dims = (terms[0].shape[0] // 2,) + terms[0].shape[1:]
        return pl.pallas_call(
            lambda *refs: split_kernel(step, *refs),
            out_shape=(shape(*dims, dtype=F32), shape(*dims)),
            in_specs=[VMEM] * len(terms),
            out_specs=(VMEM, VMEM),
            compiler_params=grant(2),
            cost_estimate=cost(0.1),
            name="split_sums",
        )(*terms)

    rounds = [("dp", 1 << i) for i in range(parts.bit_length() - 1)]
    rounds += [("gy", 1 << i) for i in range(1, lax.axis_size("gy").bit_length() - 1)]
    rounds += [("gx", 1 << i) for i in range(lax.axis_size("gx").bit_length() - 1)]
    away = swap(send, "gy", 0)
    send_stay, keep_away, keep_stay = pl.pallas_call(
        rest_kernel,
        out_shape=(shape(*blocks, dtype=F32),) * 3,
        in_specs=[VMEM, VMEM],
        out_specs=(VMEM,) * 3,
        compiler_params=grant(4),
        cost_estimate=cost(0.7),
        name="rest_of_sums",
    )(acc, sums)
    terms = [keep_stay, swap(send_stay, "gy", 0)]
    input_grad = None
    for index, (axis, step) in enumerate(rounds):
        if index == 0:
            send = add([keep_away, away], BF16)
        elif axis == "dp":
            total, send = split(terms, step)
            terms = [total]
        else:
            send = add(terms, BF16)
            terms = [send]
        if index == 0:
            later, send = lax.optimization_barrier((kernel, send))
            backward_weights, scales = back_weights(later)
        received = exchange(send, axis, step)
        if index == 0:
            input_grad = back(starts[:2], None, send)
            received, input_grad = lax.optimization_barrier((received, input_grad))
            *edges, backward_weights = lax.optimization_barrier((*edges, backward_weights))
            back_near = swap(edges[0], "gx", 0)
            back_far = swap(edges[1], "gx", 1) if many else back_near
        if index == len(rounds) - 2:
            input_grad, activation = back(
                starts[2:cut], input_grad, send, acts=(act_inner, act_edges)
            )
            received, input_grad = lax.optimization_barrier((received, input_grad))
        if index == len(rounds) - 1:
            input_grad = back(starts[cut:], input_grad, send, beyond=(back_near, back_far))
            received, input_grad = lax.optimization_barrier((received, input_grad))
        terms.append(received)
    total = add(terms, F32).reshape(SLOTS // 2, share, width)
    other = swap(total, "gy", 0)

    kernel_grad, bias_grad = pl.pallas_call(
        finish_kernel,
        out_shape=(shape(27, share, half), shape(1, share, dtype=F32)),
        in_specs=[VMEM] * 3,
        out_specs=(VMEM, VMEM),
        compiler_params=grant(4),
        name="scale_weight_grad",
    )(total, other, scales)
    return (
        activation[None],
        input_grad[None],
        jnp.swapaxes(kernel_grad.reshape(3, 3, 3, share, half), 3, 4),
        bias_grad.reshape(share),
    )


def solution(mesh):
    placed = (P("dp", "gx", "gy", None), P(), P(), P("dp", "gx", "gy", None), P())
    return jax.shard_map(
        local,
        mesh=mesh,
        in_specs=placed,
        out_specs=(
            P("dp", "gx", "gy", None),
            P("dp", "gx", "gy", None),
            P(None, None, None, None, "dp"),
            P("dp"),
        ),
        check_vma=False,
    )
```

```python
import math

import jax
import jax.numpy as jnp
from jax import lax
from jax.experimental import pallas as pl
from jax.experimental.pallas import tpu as pltpu
from jax.sharding import PartitionSpec as P

RIM = 8
THIN = 2
PAD = 16
CHUNK = 64
SLOTS = 14
VMEM = pl.BlockSpec(memory_space=pltpu.VMEM)
SMEM = pl.BlockSpec(memory_space=pltpu.SMEM)
ANY = pl.BlockSpec(memory_space=pl.ANY)
BF16, F32 = jnp.bfloat16, jnp.float32


def swap(value, axis, first):
    count = lax.axis_size(axis)
    links = []
    for low in range(first, count, 2):
        high = (low + 1) % count
        links += [(low, high), (high, low)]
    return lax.ppermute(value, axis, links)


def exchange(value, axis, step):
    axes = ("gx", "gy", "dp")
    sizes = [lax.axis_size(name) for name in axes]
    stride = {name: math.prod(sizes[i + 1 :]) for i, name in enumerate(axes)}
    flip = (step * stride[axis]) ^ stride["gy"]
    return lax.ppermute(value, axes, [(i, i ^ flip) for i in range(math.prod(sizes))])


def half_kept():
    side = lax.axis_index("gy") % 2
    for axis, first in (("gx", 1), ("gy", 2), ("dp", 1)):
        step = first
        while step < lax.axis_size(axis):
            side = side + lax.axis_index(axis) // step
            step *= 2
    return side % 2


def tap_block(taps, a, b):
    low, mid, high = taps[a, b, 0], taps[a, b, 1], taps[a, b, 2]
    return jnp.concatenate(
        [jnp.concatenate([mid, low], axis=1), jnp.concatenate([high, mid], axis=1)], axis=0
    )


def clear_corners(out, width):
    blank = jnp.zeros((width, 3 * width), BF16)
    out[3 * width :, : 3 * width] = blank
    out[:width, 3 * width :] = blank


def build_front(taps, w_ref, narrow_ref):
    width = 2 * taps.shape[3]
    clear_corners(w_ref, width)
    for a in range(3):
        for b in range(3):
            block = tap_block(taps, a, b)
            for k in range(2):
                row, col = (a + k) * width, (3 * k + b) * width
                w_ref[row : row + width, col : col + width] = block
            row, col = a * width, b * width
            narrow_ref[row : row + width, col : col + width] = block


def back_weights_kernel(inverse, taps, exponents, w_ref, scale_ref):
    half = taps.shape[3]
    width = 2 * half
    clear_corners(w_ref, width)
    for a in range(3):
        for b in range(3):
            turned = tap_block(taps, a, b).T
            for k in range(2):
                row, col = (2 - a + k) * width, (3 * k + 2 - b) * width
                w_ref[row : row + width, col : col + width] = turned
    lower = lax.broadcasted_iota(jnp.int32, (8, width), 1) < half

    def scale(t, c):
        power = lax.shift_left(jnp.int32(1), exponents[t // 3, t % 3, c] + 2)
        return power.astype(F32) * (0.25 * inverse)

    for s in range(SLOTS):
        t = 2 * (s - 9)
        if s < 9:
            low, high = scale(s, 1), scale(s, 2)
        else:
            low, high = scale(t, 0), scale(t + 1, 0) if t + 1 < 9 else inverse
        scale_ref[s] = jnp.where(lower, low, high)


def plane_taps(taps, slots, bodies, weights):
    size_y, width = bodies[0].shape
    result = jnp.dot(
        jnp.concatenate(bodies, axis=1), weights, preferred_element_type=F32
    )
    for k, p in enumerate(slots):
        for b in range(3):
            col = (3 * k + b) * width
            taps[b, p, PAD : PAD + size_y, :] = result[:, col : col + width]


def rim_taps(taps, slots, triples, weights):
    width = triples[0][0].shape[1]
    rows = 2 * RIM
    last = taps.shape[2] - PAD
    stacked = jnp.concatenate(
        [jnp.concatenate([triple[j] for triple in triples], axis=0) for j in range(3)], axis=1
    )
    result = jnp.dot(stacked, weights, preferred_element_type=F32)
    for k, p in enumerate(slots):
        for b in range(3):
            block = result[k * rows : (k + 1) * rows, b * width : (b + 1) * width]
            taps[b, p, PAD - RIM : PAD, :] = block[:RIM]
            taps[b, p, last : last + RIM, :] = block[RIM:]


def shifted_sum(taps, p, start, rows):
    return (
        taps[0, p, start - 1 : start - 1 + rows, :]
        + taps[1, p, start : start + rows, :]
        + taps[2, p, start + 1 : start + 1 + rows, :]
    )


def activate(taps, wide, p, bias, sums, u_body, u_rim, act, grad_body, grad_rim):
    size_y = taps.shape[2] - 2 * PAD
    spans = [(PAD - RIM, RIM)]
    spans += [(PAD + y, CHUNK) for y in range(0, size_y, CHUNK)]
    spans += [(PAD + size_y, RIM)]
    for start, rows in spans:
        body = rows == CHUNK
        y = start - PAD if body else (0 if start < PAD else RIM)
        preact = shifted_sum(taps, p, start, rows) + bias
        sigma = 0.5 * jnp.tanh(0.5 * preact) + 0.5
        cotangent = (u_body if body else u_rim)[y : y + rows, :].astype(F32)
        rounded = (cotangent * sigma * (1.0 + preact * (1.0 - sigma))).astype(BF16)
        exact = rounded.astype(F32)
        wide[p, start : start + rows, :] = exact
        if body:
            act[y : y + rows, :] = (preact * sigma).astype(BF16)
            grad_body[y : y + rows, :] = rounded
            sums = sums + jnp.sum(exact.reshape(rows // 8, 8, exact.shape[1]), axis=0)
        else:
            grad_rim[y : y + rows, :] = rounded
    return sums


def shifted_grads(wide, p):
    size_y = wide.shape[1] - 2 * PAD
    return jnp.concatenate(
        [wide[p, PAD + 1 - b : PAD + 1 - b + size_y, :].astype(BF16) for b in range(3)], axis=1
    )


def outer(sources, grads):
    return jnp.dot(
        jnp.concatenate([jnp.concatenate(three, axis=0) for three in sources], axis=1),
        jnp.concatenate(grads, axis=0),
        preferred_element_type=F32,
    )


def outer_turned(bodies, grads):
    return lax.dot_general(
        jnp.concatenate(grads, axis=0),
        jnp.concatenate([jnp.concatenate(three, axis=1) for three in bodies], axis=0),
        (((0,), (0,)), ((), ())),
        preferred_element_type=F32,
    )


def oriented(near, far, side, place):
    @pl.when(side == 0)
    def _():
        place(far, near)

    @pl.when(side == 1)
    def _():
        place(near, far)


def beside(axis, near, far, place, clear_low, clear_high):
    index = lax.axis_index(axis)
    oriented(near, far, index % 2, place)
    pl.when(index == 0)(clear_low)
    pl.when(index == lax.axis_size(axis) - 1)(clear_high)


def place_rims(y_near, y_far, f_rim, u_rim, gap):
    low = slice(gap, gap + THIN)
    high = slice(2 * RIM - gap - THIN, 2 * RIM - gap)

    def place(left, right):
        f_rim[:, low, :] = left[:, :THIN, :]
        u_rim[:, low, :] = left[:, THIN:, :]
        f_rim[:, high, :] = right[:, :THIN, :]
        u_rim[:, high, :] = right[:, THIN:, :]

    def clear(rows):
        blank = jnp.zeros((f_rim.shape[0], THIN, f_rim.shape[2]), BF16)
        f_rim[:, rows, :] = blank
        u_rim[:, rows, :] = blank

    for ref in (f_rim, u_rim):
        ref[...] = jnp.zeros(ref.shape, BF16)
    beside("gy", y_near, y_far, place, lambda: clear(low), lambda: clear(high))


def place_planes(x_near, x_far, around):
    def place(below, above):
        around[0] = below[...]
        around[1] = above[...]

    def clear(k):
        around[k] = jnp.zeros(around.shape[1:], BF16)

    beside("gx", x_near, x_far, place, lambda: clear(0), lambda: clear(1))


def rims_kernel(ends, near_ref, far_ref):
    rows = ends.shape[1] // 2

    def hand(tail, head):
        tail[...] = ends[:, rows:, :]
        head[...] = ends[:, :rows, :]

    oriented(far_ref, near_ref, lax.axis_index("gy") % 2, hand)


def planes_kernel(f_ref, y_near, y_far, near_ref, far_ref=None):
    size_x, size_y, width = f_ref.shape
    low = slice(size_y + RIM - THIN, size_y + RIM)
    high = slice(size_y + RIM, size_y + RIM + THIN)

    def fill(out, x):
        out[:size_y] = f_ref[x]
        out[size_y:] = jnp.zeros((2 * RIM, width), BF16)

        def place(left, right):
            out[low] = left[x, :THIN]
            out[high] = right[x, :THIN]

        def clear(rows):
            out[rows] = jnp.zeros((THIN, width), BF16)

        beside("gy", y_near, y_far, place, lambda: clear(low), lambda: clear(high))

    def hand(last, first):
        if last is not None:
            fill(last, size_x - 1)
        if first is not None:
            fill(first, 0)

    oriented(far_ref, near_ref, lax.axis_index("gx") % 2, hand)


def front_kernel(
    f_ref, kernel_ref, offsets, pre_ref, turned, narrow_ref, bias_ref, w_ref, taps
):
    size_x, size_y, width = f_ref.shape
    inner = size_x - 2
    build_front(kernel_ref, w_ref, narrow_ref)
    bias = offsets[...].reshape(1, width // 2)
    bias = jnp.concatenate([bias, bias], axis=1)
    bias_ref[...] = bias
    blank = jnp.zeros((3, inner, RIM, width), F32)
    taps[:, :, PAD - RIM : PAD, :] = blank
    taps[:, :, PAD + size_y : PAD + size_y + RIM, :] = blank
    for p in range(0, inner, 2):
        plane_taps(taps, (p, p + 1), [f_ref[p + j] for j in range(4)], w_ref[...])
        for x in range(0 if p == 0 else p + 2, p + 4):
            turned[x] = f_ref[x].T
        for q in (p, p + 1):
            for y in range(0, size_y, CHUNK):
                pre_ref[q, y : y + CHUNK, :] = shifted_sum(taps, q, PAD + y, CHUNK) + bias


def gradient(preact, cotangent):
    sigma = 0.5 * jnp.tanh(0.5 * preact) + 0.5
    rounded = (
        cotangent.astype(F32) * sigma * (1.0 + preact * (1.0 - sigma))
    ).astype(BF16)
    return preact * sigma, rounded, rounded.astype(F32)


def inner_kernel(
    f_ref, u_ref, y_near, y_far, pre_ref, turned, w_ref, bias_ref,
    act, grad_ref, rim_ref, acc_ref, sums_ref,
    f_rim, u_rim, wide, acc,
):
    size_x, size_y, width = f_ref.shape
    inner = size_x - 2
    gap = RIM - 2 * THIN

    place_rims(y_near, y_far, f_rim, u_rim, gap)
    f_rim[:, gap + THIN : RIM, :] = f_ref[:, :THIN, :]
    f_rim[:, RIM : RIM + THIN, :] = f_ref[:, size_y - THIN :, :]
    bias = bias_ref[...]
    rows = 2 * RIM
    tall = [
        jnp.concatenate([f_rim[x + j] for x in range(inner)], axis=0) for j in range(3)
    ]
    strips = jnp.dot(
        jnp.concatenate(tall, axis=1), w_ref[...], preferred_element_type=F32
    )
    row = lax.broadcasted_iota(jnp.int32, (RIM, width), 0)
    sums = jnp.zeros((8, width), F32)
    for p in range(0, inner, 2):
        for q in (p, p + 1):
            strip = [
                strips[q * rows : (q + 1) * rows, b * width : (b + 1) * width] for b in range(3)
            ]
            for side in range(2):
                part = [tap[side * RIM : (side + 1) * RIM] for tap in strip]
                preact = (
                    pltpu.roll(part[0], 1, 0) + part[1] + pltpu.roll(part[2], RIM - 1, 0) + bias
                )
                _, rounded, exact = gradient(
                    preact, u_rim[q + 1, side * RIM : (side + 1) * RIM, :]
                )
                turn = THIN if side == 0 else RIM - THIN
                exact = pltpu.roll(exact, turn, 0)
                start = PAD - RIM if side == 0 else PAD + size_y
                wide[q, start : start + RIM, :] = exact
                rim_ref[q, side * RIM : (side + 1) * RIM, :] = exact.astype(BF16)
            low = jnp.where(row == 0, pltpu.roll(strip[0][:RIM], RIM - gap - THIN + 1, 0), 0.0)
            high = jnp.where(
                row == RIM - 1, pltpu.roll(strip[2][RIM:], RIM - 1 - THIN, 0), 0.0
            )
            for y in range(0, size_y, CHUNK):
                preact = pre_ref[q, y : y + CHUNK, :]
                if y == 0:
                    preact = jnp.concatenate([preact[:RIM] + low, preact[RIM:]], axis=0)
                if y + CHUNK == size_y:
                    preact = jnp.concatenate([preact[:-RIM], preact[-RIM:] + high], axis=0)
                value, rounded, exact = gradient(preact, u_ref[q + 1, y : y + CHUNK, :])
                wide[q, PAD + y : PAD + y + CHUNK, :] = exact
                act[q, y : y + CHUNK, :] = value.astype(BF16)
                grad_ref[q, y : y + CHUNK, :] = rounded
                sums = sums + jnp.sum(exact.reshape(CHUNK // 8, 8, width), axis=0)
        grads = [shifted_grads(wide, q) for q in (p, p + 1)]
        if p < inner - 2:
            term = outer([[turned[q + j] for j in range(3)] for q in (p, p + 1)], grads)
            if p == 0:
                acc[...] = term
            else:
                acc[...] += term
        if p == inner - 4:
            for a in range(3):
                for b in range(3):
                    here, there = slice(a * width, (a + 1) * width), slice(b * width, (b + 1) * width)
                    acc_ref[there, here] = acc[here, there].T
        if p == inner - 2:
            acc_ref[...] += outer_turned(
                [[f_ref[q + j] for j in range(3)] for q in (p, p + 1)], grads
            )
    sums_ref[...] = sums


def emit_half(acc, sums, which, away, stay):
    outs = [out for out in (away, stay) if out is not None]
    blocks, count, share, width = outs[0].shape
    half = width // 2

    def block(t):
        a, b = t // 3, t % 3
        return acc[b * width : (b + 1) * width, a * width : (a + 1) * width]

    def lower(rows):
        return lax.broadcasted_iota(jnp.int32, (rows, width), 1) < half

    def middle(t):
        whole = block(t)
        rolled = pltpu.roll(whole[half:], half, 1)
        return whole[:half] + jnp.where(lower(half), rolled, 0.0)

    def low_pair(t):
        low = block(t)[half:]
        if t + 1 < 9:
            return jnp.where(lower(half), low, pltpu.roll(block(t + 1)[half:], half, 1))
        both = jnp.sum(sums, axis=0, keepdims=True)
        both = jnp.broadcast_to(both + pltpu.roll(both, half, 1), (share, width))
        turned = [
            pltpu.roll(both, (half - d * share) % width, 1) for d in range(2 * blocks)
        ]
        return jnp.where(lower(half), low, jnp.concatenate(turned, axis=0))

    def write(bit):
        def put(s, value):
            for k in range(blocks):
                for out, d in ((away, 2 * k + 1 - bit), (stay, 2 * k + bit)):
                    if out is not None:
                        out[k, s] = value[d * share : (d + 1) * share]

        @pl.when(which == 0)
        def _():
            for s in range(count):
                put(s, middle(s))

        @pl.when(which == 1)
        def _():
            for t in range(count, 9):
                put(t - count, middle(t))
            for t in range(0, 9, 2):
                put(9 + t // 2 - count, low_pair(t))

    place = lax.axis_index("dp") % 2
    pl.when(place == 0)(lambda: write(0))
    pl.when(place == 1)(lambda: write(1))


def rest_kernel(acc, sums, send_stay, keep_away, keep_stay):
    kept = half_kept()
    emit_half(acc, sums[...], 1 - kept, None, send_stay)
    emit_half(acc, sums[...], kept, keep_away, keep_stay)


def edge_kernel(
    f_ref, u_ref, y_near, y_far, x_near, x_far, w_ref, bias_ref, acc_ref, sums_ref,
    act, first_ref, last_ref, acc, bias_sums, send_ref, near_ref, *refs
):
    far_ref = refs[0] if len(refs) > 5 else None
    f_rim, u_rim, around, taps, wide = refs[-5:]
    size_x, size_y, width = f_ref.shape
    x_side = lax.axis_index("gx") % 2
    place_rims(y_near, y_far, f_rim, u_rim, RIM - THIN)
    place_planes(x_near, x_far, around)
    bias = bias_ref[...]
    weights = w_ref[...]
    tall = size_y + 2 * RIM
    bodies = [
        [around[0, :size_y], f_ref[0], f_ref[1]],
        [f_ref[size_x - 2], f_ref[size_x - 1], around[1, :size_y]],
    ]
    rims = [
        [around[0, size_y:tall], f_rim[0], f_rim[1]],
        [f_rim[size_x - 2], f_rim[size_x - 1], around[1, size_y:tall]],
    ]
    rim_taps(taps, (0, 1), rims, weights)
    for p in range(2):
        plane_taps(taps, (p,), bodies[p], weights)
    sums = sums_ref[...]
    outs = (first_ref, last_ref)
    places = (0, size_x - 1)
    for p in range(2):
        x = places[p]
        sums = activate(
            taps, wide, p, bias, sums, u_ref.at[x], u_rim.at[x], act.at[p],
            outs[p].at[pl.ds(0, size_y)], outs[p].at[pl.ds(size_y, 2 * RIM)],
        )
    acc[...] = acc_ref[...] + outer_turned(bodies, [shifted_grads(wide, p) for p in range(2)])

    def hand(last, first):
        if last is not None:
            last[...] = last_ref[...]
        if first is not None:
            first[...] = first_ref[...]

    oriented(far_ref, near_ref, x_side, hand)

    bias_sums[...] = sums
    emit_half(acc, sums, 1 - half_kept(), send_ref, None)


def store_activation(act_inner, act_edges, act_hbm, sems):
    size_x = act_hbm.shape[0]
    copies = [
        pltpu.make_async_copy(act_edges.at[0], act_hbm.at[0], sems.at[0]),
        pltpu.make_async_copy(act_edges.at[1], act_hbm.at[size_x - 1], sems.at[1]),
        pltpu.make_async_copy(act_inner, act_hbm.at[pl.ds(1, size_x - 2)], sems.at[2]),
    ]
    for copy in copies:
        copy.start()
    return copies


def back_kernel(pairs, edges, stored, grad_ref, rim_ref, first_ref, last_ref, *refs):
    x_near, x_far = refs[:2] if edges else (None, None)
    w_ref = refs[2 * edges]
    out_hbm, *act_hbm, out, taps, around, sems = refs[-5 - stored :]
    copies = []
    if stored:
        copies = store_activation(*refs[1:3], act_hbm[0], sems.at[pl.ds(out.shape[0], 3)])
    size_y, width = grad_ref.shape[1:]
    size_x = grad_ref.shape[0] + 2
    tall = size_y + 2 * RIM

    def body(x):
        if x == 0:
            return first_ref[:size_y]
        if x == size_x - 1:
            return last_ref[:size_y]
        if x < 0 or x >= size_x:
            return around[int(x > 0), :size_y]
        return grad_ref[x - 1]

    def rim(x):
        if x == 0:
            return first_ref[size_y:tall]
        if x == size_x - 1:
            return last_ref[size_y:tall]
        if x < 0 or x >= size_x:
            return around[int(x > 0), size_y:tall]
        return rim_ref[x - 1]

    if edges:
        place_planes(x_near, x_far, around)
    narrow = w_ref[: 3 * width, : 3 * width]
    planes = [x for first in pairs for x in (first, first + 1)]
    planes += [0, size_x - 1] if edges else []
    rim_taps(taps, range(len(planes)), [[rim(x + j) for j in (-1, 0, 1)] for x in planes], narrow)
    stores = []

    def multiply(k):
        x = planes[k]
        if planes[k + 1] == x + 1:
            plane_taps(taps, (k, k + 1), [body(x + j) for j in (-1, 0, 1, 2)], w_ref[...])
        else:
            for i in (k, k + 1):
                plane_taps(taps, (i,), [body(planes[i] + j) for j in (-1, 0, 1)], narrow)

    multiply(0)
    for k in range(0, len(planes), 2):
        if k + 2 < len(planes):
            multiply(k + 2)
        for i in (k, k + 1):
            for y in range(0, size_y, CHUNK):
                out[i, y : y + CHUNK, :] = shifted_sum(taps, i, PAD + y, CHUNK).astype(BF16)
            stores.append(
                pltpu.make_async_copy(out.at[i], out_hbm.at[planes[i]], sems.at[i])
            )
            stores[-1].start()
    for copy in stores + copies:
        copy.wait()


def split_kernel(step, *refs):
    *terms, keep_ref, send_ref = refs
    total = sum_refs(terms)
    bit = (lax.axis_index("dp") // step) % 2

    def place(first, second):
        for k in range(keep_ref.shape[0]):
            keep_ref[k] = total[2 * k + first]
            send_ref[k] = total[2 * k + second].astype(BF16)

    pl.when(bit == 0)(lambda: place(0, 1))
    pl.when(bit == 1)(lambda: place(1, 0))


def sum_refs(terms):
    total = terms[0][...].astype(F32)
    for term in terms[1:]:
        total = total + term[...].astype(F32)
    return total


def add_kernel(*refs):
    *terms, total_ref = refs
    total_ref[...] = sum_refs(terms).astype(total_ref.dtype)


def finish_kernel(own, other, scale_ref, grad_ref, bias_ref):
    share, half = grad_ref.shape[1:]

    def emit(first, second):
        for s in range(SLOTS):
            block = (first if s < SLOTS // 2 else second)[s % (SLOTS // 2)] * scale_ref[s, :1]
            low, high = block[:, :half], pltpu.roll(block, half, 1)[:, :half]
            t = 2 * (s - 9)
            grad_ref[3 * s + 1 if s < 9 else 3 * t] = low.astype(BF16)
            if s < SLOTS - 1:
                grad_ref[3 * s + 2 if s < 9 else 3 * t + 3] = high.astype(BF16)
            else:
                bias_ref[...] = high[:1, :share]

    kept = half_kept()

    @pl.when(kept == 0)
    def _():
        emit(own, other)

    @pl.when(kept == 1)
    def _():
        emit(other, own)


def shape(*dims, dtype=BF16):
    return jax.ShapeDtypeStruct(dims, dtype)


def grant(mebibytes):
    return pltpu.CompilerParams(vmem_limit_bytes=mebibytes * 2**20)


def cost(microseconds):
    return pl.CostEstimate(
        flops=int(1.1e9 * microseconds), bytes_accessed=0, transcendentals=0
    )


def local(features, kernel, offsets, upstream, grad_exponents):
    cells, cotangent = features[0], upstream[0]
    size_x, size_y, width = cells.shape
    half = width // 2
    tall, rows = size_y + 2 * RIM, size_y + 2 * PAD
    parts = lax.axis_size("dp")
    share = half // parts
    sources = (cells, cotangent)
    ends = jnp.concatenate(
        [source[:, :THIN] for source in sources] + [source[:, size_y - THIN :] for source in sources],
        axis=1,
    )
    rim_near, rim_far = pl.pallas_call(
        rims_kernel,
        out_shape=(shape(size_x, 2 * THIN, width),) * 2,
        in_specs=[VMEM],
        out_specs=(VMEM, VMEM),
        compiler_params=grant(1),
        cost_estimate=cost(3.0),
        name="pack_rims",
    )(ends)
    y_near = swap(rim_near, "gy", 0)
    y_far = swap(rim_far, "gy", 1)

    voxels = (
        features.shape[0] * parts * size_x * lax.axis_size("gx") * size_y * lax.axis_size("gy") * 2
    )
    def back_weights(taps):
        return pl.pallas_call(
            lambda *refs: back_weights_kernel(1.0 / math.sqrt(voxels), *refs),
            out_shape=(shape(4 * width, 6 * width), shape(SLOTS, 8, width, dtype=F32)),
            in_specs=[VMEM, SMEM],
            out_specs=(VMEM, VMEM),
            compiler_params=grant(4),
            cost_estimate=cost(1.0),
            name="back_weights",
        )(taps, grad_exponents)

    inner = size_x - 2
    preact, turned, forward_weights, bias = pl.pallas_call(
        front_kernel,
        out_shape=(
            shape(inner, size_y, width, dtype=F32),
            shape(size_x, width, size_y),
            shape(3 * width, 3 * width),
            shape(1, width, dtype=F32),
        ),
        in_specs=[VMEM] * 3,
        out_specs=(VMEM,) * 4,
        scratch_shapes=[
            pltpu.VMEM((4 * width, 6 * width), BF16),
            pltpu.VMEM((3, inner, rows, width), F32),
        ],
        compiler_params=grant(16),
        cost_estimate=cost(2.0),
        name="front_planes",
    )(cells, kernel, offsets)

    many = lax.axis_size("gx") > 2
    plane_sends = pl.pallas_call(
        planes_kernel,
        out_shape=(shape(tall, width),) * (1 + many),
        in_specs=[VMEM] * 3,
        out_specs=(VMEM,) * (1 + many),
        compiler_params=grant(1),
        cost_estimate=cost(0.1),
        name="pack_planes",
    )(cells, y_near, y_far)
    x_near = swap(plane_sends[0], "gx", 0)
    x_far = swap(plane_sends[1], "gx", 1) if many else x_near

    rims = [
        pltpu.VMEM((size_x, 2 * RIM, width), BF16),
        pltpu.VMEM((size_x, 2 * RIM, width), BF16),
    ]
    act_inner, grad, grad_rim, acc, sums = pl.pallas_call(
        inner_kernel,
        out_shape=(
            shape(inner, size_y, width),
            shape(inner, size_y, width),
            shape(inner, 2 * RIM, width),
            shape(3 * width, 3 * width, dtype=F32),
            shape(8, width, dtype=F32),
        ),
        in_specs=[VMEM] * 8,
        out_specs=(VMEM,) * 5,
        scratch_shapes=rims + [
            pltpu.VMEM((inner, rows, width), F32),
            pltpu.VMEM((3 * width, 3 * width), F32),
        ],
        compiler_params=grant(12),
        cost_estimate=cost(3.0),
        name="inner_planes",
    )(cells, cotangent, y_near, y_far, preact, turned, forward_weights, bias)

    blocks = (parts // 2, SLOTS // 2, share, width)
    act_edges, first, final, acc, sums, send, *edges = pl.pallas_call(
        edge_kernel,
        out_shape=(
            shape(2, size_y, width),
            shape(tall, width),
            shape(tall, width),
            shape(3 * width, 3 * width, dtype=F32),
            shape(8, width, dtype=F32),
            shape(*blocks, dtype=F32),
        )
        + (shape(tall, width),) * (1 + many),
        in_specs=[VMEM] * 10,
        out_specs=(VMEM,) * (7 + many),
        scratch_shapes=rims + [
            pltpu.VMEM((2, tall, width), BF16),
            pltpu.VMEM((3, 2, rows, width), F32),
            pltpu.VMEM((2, rows, width), F32),
        ],
        compiler_params=grant(12),
        cost_estimate=cost(2.0),
        name="edge_planes",
    )(
        cells, cotangent, y_near, y_far, x_near, x_far, forward_weights, bias, acc, sums,
    )

    def back(pairs, previous, after, beyond=(), acts=()):
        edges, stored = len(beyond) > 0, len(acts) > 0
        operands = [grad, grad_rim, first, final, *beyond, backward_weights, *acts]
        specs = [VMEM] * len(operands)
        aliases = {}
        if previous is not None:
            aliases = {len(operands): 0}
            operands.append(previous)
            specs.append(ANY)
        operands.append(after)
        specs.append(ANY)
        planes = 2 * len(pairs) + 2 * edges
        results = pl.pallas_call(
            lambda *refs: back_kernel(pairs, edges, stored, *refs),
            out_shape=(shape(size_x, size_y, width),) * (1 + stored),
            in_specs=specs,
            out_specs=(ANY,) * (1 + stored),
            scratch_shapes=[
                pltpu.VMEM((planes, size_y, width), BF16),
                pltpu.VMEM((3, planes, rows, width), F32),
                pltpu.VMEM((2, tall, width), BF16),
                pltpu.SemaphoreType.DMA((planes + 3 * stored,)),
            ],
            input_output_aliases=aliases,
            compiler_params=grant(12),
            cost_estimate=cost(2.5 if planes > 4 else 1.0),
            name="input_grad",
        )(*operands)
        return results if stored else results[0]

    starts = list(range(1, size_x - 1, 2))
    cut = len(starts) - 2
    def add(terms, dtype):
        return pl.pallas_call(
            add_kernel,
            out_shape=shape(*terms[0].shape, dtype=dtype),
            in_specs=[VMEM] * len(terms),
            out_specs=VMEM,
            compiler_params=grant(2),
            cost_estimate=cost(0.1),
            name="add_sums",
        )(*terms)

    def split(terms, step):
        dims = (terms[0].shape[0] // 2,) + terms[0].shape[1:]
        return pl.pallas_call(
            lambda *refs: split_kernel(step, *refs),
            out_shape=(shape(*dims, dtype=F32), shape(*dims)),
            in_specs=[VMEM] * len(terms),
            out_specs=(VMEM, VMEM),
            compiler_params=grant(2),
            cost_estimate=cost(0.1),
            name="split_sums",
        )(*terms)

    rounds = [("dp", 1 << i) for i in range(parts.bit_length() - 1)]
    rounds += [("gy", 1 << i) for i in range(1, lax.axis_size("gy").bit_length() - 1)]
    rounds += [("gx", 1 << i) for i in range(lax.axis_size("gx").bit_length() - 1)]
    away = swap(send, "gy", 0)
    send_stay, keep_away, keep_stay = pl.pallas_call(
        rest_kernel,
        out_shape=(shape(*blocks, dtype=F32),) * 3,
        in_specs=[VMEM, VMEM],
        out_specs=(VMEM,) * 3,
        compiler_params=grant(4),
        cost_estimate=cost(0.7),
        name="rest_of_sums",
    )(acc, sums)
    terms = [keep_stay, swap(send_stay, "gy", 0)]
    input_grad = None
    for index, (axis, step) in enumerate(rounds):
        if index == 0:
            send = add([keep_away, away], BF16)
        elif axis == "dp":
            total, send = split(terms, step)
            terms = [total]
        else:
            send = add(terms, BF16)
            terms = [send]
        if index == 0:
            later, send = lax.optimization_barrier((kernel, send))
            backward_weights, scales = back_weights(later)
        received = exchange(send, axis, step)
        if index == 0:
            input_grad = back(starts[:2], None, send)
            received, input_grad = lax.optimization_barrier((received, input_grad))
            *edges, backward_weights = lax.optimization_barrier((*edges, backward_weights))
            back_near = swap(edges[0], "gx", 0)
            back_far = swap(edges[1], "gx", 1) if many else back_near
        if index == len(rounds) - 2:
            input_grad, activation = back(
                starts[2:cut], input_grad, send, acts=(act_inner, act_edges)
            )
            received, input_grad = lax.optimization_barrier((received, input_grad))
        if index == len(rounds) - 1:
            input_grad = back(starts[cut:], input_grad, send, beyond=(back_near, back_far))
            received, input_grad = lax.optimization_barrier((received, input_grad))
        terms.append(received)
    total = add(terms, F32).reshape(SLOTS // 2, share, width)
    other = swap(total, "gy", 0)

    kernel_grad, bias_grad = pl.pallas_call(
        finish_kernel,
        out_shape=(shape(27, share, half), shape(1, share, dtype=F32)),
        in_specs=[VMEM] * 3,
        out_specs=(VMEM, VMEM),
        compiler_params=grant(4),
        name="scale_weight_grad",
    )(total, other, scales)
    return (
        activation[None],
        input_grad[None],
        jnp.swapaxes(kernel_grad.reshape(3, 3, 3, share, half), 3, 4),
        bias_grad.reshape(share),
    )


def solution(mesh):
    placed = (P("dp", "gx", "gy", None), P(), P(), P("dp", "gx", "gy", None), P())
    return jax.shard_map(
        local,
        mesh=mesh,
        in_specs=placed,
        out_specs=(
            P("dp", "gx", "gy", None),
            P("dp", "gx", "gy", None),
            P(None, None, None, None, "dp"),
            P("dp"),
        ),
        check_vma=False,
    )
```

```python
import math

import jax
import jax.numpy as jnp
from jax import lax
from jax.experimental import pallas as pl
from jax.experimental.pallas import tpu as pltpu
from jax.sharding import PartitionSpec as P

RIM = 8
THIN = 2
PAD = 16
CHUNK = 64
SLOTS = 14
VMEM = pl.BlockSpec(memory_space=pltpu.VMEM)
SMEM = pl.BlockSpec(memory_space=pltpu.SMEM)
ANY = pl.BlockSpec(memory_space=pl.ANY)
BF16, F32 = jnp.bfloat16, jnp.float32


def swap(value, axis, first):
    count = lax.axis_size(axis)
    links = []
    for low in range(first, count, 2):
        high = (low + 1) % count
        links += [(low, high), (high, low)]
    return lax.ppermute(value, axis, links)


def exchange(value, axis, step):
    axes = ("gx", "gy", "dp")
    sizes = [lax.axis_size(name) for name in axes]
    stride = {name: math.prod(sizes[i + 1 :]) for i, name in enumerate(axes)}
    flip = (step * stride[axis]) ^ stride["gy"]
    return lax.ppermute(value, axes, [(i, i ^ flip) for i in range(math.prod(sizes))])


def half_kept():
    side = lax.axis_index("gy") % 2
    for axis, first in (("gx", 1), ("gy", 2), ("dp", 1)):
        step = first
        while step < lax.axis_size(axis):
            side = side + lax.axis_index(axis) // step
            step *= 2
    return side % 2


def tap_block(taps, a, b):
    low, mid, high = taps[a, b, 0], taps[a, b, 1], taps[a, b, 2]
    return jnp.concatenate(
        [jnp.concatenate([mid, low], axis=1), jnp.concatenate([high, mid], axis=1)], axis=0
    )


def clear_corners(out, width):
    blank = jnp.zeros((width, 3 * width), BF16)
    out[3 * width :, : 3 * width] = blank
    out[:width, 3 * width :] = blank


def build_front(taps, w_ref, narrow_ref):
    width = 2 * taps.shape[3]
    clear_corners(w_ref, width)
    for a in range(3):
        for b in range(3):
            block = tap_block(taps, a, b)
            for k in range(2):
                row, col = (a + k) * width, (3 * k + b) * width
                w_ref[row : row + width, col : col + width] = block
            row, col = a * width, b * width
            narrow_ref[row : row + width, col : col + width] = block


def back_weights_kernel(inverse, taps, exponents, w_ref, scale_ref):
    half = taps.shape[3]
    width = 2 * half
    clear_corners(w_ref, width)
    for a in range(3):
        for b in range(3):
            turned = tap_block(taps, a, b).T
            for k in range(2):
                row, col = (2 - a + k) * width, (3 * k + 2 - b) * width
                w_ref[row : row + width, col : col + width] = turned
    lower = lax.broadcasted_iota(jnp.int32, (8, width), 1) < half

    def scale(t, c):
        power = lax.shift_left(jnp.int32(1), exponents[t // 3, t % 3, c] + 2)
        return power.astype(F32) * (0.25 * inverse)

    for s in range(SLOTS):
        t = 2 * (s - 9)
        if s < 9:
            low, high = scale(s, 1), scale(s, 2)
        else:
            low, high = scale(t, 0), scale(t + 1, 0) if t + 1 < 9 else inverse
        scale_ref[s] = jnp.where(lower, low, high)


def plane_taps(taps, slots, bodies, weights):
    size_y, width = bodies[0].shape
    result = jnp.dot(
        jnp.concatenate(bodies, axis=1), weights, preferred_element_type=F32
    )
    for k, p in enumerate(slots):
        for b in range(3):
            col = (3 * k + b) * width
            taps[b, p, PAD : PAD + size_y, :] = result[:, col : col + width]


def rim_taps(taps, slots, triples, weights):
    width = triples[0][0].shape[1]
    rows = 2 * RIM
    last = taps.shape[2] - PAD
    stacked = jnp.concatenate(
        [jnp.concatenate([triple[j] for triple in triples], axis=0) for j in range(3)], axis=1
    )
    result = jnp.dot(stacked, weights, preferred_element_type=F32)
    for k, p in enumerate(slots):
        for b in range(3):
            block = result[k * rows : (k + 1) * rows, b * width : (b + 1) * width]
            taps[b, p, PAD - RIM : PAD, :] = block[:RIM]
            taps[b, p, last : last + RIM, :] = block[RIM:]


def shifted_sum(taps, p, start, rows):
    return (
        taps[0, p, start - 1 : start - 1 + rows, :]
        + taps[1, p, start : start + rows, :]
        + taps[2, p, start + 1 : start + 1 + rows, :]
    )


def activate(taps, wide, p, bias, u_body, u_rim, act, grad_body, grad_rim):
    size_y = taps.shape[2] - 2 * PAD
    spans = [(PAD - RIM, RIM)]
    spans += [(PAD + y, CHUNK) for y in range(0, size_y, CHUNK)]
    spans += [(PAD + size_y, RIM)]
    for start, rows in spans:
        body = rows == CHUNK
        y = start - PAD if body else (0 if start < PAD else RIM)
        preact = shifted_sum(taps, p, start, rows) + bias
        sigma = 0.5 * jnp.tanh(0.5 * preact) + 0.5
        cotangent = (u_body if body else u_rim)[y : y + rows, :].astype(F32)
        rounded = (cotangent * sigma * (1.0 + preact * (1.0 - sigma))).astype(BF16)
        exact = rounded.astype(F32)
        wide[p, start : start + rows, :] = exact
        if body:
            act[y : y + rows, :] = (preact * sigma).astype(BF16)
            grad_body[y : y + rows, :] = rounded
        else:
            grad_rim[y : y + rows, :] = rounded


def body_sum(wide, p):
    size_y, width = wide.shape[1] - 2 * PAD, wide.shape[2]
    return jnp.sum(wide[p, PAD : PAD + size_y, :].reshape(size_y // 8, 8, width), axis=0)


def shifted_grads(wide, p):
    size_y = wide.shape[1] - 2 * PAD
    return jnp.concatenate(
        [wide[p, PAD + 1 - b : PAD + 1 - b + size_y, :].astype(BF16) for b in range(3)], axis=1
    )


def outer(sources, grads):
    return jnp.dot(
        jnp.concatenate([jnp.concatenate(three, axis=0) for three in sources], axis=1),
        jnp.concatenate(grads, axis=0),
        preferred_element_type=F32,
    )


def outer_turned(bodies, grads):
    return lax.dot_general(
        jnp.concatenate(grads, axis=0),
        jnp.concatenate([jnp.concatenate(three, axis=1) for three in bodies], axis=0),
        (((0,), (0,)), ((), ())),
        preferred_element_type=F32,
    )


def oriented(near, far, side, place):
    @pl.when(side == 0)
    def _():
        place(far, near)

    @pl.when(side == 1)
    def _():
        place(near, far)


def beside(axis, near, far, place, clear_low, clear_high):
    index = lax.axis_index(axis)
    oriented(near, far, index % 2, place)
    pl.when(index == 0)(clear_low)
    pl.when(index == lax.axis_size(axis) - 1)(clear_high)


def place_rims(y_near, y_far, f_rim, u_rim, gap):
    low = slice(gap, gap + THIN)
    high = slice(2 * RIM - gap - THIN, 2 * RIM - gap)

    def place(left, right):
        f_rim[:, low, :] = left[:, :THIN, :]
        u_rim[:, low, :] = left[:, THIN:, :]
        f_rim[:, high, :] = right[:, :THIN, :]
        u_rim[:, high, :] = right[:, THIN:, :]

    def clear(rows):
        blank = jnp.zeros((f_rim.shape[0], THIN, f_rim.shape[2]), BF16)
        f_rim[:, rows, :] = blank
        u_rim[:, rows, :] = blank

    for ref in (f_rim, u_rim):
        ref[...] = jnp.zeros(ref.shape, BF16)
    beside("gy", y_near, y_far, place, lambda: clear(low), lambda: clear(high))


def place_planes(x_near, x_far, around):
    def place(below, above):
        around[0] = below[...]
        around[1] = above[...]

    def clear(k):
        around[k] = jnp.zeros(around.shape[1:], BF16)

    beside("gx", x_near, x_far, place, lambda: clear(0), lambda: clear(1))


def rims_kernel(ends, near_ref, far_ref):
    rows = ends.shape[1] // 2

    def hand(tail, head):
        tail[...] = ends[:, rows:, :]
        head[...] = ends[:, :rows, :]

    oriented(far_ref, near_ref, lax.axis_index("gy") % 2, hand)


def planes_kernel(f_ref, y_near, y_far, near_ref, far_ref=None):
    size_x, size_y, width = f_ref.shape
    low = slice(size_y + RIM - THIN, size_y + RIM)
    high = slice(size_y + RIM, size_y + RIM + THIN)

    def fill(out, x):
        out[:size_y] = f_ref[x]
        out[size_y:] = jnp.zeros((2 * RIM, width), BF16)

        def place(left, right):
            out[low] = left[x, :THIN]
            out[high] = right[x, :THIN]

        def clear(rows):
            out[rows] = jnp.zeros((THIN, width), BF16)

        beside("gy", y_near, y_far, place, lambda: clear(low), lambda: clear(high))

    def hand(last, first):
        if last is not None:
            fill(last, size_x - 1)
        if first is not None:
            fill(first, 0)

    oriented(far_ref, near_ref, lax.axis_index("gx") % 2, hand)


def front_kernel(
    f_ref, kernel_ref, offsets, pre_ref, turned, narrow_ref, bias_ref, w_ref, taps
):
    size_x, size_y, width = f_ref.shape
    inner = size_x - 2
    build_front(kernel_ref, w_ref, narrow_ref)
    bias = offsets[...].reshape(1, width // 2)
    bias = jnp.concatenate([bias, bias], axis=1)
    bias_ref[...] = bias
    blank = jnp.zeros((3, inner, RIM, width), F32)
    taps[:, :, PAD - RIM : PAD, :] = blank
    taps[:, :, PAD + size_y : PAD + size_y + RIM, :] = blank
    for p in range(0, inner, 2):
        plane_taps(taps, (p, p + 1), [f_ref[p + j] for j in range(4)], w_ref[...])
        for x in range(0 if p == 0 else p + 2, p + 4):
            turned[x] = f_ref[x].T
        for q in (p, p + 1):
            for y in range(0, size_y, CHUNK):
                pre_ref[q, y : y + CHUNK, :] = shifted_sum(taps, q, PAD + y, CHUNK) + bias


def gradient(preact, cotangent):
    sigma = 0.5 * jnp.tanh(0.5 * preact) + 0.5
    rounded = (
        cotangent.astype(F32) * sigma * (1.0 + preact * (1.0 - sigma))
    ).astype(BF16)
    return preact * sigma, rounded, rounded.astype(F32)


def inner_kernel(
    f_ref, u_ref, y_near, y_far, pre_ref, turned, w_ref, bias_ref,
    act, grad_ref, rim_ref, acc_ref, sums_ref,
    f_rim, u_rim, wide, acc,
):
    size_x, size_y, width = f_ref.shape
    inner = size_x - 2
    gap = RIM - 2 * THIN

    place_rims(y_near, y_far, f_rim, u_rim, gap)
    f_rim[:, gap + THIN : RIM, :] = f_ref[:, :THIN, :]
    f_rim[:, RIM : RIM + THIN, :] = f_ref[:, size_y - THIN :, :]
    bias = bias_ref[...]
    rows = 2 * RIM
    tall = [
        jnp.concatenate([f_rim[x + j] for x in range(inner)], axis=0) for j in range(3)
    ]
    strips = jnp.dot(
        jnp.concatenate(tall, axis=1), w_ref[...], preferred_element_type=F32
    )
    row = lax.broadcasted_iota(jnp.int32, (RIM, width), 0)
    sums = jnp.zeros((8, width), F32)
    for p in range(0, inner, 2):
        for q in (p, p + 1):
            strip = [
                strips[q * rows : (q + 1) * rows, b * width : (b + 1) * width] for b in range(3)
            ]
            for side in range(2):
                part = [tap[side * RIM : (side + 1) * RIM] for tap in strip]
                preact = (
                    pltpu.roll(part[0], 1, 0) + part[1] + pltpu.roll(part[2], RIM - 1, 0) + bias
                )
                _, rounded, exact = gradient(
                    preact, u_rim[q + 1, side * RIM : (side + 1) * RIM, :]
                )
                turn = THIN if side == 0 else RIM - THIN
                exact = pltpu.roll(exact, turn, 0)
                start = PAD - RIM if side == 0 else PAD + size_y
                wide[q, start : start + RIM, :] = exact
                rim_ref[q, side * RIM : (side + 1) * RIM, :] = exact.astype(BF16)
            low = jnp.where(row == 0, pltpu.roll(strip[0][:RIM], RIM - gap - THIN + 1, 0), 0.0)
            high = jnp.where(
                row == RIM - 1, pltpu.roll(strip[2][RIM:], RIM - 1 - THIN, 0), 0.0
            )
            for y in range(0, size_y, CHUNK):
                preact = pre_ref[q, y : y + CHUNK, :]
                if y == 0:
                    preact = jnp.concatenate([preact[:RIM] + low, preact[RIM:]], axis=0)
                if y + CHUNK == size_y:
                    preact = jnp.concatenate([preact[:-RIM], preact[-RIM:] + high], axis=0)
                value, rounded, exact = gradient(preact, u_ref[q + 1, y : y + CHUNK, :])
                wide[q, PAD + y : PAD + y + CHUNK, :] = exact
                act[q, y : y + CHUNK, :] = value.astype(BF16)
                grad_ref[q, y : y + CHUNK, :] = rounded
        grads = [shifted_grads(wide, q) for q in (p, p + 1)]
        sums = sums + body_sum(wide, p) + body_sum(wide, p + 1)
        if p < inner - 2:
            term = outer([[turned[q + j] for j in range(3)] for q in (p, p + 1)], grads)
            if p == 0:
                acc[...] = term
            else:
                acc[...] += term
        if p == inner - 4:
            for a in range(3):
                for b in range(3):
                    here, there = slice(a * width, (a + 1) * width), slice(b * width, (b + 1) * width)
                    acc_ref[there, here] = acc[here, there].T
        if p == inner - 2:
            acc_ref[...] += outer_turned(
                [[f_ref[q + j] for j in range(3)] for q in (p, p + 1)], grads
            )
    sums_ref[...] = sums


def emit_half(acc, sums, which, away, stay):
    outs = [out for out in (away, stay) if out is not None]
    blocks, count, share, width = outs[0].shape
    half = width // 2

    def block(t):
        a, b = t // 3, t % 3
        return acc[b * width : (b + 1) * width, a * width : (a + 1) * width]

    def lower(rows):
        return lax.broadcasted_iota(jnp.int32, (rows, width), 1) < half

    def middle(t):
        whole = block(t)
        rolled = pltpu.roll(whole[half:], half, 1)
        return whole[:half] + jnp.where(lower(half), rolled, 0.0)

    def low_pair(t):
        low = block(t)[half:]
        if t + 1 < 9:
            return jnp.where(lower(half), low, pltpu.roll(block(t + 1)[half:], half, 1))
        both = jnp.sum(sums, axis=0, keepdims=True)
        both = jnp.broadcast_to(both + pltpu.roll(both, half, 1), (share, width))
        turned = [
            pltpu.roll(both, (half - d * share) % width, 1) for d in range(2 * blocks)
        ]
        return jnp.where(lower(half), low, jnp.concatenate(turned, axis=0))

    def write(bit):
        def put(s, value):
            for k in range(blocks):
                for out, d in ((away, 2 * k + 1 - bit), (stay, 2 * k + bit)):
                    if out is not None:
                        out[k, s] = value[d * share : (d + 1) * share]

        @pl.when(which == 0)
        def _():
            for s in range(count):
                put(s, middle(s))

        @pl.when(which == 1)
        def _():
            for t in range(count, 9):
                put(t - count, middle(t))
            for t in range(0, 9, 2):
                put(9 + t // 2 - count, low_pair(t))

    place = lax.axis_index("dp") % 2
    pl.when(place == 0)(lambda: write(0))
    pl.when(place == 1)(lambda: write(1))


def rest_kernel(acc, sums, send_stay, keep_away, keep_stay):
    kept = half_kept()
    emit_half(acc, sums[...], 1 - kept, None, send_stay)
    emit_half(acc, sums[...], kept, keep_away, keep_stay)


def edge_kernel(
    f_ref, u_ref, y_near, y_far, x_near, x_far, w_ref, bias_ref, acc_ref, sums_ref,
    act, first_ref, last_ref, acc, bias_sums, send_ref, near_ref, *refs
):
    far_ref = refs[0] if len(refs) > 5 else None
    f_rim, u_rim, around, taps, wide = refs[-5:]
    size_x, size_y, width = f_ref.shape
    x_side = lax.axis_index("gx") % 2
    place_rims(y_near, y_far, f_rim, u_rim, RIM - THIN)
    place_planes(x_near, x_far, around)
    bias = bias_ref[...]
    weights = w_ref[...]
    tall = size_y + 2 * RIM
    bodies = [
        [around[0, :size_y], f_ref[0], f_ref[1]],
        [f_ref[size_x - 2], f_ref[size_x - 1], around[1, :size_y]],
    ]
    rims = [
        [around[0, size_y:tall], f_rim[0], f_rim[1]],
        [f_rim[size_x - 2], f_rim[size_x - 1], around[1, size_y:tall]],
    ]
    rim_taps(taps, (0, 1), rims, weights)
    for p in range(2):
        plane_taps(taps, (p,), bodies[p], weights)
    outs = (first_ref, last_ref)
    places = (0, size_x - 1)
    for p in range(2):
        x = places[p]
        activate(
            taps, wide, p, bias, u_ref.at[x], u_rim.at[x], act.at[p],
            outs[p].at[pl.ds(0, size_y)], outs[p].at[pl.ds(size_y, 2 * RIM)],
        )
    acc[...] = acc_ref[...] + outer_turned(bodies, [shifted_grads(wide, p) for p in range(2)])
    sums = sums_ref[...] + body_sum(wide, 0) + body_sum(wide, 1)

    def hand(last, first):
        if last is not None:
            last[...] = last_ref[...]
        if first is not None:
            first[...] = first_ref[...]

    oriented(far_ref, near_ref, x_side, hand)

    bias_sums[...] = sums
    emit_half(acc, sums, 1 - half_kept(), send_ref, None)


def store_activation(act_inner, act_edges, act_hbm, sems):
    size_x = act_hbm.shape[0]
    copies = [
        pltpu.make_async_copy(act_edges.at[0], act_hbm.at[0], sems.at[0]),
        pltpu.make_async_copy(act_edges.at[1], act_hbm.at[size_x - 1], sems.at[1]),
        pltpu.make_async_copy(act_inner, act_hbm.at[pl.ds(1, size_x - 2)], sems.at[2]),
    ]
    for copy in copies:
        copy.start()
    return copies


def back_kernel(pairs, edges, stored, grad_ref, rim_ref, first_ref, last_ref, *refs):
    x_near, x_far = refs[:2] if edges else (None, None)
    w_ref = refs[2 * edges]
    out_hbm, *act_hbm, out, taps, around, sems = refs[-5 - stored :]
    copies = []
    if stored:
        copies = store_activation(*refs[1:3], act_hbm[0], sems.at[pl.ds(out.shape[0], 3)])
    size_y, width = grad_ref.shape[1:]
    size_x = grad_ref.shape[0] + 2
    tall = size_y + 2 * RIM

    def body(x):
        if x == 0:
            return first_ref[:size_y]
        if x == size_x - 1:
            return last_ref[:size_y]
        if x < 0 or x >= size_x:
            return around[int(x > 0), :size_y]
        return grad_ref[x - 1]

    def rim(x):
        if x == 0:
            return first_ref[size_y:tall]
        if x == size_x - 1:
            return last_ref[size_y:tall]
        if x < 0 or x >= size_x:
            return around[int(x > 0), size_y:tall]
        return rim_ref[x - 1]

    if edges:
        place_planes(x_near, x_far, around)
    narrow = w_ref[: 3 * width, : 3 * width]
    planes = [x for first in pairs for x in (first, first + 1)]
    planes += [0, size_x - 1] if edges else []
    rim_taps(taps, range(len(planes)), [[rim(x + j) for j in (-1, 0, 1)] for x in planes], narrow)
    stores = []

    def multiply(k):
        x = planes[k]
        if planes[k + 1] == x + 1:
            plane_taps(taps, (k, k + 1), [body(x + j) for j in (-1, 0, 1, 2)], w_ref[...])
        else:
            for i in (k, k + 1):
                plane_taps(taps, (i,), [body(planes[i] + j) for j in (-1, 0, 1)], narrow)

    multiply(0)
    for k in range(0, len(planes), 2):
        if k + 2 < len(planes):
            multiply(k + 2)
        for i in (k, k + 1):
            for y in range(0, size_y, CHUNK):
                out[i, y : y + CHUNK, :] = shifted_sum(taps, i, PAD + y, CHUNK).astype(BF16)
            stores.append(
                pltpu.make_async_copy(out.at[i], out_hbm.at[planes[i]], sems.at[i])
            )
            stores[-1].start()
    for copy in stores + copies:
        copy.wait()


def split_kernel(step, *refs):
    *terms, keep_ref, send_ref = refs
    total = sum_refs(terms)
    bit = (lax.axis_index("dp") // step) % 2

    def place(first, second):
        for k in range(keep_ref.shape[0]):
            keep_ref[k] = total[2 * k + first]
            send_ref[k] = total[2 * k + second].astype(BF16)

    pl.when(bit == 0)(lambda: place(0, 1))
    pl.when(bit == 1)(lambda: place(1, 0))


def sum_refs(terms):
    total = terms[0][...].astype(F32)
    for term in terms[1:]:
        total = total + term[...].astype(F32)
    return total


def add_kernel(*refs):
    *terms, total_ref = refs
    total_ref[...] = sum_refs(terms).astype(total_ref.dtype)


def finish_kernel(own, other, scale_ref, grad_ref, bias_ref):
    share, half = grad_ref.shape[1:]

    def emit(first, second):
        for s in range(SLOTS):
            block = (first if s < SLOTS // 2 else second)[s % (SLOTS // 2)] * scale_ref[s, :1]
            low, high = block[:, :half], pltpu.roll(block, half, 1)[:, :half]
            t = 2 * (s - 9)
            grad_ref[3 * s + 1 if s < 9 else 3 * t] = low.astype(BF16)
            if s < SLOTS - 1:
                grad_ref[3 * s + 2 if s < 9 else 3 * t + 3] = high.astype(BF16)
            else:
                bias_ref[...] = high[:1, :share]

    kept = half_kept()

    @pl.when(kept == 0)
    def _():
        emit(own, other)

    @pl.when(kept == 1)
    def _():
        emit(other, own)


def shape(*dims, dtype=BF16):
    return jax.ShapeDtypeStruct(dims, dtype)


def grant(mebibytes):
    return pltpu.CompilerParams(vmem_limit_bytes=mebibytes * 2**20)


def cost(microseconds):
    return pl.CostEstimate(
        flops=int(1.1e9 * microseconds), bytes_accessed=0, transcendentals=0
    )


def local(features, kernel, offsets, upstream, grad_exponents):
    cells, cotangent = features[0], upstream[0]
    size_x, size_y, width = cells.shape
    half = width // 2
    tall, rows = size_y + 2 * RIM, size_y + 2 * PAD
    parts = lax.axis_size("dp")
    share = half // parts
    sources = (cells, cotangent)
    ends = jnp.concatenate(
        [source[:, :THIN] for source in sources] + [source[:, size_y - THIN :] for source in sources],
        axis=1,
    )
    rim_near, rim_far = pl.pallas_call(
        rims_kernel,
        out_shape=(shape(size_x, 2 * THIN, width),) * 2,
        in_specs=[VMEM],
        out_specs=(VMEM, VMEM),
        compiler_params=grant(1),
        cost_estimate=cost(3.0),
        name="pack_rims",
    )(ends)
    y_near = swap(rim_near, "gy", 0)
    y_far = swap(rim_far, "gy", 1)

    voxels = (
        features.shape[0] * parts * size_x * lax.axis_size("gx") * size_y * lax.axis_size("gy") * 2
    )
    def back_weights(taps):
        return pl.pallas_call(
            lambda *refs: back_weights_kernel(1.0 / math.sqrt(voxels), *refs),
            out_shape=(shape(4 * width, 6 * width), shape(SLOTS, 8, width, dtype=F32)),
            in_specs=[VMEM, SMEM],
            out_specs=(VMEM, VMEM),
            compiler_params=grant(4),
            cost_estimate=cost(1.0),
            name="back_weights",
        )(taps, grad_exponents)

    inner = size_x - 2
    preact, turned, forward_weights, bias = pl.pallas_call(
        front_kernel,
        out_shape=(
            shape(inner, size_y, width, dtype=F32),
            shape(size_x, width, size_y),
            shape(3 * width, 3 * width),
            shape(1, width, dtype=F32),
        ),
        in_specs=[VMEM] * 3,
        out_specs=(VMEM,) * 4,
        scratch_shapes=[
            pltpu.VMEM((4 * width, 6 * width), BF16),
            pltpu.VMEM((3, inner, rows, width), F32),
        ],
        compiler_params=grant(16),
        cost_estimate=cost(2.0),
        name="front_planes",
    )(cells, kernel, offsets)

    many = lax.axis_size("gx") > 2
    plane_sends = pl.pallas_call(
        planes_kernel,
        out_shape=(shape(tall, width),) * (1 + many),
        in_specs=[VMEM] * 3,
        out_specs=(VMEM,) * (1 + many),
        compiler_params=grant(1),
        cost_estimate=cost(0.1),
        name="pack_planes",
    )(cells, y_near, y_far)
    x_near = swap(plane_sends[0], "gx", 0)
    x_far = swap(plane_sends[1], "gx", 1) if many else x_near

    rims = [
        pltpu.VMEM((size_x, 2 * RIM, width), BF16),
        pltpu.VMEM((size_x, 2 * RIM, width), BF16),
    ]
    act_inner, grad, grad_rim, acc, sums = pl.pallas_call(
        inner_kernel,
        out_shape=(
            shape(inner, size_y, width),
            shape(inner, size_y, width),
            shape(inner, 2 * RIM, width),
            shape(3 * width, 3 * width, dtype=F32),
            shape(8, width, dtype=F32),
        ),
        in_specs=[VMEM] * 8,
        out_specs=(VMEM,) * 5,
        scratch_shapes=rims + [
            pltpu.VMEM((inner, rows, width), F32),
            pltpu.VMEM((3 * width, 3 * width), F32),
        ],
        compiler_params=grant(12),
        cost_estimate=cost(3.0),
        name="inner_planes",
    )(cells, cotangent, y_near, y_far, preact, turned, forward_weights, bias)

    blocks = (parts // 2, SLOTS // 2, share, width)
    act_edges, first, final, acc, sums, send, *edges = pl.pallas_call(
        edge_kernel,
        out_shape=(
            shape(2, size_y, width),
            shape(tall, width),
            shape(tall, width),
            shape(3 * width, 3 * width, dtype=F32),
            shape(8, width, dtype=F32),
            shape(*blocks, dtype=F32),
        )
        + (shape(tall, width),) * (1 + many),
        in_specs=[VMEM] * 10,
        out_specs=(VMEM,) * (7 + many),
        scratch_shapes=rims + [
            pltpu.VMEM((2, tall, width), BF16),
            pltpu.VMEM((3, 2, rows, width), F32),
            pltpu.VMEM((2, rows, width), F32),
        ],
        compiler_params=grant(12),
        cost_estimate=cost(2.0),
        name="edge_planes",
    )(
        cells, cotangent, y_near, y_far, x_near, x_far, forward_weights, bias, acc, sums,
    )

    def back(pairs, previous, after, beyond=(), acts=()):
        edges, stored = len(beyond) > 0, len(acts) > 0
        operands = [grad, grad_rim, first, final, *beyond, backward_weights, *acts]
        specs = [VMEM] * len(operands)
        aliases = {}
        if previous is not None:
            aliases = {len(operands): 0}
            operands.append(previous)
            specs.append(ANY)
        operands.append(after)
        specs.append(ANY)
        planes = 2 * len(pairs) + 2 * edges
        results = pl.pallas_call(
            lambda *refs: back_kernel(pairs, edges, stored, *refs),
            out_shape=(shape(size_x, size_y, width),) * (1 + stored),
            in_specs=specs,
            out_specs=(ANY,) * (1 + stored),
            scratch_shapes=[
                pltpu.VMEM((planes, size_y, width), BF16),
                pltpu.VMEM((3, planes, rows, width), F32),
                pltpu.VMEM((2, tall, width), BF16),
                pltpu.SemaphoreType.DMA((planes + 3 * stored,)),
            ],
            input_output_aliases=aliases,
            compiler_params=grant(12),
            cost_estimate=cost(2.5 if planes > 4 else 1.0),
            name="input_grad",
        )(*operands)
        return results if stored else results[0]

    starts = list(range(1, size_x - 1, 2))
    cut = len(starts) - 2
    def add(terms, dtype):
        return pl.pallas_call(
            add_kernel,
            out_shape=shape(*terms[0].shape, dtype=dtype),
            in_specs=[VMEM] * len(terms),
            out_specs=VMEM,
            compiler_params=grant(2),
            cost_estimate=cost(0.1),
            name="add_sums",
        )(*terms)

    def split(terms, step):
        dims = (terms[0].shape[0] // 2,) + terms[0].shape[1:]
        return pl.pallas_call(
            lambda *refs: split_kernel(step, *refs),
            out_shape=(shape(*dims, dtype=F32), shape(*dims)),
            in_specs=[VMEM] * len(terms),
            out_specs=(VMEM, VMEM),
            compiler_params=grant(2),
            cost_estimate=cost(0.1),
            name="split_sums",
        )(*terms)

    rounds = [("dp", 1 << i) for i in range(parts.bit_length() - 1)]
    rounds += [("gy", 1 << i) for i in range(1, lax.axis_size("gy").bit_length() - 1)]
    rounds += [("gx", 1 << i) for i in range(lax.axis_size("gx").bit_length() - 1)]
    away = swap(send, "gy", 0)
    send_stay, keep_away, keep_stay = pl.pallas_call(
        rest_kernel,
        out_shape=(shape(*blocks, dtype=F32),) * 3,
        in_specs=[VMEM, VMEM],
        out_specs=(VMEM,) * 3,
        compiler_params=grant(4),
        cost_estimate=cost(0.7),
        name="rest_of_sums",
    )(acc, sums)
    terms = [keep_stay, swap(send_stay, "gy", 0)]
    input_grad = None
    for index, (axis, step) in enumerate(rounds):
        if index == 0:
            send = add([keep_away, away], BF16)
        elif axis == "dp":
            total, send = split(terms, step)
            terms = [total]
        else:
            send = add(terms, BF16)
            terms = [send]
        if index == 0:
            later, send = lax.optimization_barrier((kernel, send))
            backward_weights, scales = back_weights(later)
        received = exchange(send, axis, step)
        if index == 0:
            input_grad = back(starts[:2], None, send)
            received, input_grad = lax.optimization_barrier((received, input_grad))
            *edges, backward_weights = lax.optimization_barrier((*edges, backward_weights))
            back_near = swap(edges[0], "gx", 0)
            back_far = swap(edges[1], "gx", 1) if many else back_near
        if index == len(rounds) - 2:
            input_grad, activation = back(
                starts[2:cut], input_grad, send, acts=(act_inner, act_edges)
            )
            received, input_grad = lax.optimization_barrier((received, input_grad))
        if index == len(rounds) - 1:
            input_grad = back(starts[cut:], input_grad, send, beyond=(back_near, back_far))
            received, input_grad = lax.optimization_barrier((received, input_grad))
        terms.append(received)
    total = add(terms, F32).reshape(SLOTS // 2, share, width)
    other = swap(total, "gy", 0)

    kernel_grad, bias_grad = pl.pallas_call(
        finish_kernel,
        out_shape=(shape(27, share, half), shape(1, share, dtype=F32)),
        in_specs=[VMEM] * 3,
        out_specs=(VMEM, VMEM),
        compiler_params=grant(4),
        name="scale_weight_grad",
    )(total, other, scales)
    return (
        activation[None],
        input_grad[None],
        jnp.swapaxes(kernel_grad.reshape(3, 3, 3, share, half), 3, 4),
        bias_grad.reshape(share),
    )


def solution(mesh):
    placed = (P("dp", "gx", "gy", None), P(), P(), P("dp", "gx", "gy", None), P())
    return jax.shard_map(
        local,
        mesh=mesh,
        in_specs=placed,
        out_specs=(
            P("dp", "gx", "gy", None),
            P("dp", "gx", "gy", None),
            P(None, None, None, None, "dp"),
            P("dp"),
        ),
        check_vma=False,
    )
```

```python
import math

import jax
import jax.numpy as jnp
from jax import lax
from jax.experimental import pallas as pl
from jax.experimental.pallas import tpu as pltpu
from jax.sharding import PartitionSpec as P

RIM = 8
THIN = 2
PAD = 16
CHUNK = 64
SLOTS = 14
VMEM = pl.BlockSpec(memory_space=pltpu.VMEM)
SMEM = pl.BlockSpec(memory_space=pltpu.SMEM)
ANY = pl.BlockSpec(memory_space=pl.ANY)
BF16, F32 = jnp.bfloat16, jnp.float32


def swap(value, axis, first):
    count = lax.axis_size(axis)
    links = []
    for low in range(first, count, 2):
        high = (low + 1) % count
        links += [(low, high), (high, low)]
    return lax.ppermute(value, axis, links)


def exchange(value, axis, step):
    axes = ("gx", "gy", "dp")
    sizes = [lax.axis_size(name) for name in axes]
    stride = {name: math.prod(sizes[i + 1 :]) for i, name in enumerate(axes)}
    flip = (step * stride[axis]) ^ stride["gy"]
    return lax.ppermute(value, axes, [(i, i ^ flip) for i in range(math.prod(sizes))])


def half_kept():
    side = lax.axis_index("gy") % 2
    for axis, first in (("gx", 1), ("gy", 2), ("dp", 1)):
        step = first
        while step < lax.axis_size(axis):
            side = side + lax.axis_index(axis) // step
            step *= 2
    return side % 2


def tap_block(taps, a, b):
    low, mid, high = taps[a, b, 0], taps[a, b, 1], taps[a, b, 2]
    return jnp.concatenate(
        [jnp.concatenate([mid, low], axis=1), jnp.concatenate([high, mid], axis=1)], axis=0
    )


def clear_corners(out, width):
    blank = jnp.zeros((width, 3 * width), BF16)
    out[3 * width :, : 3 * width] = blank
    out[:width, 3 * width :] = blank


def build_front(taps, w_ref, narrow_ref):
    width = 2 * taps.shape[3]
    clear_corners(w_ref, width)
    for a in range(3):
        for b in range(3):
            block = tap_block(taps, a, b)
            for k in range(2):
                row, col = (a + k) * width, (3 * k + b) * width
                w_ref[row : row + width, col : col + width] = block
            row, col = a * width, b * width
            narrow_ref[row : row + width, col : col + width] = block


def back_weights_kernel(inverse, taps, exponents, w_ref, scale_ref):
    half = taps.shape[3]
    width = 2 * half
    clear_corners(w_ref, width)
    for a in range(3):
        for b in range(3):
            turned = tap_block(taps, a, b).T
            for k in range(2):
                row, col = (2 - a + k) * width, (3 * k + 2 - b) * width
                w_ref[row : row + width, col : col + width] = turned
    lower = lax.broadcasted_iota(jnp.int32, (8, width), 1) < half

    def scale(t, c):
        power = lax.shift_left(jnp.int32(1), exponents[t // 3, t % 3, c] + 2)
        return power.astype(F32) * (0.25 * inverse)

    for s in range(SLOTS):
        t = 2 * (s - 9)
        if s < 9:
            low, high = scale(s, 1), scale(s, 2)
        else:
            low, high = scale(t, 0), scale(t + 1, 0) if t + 1 < 9 else inverse
        scale_ref[s] = jnp.where(lower, low, high)


def plane_taps(taps, slots, bodies, weights):
    size_y, width = bodies[0].shape
    result = jnp.dot(
        jnp.concatenate(bodies, axis=1), weights, preferred_element_type=F32
    )
    for k, p in enumerate(slots):
        for b in range(3):
            col = (3 * k + b) * width
            taps[b, p, PAD : PAD + size_y, :] = result[:, col : col + width]


def rim_taps(taps, slots, triples, weights):
    width = triples[0][0].shape[1]
    rows = 2 * RIM
    last = taps.shape[2] - PAD
    stacked = jnp.concatenate(
        [jnp.concatenate([triple[j] for triple in triples], axis=0) for j in range(3)], axis=1
    )
    result = jnp.dot(stacked, weights, preferred_element_type=F32)
    for k, p in enumerate(slots):
        for b in range(3):
            block = result[k * rows : (k + 1) * rows, b * width : (b + 1) * width]
            taps[b, p, PAD - RIM : PAD, :] = block[:RIM]
            taps[b, p, last : last + RIM, :] = block[RIM:]


def shifted_sum(taps, p, start, rows):
    return (
        taps[0, p, start - 1 : start - 1 + rows, :]
        + taps[1, p, start : start + rows, :]
        + taps[2, p, start + 1 : start + 1 + rows, :]
    )


def activate(taps, wide, p, bias, u_body, u_rim, act, grad_body, grad_rim):
    size_y = taps.shape[2] - 2 * PAD
    spans = [(PAD - RIM, RIM)]
    spans += [(PAD + y, CHUNK) for y in range(0, size_y, CHUNK)]
    spans += [(PAD + size_y, RIM)]
    for start, rows in spans:
        body = rows == CHUNK
        y = start - PAD if body else (0 if start < PAD else RIM)
        preact = shifted_sum(taps, p, start, rows) + bias
        sigma = 0.5 * jnp.tanh(0.5 * preact) + 0.5
        cotangent = (u_body if body else u_rim)[y : y + rows, :].astype(F32)
        rounded = (cotangent * sigma * (1.0 + preact * (1.0 - sigma))).astype(BF16)
        exact = rounded.astype(F32)
        wide[p, start : start + rows, :] = exact
        if body:
            act[y : y + rows, :] = (preact * sigma).astype(BF16)
            grad_body[y : y + rows, :] = rounded
        else:
            grad_rim[y : y + rows, :] = rounded


def body_sum(wide, p):
    size_y, width = wide.shape[1] - 2 * PAD, wide.shape[2]
    return jnp.sum(wide[p, PAD : PAD + size_y, :].reshape(size_y // 8, 8, width), axis=0)


def shifted_grads(wide, p):
    size_y = wide.shape[1] - 2 * PAD
    return jnp.concatenate(
        [wide[p, PAD + 1 - b : PAD + 1 - b + size_y, :].astype(BF16) for b in range(3)], axis=1
    )


def outer(sources, grads):
    return jnp.dot(
        jnp.concatenate([jnp.concatenate(three, axis=0) for three in sources], axis=1),
        jnp.concatenate(grads, axis=0),
        preferred_element_type=F32,
    )


def outer_turned(bodies, grads):
    return lax.dot_general(
        jnp.concatenate(grads, axis=0),
        jnp.concatenate([jnp.concatenate(three, axis=1) for three in bodies], axis=0),
        (((0,), (0,)), ((), ())),
        preferred_element_type=F32,
    )


def oriented(near, far, side, place):
    @pl.when(side == 0)
    def _():
        place(far, near)

    @pl.when(side == 1)
    def _():
        place(near, far)


def beside(axis, near, far, place, clear_low, clear_high):
    index = lax.axis_index(axis)
    oriented(near, far, index % 2, place)
    pl.when(index == 0)(clear_low)
    pl.when(index == lax.axis_size(axis) - 1)(clear_high)


def place_rims(y_near, y_far, f_rim, u_rim, gap):
    low = slice(gap, gap + THIN)
    high = slice(2 * RIM - gap - THIN, 2 * RIM - gap)

    def place(left, right):
        f_rim[:, low, :] = left[:, :THIN, :]
        u_rim[:, low, :] = left[:, THIN:, :]
        f_rim[:, high, :] = right[:, :THIN, :]
        u_rim[:, high, :] = right[:, THIN:, :]

    def clear(rows):
        blank = jnp.zeros((f_rim.shape[0], THIN, f_rim.shape[2]), BF16)
        f_rim[:, rows, :] = blank
        u_rim[:, rows, :] = blank

    for ref in (f_rim, u_rim):
        ref[...] = jnp.zeros(ref.shape, BF16)
    beside("gy", y_near, y_far, place, lambda: clear(low), lambda: clear(high))


def place_planes(x_near, x_far, around):
    def place(below, above):
        around[0] = below[...]
        around[1] = above[...]

    def clear(k):
        around[k] = jnp.zeros(around.shape[1:], BF16)

    beside("gx", x_near, x_far, place, lambda: clear(0), lambda: clear(1))


def rims_kernel(ends, near_ref, far_ref):
    rows = ends.shape[1] // 2

    def hand(tail, head):
        tail[...] = ends[:, rows:, :]
        head[...] = ends[:, :rows, :]

    oriented(far_ref, near_ref, lax.axis_index("gy") % 2, hand)


def planes_kernel(f_ref, y_near, y_far, near_ref, far_ref=None):
    size_x, size_y, width = f_ref.shape
    low = slice(size_y + RIM - THIN, size_y + RIM)
    high = slice(size_y + RIM, size_y + RIM + THIN)

    def fill(out, x):
        out[:size_y] = f_ref[x]
        out[size_y:] = jnp.zeros((2 * RIM, width), BF16)

        def place(left, right):
            out[low] = left[x, :THIN]
            out[high] = right[x, :THIN]

        def clear(rows):
            out[rows] = jnp.zeros((THIN, width), BF16)

        beside("gy", y_near, y_far, place, lambda: clear(low), lambda: clear(high))

    def hand(last, first):
        if last is not None:
            fill(last, size_x - 1)
        if first is not None:
            fill(first, 0)

    oriented(far_ref, near_ref, lax.axis_index("gx") % 2, hand)


def front_kernel(
    f_ref, kernel_ref, offsets, pre_ref, turned, narrow_ref, bias_ref, w_ref, taps
):
    size_x, size_y, width = f_ref.shape
    inner = size_x - 2
    build_front(kernel_ref, w_ref, narrow_ref)
    bias = offsets[...].reshape(1, width // 2)
    bias = jnp.concatenate([bias, bias], axis=1)
    bias_ref[...] = bias
    blank = jnp.zeros((3, inner, RIM, width), F32)
    taps[:, :, PAD - RIM : PAD, :] = blank
    taps[:, :, PAD + size_y : PAD + size_y + RIM, :] = blank
    for p in range(0, inner, 2):
        plane_taps(taps, (p, p + 1), [f_ref[p + j] for j in range(4)], w_ref[...])
        for x in range(0 if p == 0 else p + 2, p + 4):
            turned[x] = f_ref[x].T
        for q in (p, p + 1):
            for y in range(0, size_y, CHUNK):
                pre_ref[q, y : y + CHUNK, :] = shifted_sum(taps, q, PAD + y, CHUNK) + bias


def gradient(preact, cotangent):
    sigma = 0.5 * jnp.tanh(0.5 * preact) + 0.5
    rounded = (
        cotangent.astype(F32) * sigma * (1.0 + preact * (1.0 - sigma))
    ).astype(BF16)
    return preact * sigma, rounded, rounded.astype(F32)


def inner_kernel(
    f_ref, u_ref, y_near, y_far, pre_ref, turned, w_ref, bias_ref,
    act, grad_ref, rim_ref, acc_ref, sums_ref, part_ref,
    f_rim, u_rim, wide, acc,
):
    size_x, size_y, width = f_ref.shape
    inner = size_x - 2
    gap = RIM - 2 * THIN

    place_rims(y_near, y_far, f_rim, u_rim, gap)
    f_rim[:, gap + THIN : RIM, :] = f_ref[:, :THIN, :]
    f_rim[:, RIM : RIM + THIN, :] = f_ref[:, size_y - THIN :, :]
    for p, (x, row) in enumerate(((0, width), (size_x - 2, 0))):
        part_ref[p] = jnp.dot(
            jnp.concatenate([f_ref[x], f_ref[x + 1]], axis=1),
            w_ref[row : row + 2 * width, :],
            preferred_element_type=F32,
        )
    bias = bias_ref[...]
    rows = 2 * RIM
    tall = [
        jnp.concatenate([f_rim[x + j] for x in range(inner)], axis=0) for j in range(3)
    ]
    strips = jnp.dot(
        jnp.concatenate(tall, axis=1), w_ref[...], preferred_element_type=F32
    )
    row = lax.broadcasted_iota(jnp.int32, (RIM, width), 0)
    sums = jnp.zeros((8, width), F32)
    for p in range(0, inner, 2):
        for q in (p, p + 1):
            strip = [
                strips[q * rows : (q + 1) * rows, b * width : (b + 1) * width] for b in range(3)
            ]
            for side in range(2):
                part = [tap[side * RIM : (side + 1) * RIM] for tap in strip]
                preact = (
                    pltpu.roll(part[0], 1, 0) + part[1] + pltpu.roll(part[2], RIM - 1, 0) + bias
                )
                _, rounded, exact = gradient(
                    preact, u_rim[q + 1, side * RIM : (side + 1) * RIM, :]
                )
                turn = THIN if side == 0 else RIM - THIN
                exact = pltpu.roll(exact, turn, 0)
                start = PAD - RIM if side == 0 else PAD + size_y
                wide[q, start : start + RIM, :] = exact
                rim_ref[q, side * RIM : (side + 1) * RIM, :] = exact.astype(BF16)
            low = jnp.where(row == 0, pltpu.roll(strip[0][:RIM], RIM - gap - THIN + 1, 0), 0.0)
            high = jnp.where(
                row == RIM - 1, pltpu.roll(strip[2][RIM:], RIM - 1 - THIN, 0), 0.0
            )
            for y in range(0, size_y, CHUNK):
                preact = pre_ref[q, y : y + CHUNK, :]
                if y == 0:
                    preact = jnp.concatenate([preact[:RIM] + low, preact[RIM:]], axis=0)
                if y + CHUNK == size_y:
                    preact = jnp.concatenate([preact[:-RIM], preact[-RIM:] + high], axis=0)
                value, rounded, exact = gradient(preact, u_ref[q + 1, y : y + CHUNK, :])
                wide[q, PAD + y : PAD + y + CHUNK, :] = exact
                act[q, y : y + CHUNK, :] = value.astype(BF16)
                grad_ref[q, y : y + CHUNK, :] = rounded
        grads = [shifted_grads(wide, q) for q in (p, p + 1)]
        sums = sums + body_sum(wide, p) + body_sum(wide, p + 1)
        if p < inner - 2:
            term = outer([[turned[q + j] for j in range(3)] for q in (p, p + 1)], grads)
            if p == 0:
                acc[...] = term
            else:
                acc[...] += term
        if p == inner - 4:
            for a in range(3):
                for b in range(3):
                    here, there = slice(a * width, (a + 1) * width), slice(b * width, (b + 1) * width)
                    acc_ref[there, here] = acc[here, there].T
        if p == inner - 2:
            acc_ref[...] += outer_turned(
                [[f_ref[q + j] for j in range(3)] for q in (p, p + 1)], grads
            )
    sums_ref[...] = sums


def emit_half(acc, sums, which, away, stay):
    outs = [out for out in (away, stay) if out is not None]
    blocks, count, share, width = outs[0].shape
    half = width // 2

    def block(t):
        a, b = t // 3, t % 3
        return acc[b * width : (b + 1) * width, a * width : (a + 1) * width]

    def lower(rows):
        return lax.broadcasted_iota(jnp.int32, (rows, width), 1) < half

    def middle(t):
        whole = block(t)
        rolled = pltpu.roll(whole[half:], half, 1)
        return whole[:half] + jnp.where(lower(half), rolled, 0.0)

    def low_pair(t):
        low = block(t)[half:]
        if t + 1 < 9:
            return jnp.where(lower(half), low, pltpu.roll(block(t + 1)[half:], half, 1))
        both = jnp.sum(sums, axis=0, keepdims=True)
        both = jnp.broadcast_to(both + pltpu.roll(both, half, 1), (share, width))
        turned = [
            pltpu.roll(both, (half - d * share) % width, 1) for d in range(2 * blocks)
        ]
        return jnp.where(lower(half), low, jnp.concatenate(turned, axis=0))

    def write(bit):
        def put(s, value):
            for k in range(blocks):
                for out, d in ((away, 2 * k + 1 - bit), (stay, 2 * k + bit)):
                    if out is not None:
                        out[k, s] = value[d * share : (d + 1) * share].astype(out.dtype)

        @pl.when(which == 0)
        def _():
            for s in range(count):
                put(s, middle(s))

        @pl.when(which == 1)
        def _():
            for t in range(count, 9):
                put(t - count, middle(t))
            for t in range(0, 9, 2):
                put(9 + t // 2 - count, low_pair(t))

    place = lax.axis_index("dp") % 2
    pl.when(place == 0)(lambda: write(0))
    pl.when(place == 1)(lambda: write(1))


def rest_kernel(acc, sums, send_stay, keep_away, keep_stay):
    kept = half_kept()
    emit_half(acc, sums[...], 1 - kept, None, send_stay)
    emit_half(acc, sums[...], kept, keep_away, keep_stay)


def edge_kernel(
    f_ref, u_ref, y_near, y_far, x_near, x_far, w_ref, bias_ref, acc_ref, sums_ref,
    part_ref, act, first_ref, last_ref, acc, bias_sums, send_ref, near_ref, *refs
):
    far_ref = refs[0] if len(refs) > 5 else None
    f_rim, u_rim, around, taps, wide = refs[-5:]
    size_x, size_y, width = f_ref.shape
    x_side = lax.axis_index("gx") % 2
    place_rims(y_near, y_far, f_rim, u_rim, RIM - THIN)
    place_planes(x_near, x_far, around)
    bias = bias_ref[...]
    weights = w_ref[...]
    tall = size_y + 2 * RIM
    bodies = [
        [around[0, :size_y], f_ref[0], f_ref[1]],
        [f_ref[size_x - 2], f_ref[size_x - 1], around[1, :size_y]],
    ]
    rims = [
        [around[0, size_y:tall], f_rim[0], f_rim[1]],
        [f_rim[size_x - 2], f_rim[size_x - 1], around[1, size_y:tall]],
    ]
    rim_taps(taps, (0, 1), rims, weights)
    for p in range(2):
        row = 2 * p * width
        result = part_ref[p] + jnp.dot(
            around[p, :size_y], weights[row : row + width], preferred_element_type=F32
        )
        for b in range(3):
            taps[b, p, PAD : PAD + size_y, :] = result[:, b * width : (b + 1) * width]
    outs = (first_ref, last_ref)
    places = (0, size_x - 1)
    for p in range(2):
        x = places[p]
        activate(
            taps, wide, p, bias, u_ref.at[x], u_rim.at[x], act.at[p],
            outs[p].at[pl.ds(0, size_y)], outs[p].at[pl.ds(size_y, 2 * RIM)],
        )
    acc[...] = acc_ref[...] + outer_turned(bodies, [shifted_grads(wide, p) for p in range(2)])
    sums = sums_ref[...] + body_sum(wide, 0) + body_sum(wide, 1)

    def hand(last, first):
        if last is not None:
            last[...] = last_ref[...]
        if first is not None:
            first[...] = first_ref[...]

    oriented(far_ref, near_ref, x_side, hand)

    bias_sums[...] = sums
    emit_half(acc, sums, 1 - half_kept(), send_ref, None)


def store_activation(act_inner, act_edges, act_hbm, sems):
    size_x = act_hbm.shape[0]
    copies = [
        pltpu.make_async_copy(act_edges.at[0], act_hbm.at[0], sems.at[0]),
        pltpu.make_async_copy(act_edges.at[1], act_hbm.at[size_x - 1], sems.at[1]),
        pltpu.make_async_copy(act_inner, act_hbm.at[pl.ds(1, size_x - 2)], sems.at[2]),
    ]
    for copy in copies:
        copy.start()
    return copies


def back_kernel(pairs, edges, stored, grad_ref, rim_ref, first_ref, last_ref, *refs):
    x_near, x_far = refs[:2] if edges else (None, None)
    w_ref = refs[2 * edges]
    out_hbm, *act_hbm, out, taps, around, sems = refs[-5 - stored :]
    copies = []
    if stored:
        copies = store_activation(*refs[1:3], act_hbm[0], sems.at[pl.ds(out.shape[0], 3)])
    size_y, width = grad_ref.shape[1:]
    size_x = grad_ref.shape[0] + 2
    tall = size_y + 2 * RIM

    def body(x):
        if x == 0:
            return first_ref[:size_y]
        if x == size_x - 1:
            return last_ref[:size_y]
        if x < 0 or x >= size_x:
            return around[int(x > 0), :size_y]
        return grad_ref[x - 1]

    def rim(x):
        if x == 0:
            return first_ref[size_y:tall]
        if x == size_x - 1:
            return last_ref[size_y:tall]
        if x < 0 or x >= size_x:
            return around[int(x > 0), size_y:tall]
        return rim_ref[x - 1]

    if edges:
        place_planes(x_near, x_far, around)
    narrow = w_ref[: 3 * width, : 3 * width]
    planes = [x for first in pairs for x in (first, first + 1)]
    planes += [0, size_x - 1] if edges else []
    rim_taps(taps, range(len(planes)), [[rim(x + j) for j in (-1, 0, 1)] for x in planes], narrow)
    stores = []

    def multiply(k):
        x = planes[k]
        if planes[k + 1] == x + 1:
            plane_taps(taps, (k, k + 1), [body(x + j) for j in (-1, 0, 1, 2)], w_ref[...])
        else:
            for i in (k, k + 1):
                plane_taps(taps, (i,), [body(planes[i] + j) for j in (-1, 0, 1)], narrow)

    multiply(0)
    for k in range(0, len(planes), 2):
        if k + 2 < len(planes):
            multiply(k + 2)
        for i in (k, k + 1):
            for y in range(0, size_y, CHUNK):
                out[i, y : y + CHUNK, :] = shifted_sum(taps, i, PAD + y, CHUNK).astype(BF16)
            stores.append(
                pltpu.make_async_copy(out.at[i], out_hbm.at[planes[i]], sems.at[i])
            )
            stores[-1].start()
    for copy in stores + copies:
        copy.wait()


def split_kernel(step, *refs):
    *terms, keep_ref, send_ref = refs
    total = sum_refs(terms)
    bit = (lax.axis_index("dp") // step) % 2

    def place(first, second):
        for k in range(keep_ref.shape[0]):
            keep_ref[k] = total[2 * k + first]
            send_ref[k] = total[2 * k + second].astype(BF16)

    pl.when(bit == 0)(lambda: place(0, 1))
    pl.when(bit == 1)(lambda: place(1, 0))


def sum_refs(terms):
    total = terms[0][...].astype(F32)
    for term in terms[1:]:
        total = total + term[...].astype(F32)
    return total


def add_kernel(*refs):
    *terms, total_ref = refs
    total_ref[...] = sum_refs(terms).astype(total_ref.dtype)


def finish_kernel(own, other, scale_ref, grad_ref, bias_ref):
    share, half = grad_ref.shape[1:]

    def emit(first, second):
        for s in range(SLOTS):
            block = (first if s < SLOTS // 2 else second)[s % (SLOTS // 2)] * scale_ref[s, :1]
            low, high = block[:, :half], pltpu.roll(block, half, 1)[:, :half]
            t = 2 * (s - 9)
            grad_ref[3 * s + 1 if s < 9 else 3 * t] = low.astype(BF16)
            if s < SLOTS - 1:
                grad_ref[3 * s + 2 if s < 9 else 3 * t + 3] = high.astype(BF16)
            else:
                bias_ref[...] = high[:1, :share]

    kept = half_kept()

    @pl.when(kept == 0)
    def _():
        emit(own, other)

    @pl.when(kept == 1)
    def _():
        emit(other, own)


def shape(*dims, dtype=BF16):
    return jax.ShapeDtypeStruct(dims, dtype)


def grant(mebibytes):
    return pltpu.CompilerParams(vmem_limit_bytes=mebibytes * 2**20)


def cost(microseconds):
    return pl.CostEstimate(
        flops=int(1.1e9 * microseconds), bytes_accessed=0, transcendentals=0
    )


def local(features, kernel, offsets, upstream, grad_exponents):
    cells, cotangent = features[0], upstream[0]
    size_x, size_y, width = cells.shape
    half = width // 2
    tall, rows = size_y + 2 * RIM, size_y + 2 * PAD
    parts = lax.axis_size("dp")
    share = half // parts
    sources = (cells, cotangent)
    ends = jnp.concatenate(
        [source[:, :THIN] for source in sources] + [source[:, size_y - THIN :] for source in sources],
        axis=1,
    )
    rim_near, rim_far = pl.pallas_call(
        rims_kernel,
        out_shape=(shape(size_x, 2 * THIN, width),) * 2,
        in_specs=[VMEM],
        out_specs=(VMEM, VMEM),
        compiler_params=grant(1),
        cost_estimate=cost(3.0),
        name="pack_rims",
    )(ends)
    y_near = swap(rim_near, "gy", 0)
    y_far = swap(rim_far, "gy", 1)

    voxels = (
        features.shape[0] * parts * size_x * lax.axis_size("gx") * size_y * lax.axis_size("gy") * 2
    )
    def back_weights(taps):
        return pl.pallas_call(
            lambda *refs: back_weights_kernel(1.0 / math.sqrt(voxels), *refs),
            out_shape=(shape(4 * width, 6 * width), shape(SLOTS, 8, width, dtype=F32)),
            in_specs=[VMEM, SMEM],
            out_specs=(VMEM, VMEM),
            compiler_params=grant(4),
            cost_estimate=cost(1.0),
            name="back_weights",
        )(taps, grad_exponents)

    inner = size_x - 2
    preact, turned, forward_weights, bias = pl.pallas_call(
        front_kernel,
        out_shape=(
            shape(inner, size_y, width, dtype=F32),
            shape(size_x, width, size_y),
            shape(3 * width, 3 * width),
            shape(1, width, dtype=F32),
        ),
        in_specs=[VMEM] * 3,
        out_specs=(VMEM,) * 4,
        scratch_shapes=[
            pltpu.VMEM((4 * width, 6 * width), BF16),
            pltpu.VMEM((3, inner, rows, width), F32),
        ],
        compiler_params=grant(16),
        cost_estimate=cost(2.0),
        name="front_planes",
    )(cells, kernel, offsets)

    many = lax.axis_size("gx") > 2
    plane_sends = pl.pallas_call(
        planes_kernel,
        out_shape=(shape(tall, width),) * (1 + many),
        in_specs=[VMEM] * 3,
        out_specs=(VMEM,) * (1 + many),
        compiler_params=grant(1),
        cost_estimate=cost(0.1),
        name="pack_planes",
    )(cells, y_near, y_far)
    x_near = swap(plane_sends[0], "gx", 0)
    x_far = swap(plane_sends[1], "gx", 1) if many else x_near

    rims = [
        pltpu.VMEM((size_x, 2 * RIM, width), BF16),
        pltpu.VMEM((size_x, 2 * RIM, width), BF16),
    ]
    act_inner, grad, grad_rim, acc, sums, part = pl.pallas_call(
        inner_kernel,
        out_shape=(
            shape(inner, size_y, width),
            shape(inner, size_y, width),
            shape(inner, 2 * RIM, width),
            shape(3 * width, 3 * width, dtype=F32),
            shape(8, width, dtype=F32),
            shape(2, size_y, 3 * width, dtype=F32),
        ),
        in_specs=[VMEM] * 8,
        out_specs=(VMEM,) * 6,
        scratch_shapes=rims + [
            pltpu.VMEM((inner, rows, width), F32),
            pltpu.VMEM((3 * width, 3 * width), F32),
        ],
        compiler_params=grant(12),
        cost_estimate=cost(3.0),
        name="inner_planes",
    )(cells, cotangent, y_near, y_far, preact, turned, forward_weights, bias)

    blocks = (parts // 2, SLOTS // 2, share, width)
    act_edges, first, final, acc, sums, send, *edges = pl.pallas_call(
        edge_kernel,
        out_shape=(
            shape(2, size_y, width),
            shape(tall, width),
            shape(tall, width),
            shape(3 * width, 3 * width, dtype=F32),
            shape(8, width, dtype=F32),
            shape(*blocks),
        )
        + (shape(tall, width),) * (1 + many),
        in_specs=[VMEM] * 11,
        out_specs=(VMEM,) * (7 + many),
        scratch_shapes=rims + [
            pltpu.VMEM((2, tall, width), BF16),
            pltpu.VMEM((3, 2, rows, width), F32),
            pltpu.VMEM((2, rows, width), F32),
        ],
        compiler_params=grant(12),
        cost_estimate=cost(2.0),
        name="edge_planes",
    )(
        cells, cotangent, y_near, y_far, x_near, x_far, forward_weights, bias, acc, sums, part,
    )

    def back(pairs, previous, after, beyond=(), acts=()):
        edges, stored = len(beyond) > 0, len(acts) > 0
        operands = [grad, grad_rim, first, final, *beyond, backward_weights, *acts]
        specs = [VMEM] * len(operands)
        aliases = {}
        if previous is not None:
            aliases = {len(operands): 0}
            operands.append(previous)
            specs.append(ANY)
        operands.append(after)
        specs.append(ANY)
        planes = 2 * len(pairs) + 2 * edges
        results = pl.pallas_call(
            lambda *refs: back_kernel(pairs, edges, stored, *refs),
            out_shape=(shape(size_x, size_y, width),) * (1 + stored),
            in_specs=specs,
            out_specs=(ANY,) * (1 + stored),
            scratch_shapes=[
                pltpu.VMEM((planes, size_y, width), BF16),
                pltpu.VMEM((3, planes, rows, width), F32),
                pltpu.VMEM((2, tall, width), BF16),
                pltpu.SemaphoreType.DMA((planes + 3 * stored,)),
            ],
            input_output_aliases=aliases,
            compiler_params=grant(12),
            cost_estimate=cost(2.5 if planes > 4 else 1.0),
            name="input_grad",
        )(*operands)
        return results if stored else results[0]

    starts = list(range(1, size_x - 1, 2))
    cut = len(starts) - 2
    def add(terms, dtype):
        return pl.pallas_call(
            add_kernel,
            out_shape=shape(*terms[0].shape, dtype=dtype),
            in_specs=[VMEM] * len(terms),
            out_specs=VMEM,
            compiler_params=grant(2),
            cost_estimate=cost(0.1),
            name="add_sums",
        )(*terms)

    def split(terms, step):
        dims = (terms[0].shape[0] // 2,) + terms[0].shape[1:]
        return pl.pallas_call(
            lambda *refs: split_kernel(step, *refs),
            out_shape=(shape(*dims, dtype=F32), shape(*dims)),
            in_specs=[VMEM] * len(terms),
            out_specs=(VMEM, VMEM),
            compiler_params=grant(2),
            cost_estimate=cost(0.1),
            name="split_sums",
        )(*terms)

    rounds = [("dp", 1 << i) for i in range(parts.bit_length() - 1)]
    rounds += [("gy", 1 << i) for i in range(1, lax.axis_size("gy").bit_length() - 1)]
    rounds += [("gx", 1 << i) for i in range(lax.axis_size("gx").bit_length() - 1)]
    away = swap(send, "gy", 0)
    send_stay, keep_away, keep_stay = pl.pallas_call(
        rest_kernel,
        out_shape=(shape(*blocks, dtype=F32),) * 3,
        in_specs=[VMEM, VMEM],
        out_specs=(VMEM,) * 3,
        compiler_params=grant(4),
        cost_estimate=cost(0.7),
        name="rest_of_sums",
    )(acc, sums)
    terms = [keep_stay, swap(send_stay, "gy", 0)]
    input_grad = None
    for index, (axis, step) in enumerate(rounds):
        if index == 0:
            send = add([keep_away, away], BF16)
        elif axis == "dp":
            total, send = split(terms, step)
            terms = [total]
        else:
            send = add(terms, BF16)
            terms = [send]
        if index == 0:
            later, send = lax.optimization_barrier((kernel, send))
            backward_weights, scales = back_weights(later)
        received = exchange(send, axis, step)
        if index == 0:
            input_grad = back(starts[:2], None, send)
            received, input_grad = lax.optimization_barrier((received, input_grad))
            *edges, backward_weights = lax.optimization_barrier((*edges, backward_weights))
            back_near = swap(edges[0], "gx", 0)
            back_far = swap(edges[1], "gx", 1) if many else back_near
        if index == len(rounds) - 2:
            input_grad, activation = back(
                starts[2:cut], input_grad, send, acts=(act_inner, act_edges)
            )
            received, input_grad = lax.optimization_barrier((received, input_grad))
        if index == len(rounds) - 1:
            input_grad = back(starts[cut:], input_grad, send, beyond=(back_near, back_far))
            received, input_grad = lax.optimization_barrier((received, input_grad))
        terms.append(received)
    total = add(terms, F32).reshape(SLOTS // 2, share, width)
    other = swap(total, "gy", 0)

    kernel_grad, bias_grad = pl.pallas_call(
        finish_kernel,
        out_shape=(shape(27, share, half), shape(1, share, dtype=F32)),
        in_specs=[VMEM] * 3,
        out_specs=(VMEM, VMEM),
        compiler_params=grant(4),
        name="scale_weight_grad",
    )(total, other, scales)
    return (
        activation[None],
        input_grad[None],
        jnp.swapaxes(kernel_grad.reshape(3, 3, 3, share, half), 3, 4),
        bias_grad.reshape(share),
    )


def solution(mesh):
    placed = (P("dp", "gx", "gy", None), P(), P(), P("dp", "gx", "gy", None), P())
    return jax.shard_map(
        local,
        mesh=mesh,
        in_specs=placed,
        out_specs=(
            P("dp", "gx", "gy", None),
            P("dp", "gx", "gy", None),
            P(None, None, None, None, "dp"),
            P("dp"),
        ),
        check_vma=False,
    )
```

```python
import math

import jax
import jax.numpy as jnp
from jax import lax
from jax.experimental import pallas as pl
from jax.experimental.pallas import tpu as pltpu
from jax.sharding import PartitionSpec as P

RIM = 8
THIN = 2
PAD = 16
CHUNK = 32
SLOTS = 14
VMEM = pl.BlockSpec(memory_space=pltpu.VMEM)
SMEM = pl.BlockSpec(memory_space=pltpu.SMEM)
ANY = pl.BlockSpec(memory_space=pl.ANY)
BF16, F32 = jnp.bfloat16, jnp.float32


def swap(value, axis, first):
    count = lax.axis_size(axis)
    links = []
    for low in range(first, count, 2):
        high = (low + 1) % count
        links += [(low, high), (high, low)]
    return lax.ppermute(value, axis, links)


def exchange(value, axis, step):
    axes = ("gx", "gy", "dp")
    sizes = [lax.axis_size(name) for name in axes]
    stride = {name: math.prod(sizes[i + 1 :]) for i, name in enumerate(axes)}
    flip = (step * stride[axis]) ^ stride["gy"]
    return lax.ppermute(value, axes, [(i, i ^ flip) for i in range(math.prod(sizes))])


def half_kept():
    side = lax.axis_index("gy") % 2
    for axis, first in (("gx", 1), ("gy", 2), ("dp", 1)):
        step = first
        while step < lax.axis_size(axis):
            side = side + lax.axis_index(axis) // step
            step *= 2
    return side % 2


def tap_block(taps, a, b):
    low, mid, high = taps[a, b, 0], taps[a, b, 1], taps[a, b, 2]
    return jnp.concatenate(
        [jnp.concatenate([mid, low], axis=1), jnp.concatenate([high, mid], axis=1)], axis=0
    )


def clear_corners(out, width):
    blank = jnp.zeros((width, 3 * width), BF16)
    out[3 * width :, : 3 * width] = blank
    out[:width, 3 * width :] = blank


def build_front(taps, w_ref, narrow_ref):
    width = 2 * taps.shape[3]
    clear_corners(w_ref, width)
    for a in range(3):
        for b in range(3):
            block = tap_block(taps, a, b)
            for k in range(2):
                row, col = (a + k) * width, (3 * k + b) * width
                w_ref[row : row + width, col : col + width] = block
            row, col = a * width, b * width
            narrow_ref[row : row + width, col : col + width] = block


def back_weights_kernel(inverse, taps, exponents, w_ref, scale_ref):
    half = taps.shape[3]
    width = 2 * half
    clear_corners(w_ref, width)
    for a in range(3):
        for b in range(3):
            turned = tap_block(taps, a, b).T
            for k in range(2):
                row, col = (2 - a + k) * width, (3 * k + 2 - b) * width
                w_ref[row : row + width, col : col + width] = turned
    lower = lax.broadcasted_iota(jnp.int32, (8, width), 1) < half

    def scale(t, c):
        power = lax.shift_left(jnp.int32(1), exponents[t // 3, t % 3, c] + 2)
        return power.astype(F32) * (0.25 * inverse)

    for s in range(SLOTS):
        t = 2 * (s - 9)
        if s < 9:
            low, high = scale(s, 1), scale(s, 2)
        else:
            low, high = scale(t, 0), scale(t + 1, 0) if t + 1 < 9 else inverse
        scale_ref[s] = jnp.where(lower, low, high)


def plane_taps(taps, slots, bodies, weights):
    size_y, width = bodies[0].shape
    result = jnp.dot(
        jnp.concatenate(bodies, axis=1), weights, preferred_element_type=F32
    )
    for k, p in enumerate(slots):
        for b in range(3):
            col = (3 * k + b) * width
            taps[b, p, PAD : PAD + size_y, :] = result[:, col : col + width]


def rim_taps(taps, slots, triples, weights):
    width = triples[0][0].shape[1]
    rows = 2 * RIM
    last = taps.shape[2] - PAD
    stacked = jnp.concatenate(
        [jnp.concatenate([triple[j] for triple in triples], axis=0) for j in range(3)], axis=1
    )
    result = jnp.dot(stacked, weights, preferred_element_type=F32)
    for k, p in enumerate(slots):
        for b in range(3):
            block = result[k * rows : (k + 1) * rows, b * width : (b + 1) * width]
            taps[b, p, PAD - RIM : PAD, :] = block[:RIM]
            taps[b, p, last : last + RIM, :] = block[RIM:]


def shifted_sum(taps, p, start, rows):
    return (
        taps[0, p, start - 1 : start - 1 + rows, :]
        + taps[1, p, start : start + rows, :]
        + taps[2, p, start + 1 : start + 1 + rows, :]
    )


def activate(taps, wide, p, bias, u_body, u_rim, act, grad_body, grad_rim):
    size_y = taps.shape[2] - 2 * PAD
    spans = [(PAD - RIM, RIM)]
    spans += [(PAD + y, CHUNK) for y in range(0, size_y, CHUNK)]
    spans += [(PAD + size_y, RIM)]
    for start, rows in spans:
        body = rows == CHUNK
        y = start - PAD if body else (0 if start < PAD else RIM)
        preact = shifted_sum(taps, p, start, rows) + bias
        sigma = 0.5 * jnp.tanh(0.5 * preact) + 0.5
        cotangent = (u_body if body else u_rim)[y : y + rows, :].astype(F32)
        rounded = (cotangent * sigma * (1.0 + preact * (1.0 - sigma))).astype(BF16)
        exact = rounded.astype(F32)
        wide[p, start : start + rows, :] = exact
        if body:
            act[y : y + rows, :] = (preact * sigma).astype(BF16)
            grad_body[y : y + rows, :] = rounded
        else:
            grad_rim[y : y + rows, :] = rounded


def body_sum(wide, p):
    size_y, width = wide.shape[1] - 2 * PAD, wide.shape[2]
    return jnp.sum(wide[p, PAD : PAD + size_y, :].reshape(size_y // 8, 8, width), axis=0)


def shifted_grads(wide, p):
    size_y = wide.shape[1] - 2 * PAD
    return jnp.concatenate(
        [wide[p, PAD + 1 - b : PAD + 1 - b + size_y, :].astype(BF16) for b in range(3)], axis=1
    )


def outer(sources, grads):
    return jnp.dot(
        jnp.concatenate([jnp.concatenate(three, axis=0) for three in sources], axis=1),
        jnp.concatenate(grads, axis=0),
        preferred_element_type=F32,
    )


def outer_turned(bodies, grads):
    return lax.dot_general(
        jnp.concatenate(grads, axis=0),
        jnp.concatenate([jnp.concatenate(three, axis=1) for three in bodies], axis=0),
        (((0,), (0,)), ((), ())),
        preferred_element_type=F32,
    )


def oriented(near, far, side, place):
    @pl.when(side == 0)
    def _():
        place(far, near)

    @pl.when(side == 1)
    def _():
        place(near, far)


def beside(axis, near, far, place, clear_low, clear_high):
    index = lax.axis_index(axis)
    oriented(near, far, index % 2, place)
    pl.when(index == 0)(clear_low)
    pl.when(index == lax.axis_size(axis) - 1)(clear_high)


def place_rims(y_near, y_far, f_rim, u_rim, gap):
    low = slice(gap, gap + THIN)
    high = slice(2 * RIM - gap - THIN, 2 * RIM - gap)

    def place(left, right):
        f_rim[:, low, :] = left[:, :THIN, :]
        u_rim[:, low, :] = left[:, THIN:, :]
        f_rim[:, high, :] = right[:, :THIN, :]
        u_rim[:, high, :] = right[:, THIN:, :]

    def clear(rows):
        blank = jnp.zeros((f_rim.shape[0], THIN, f_rim.shape[2]), BF16)
        f_rim[:, rows, :] = blank
        u_rim[:, rows, :] = blank

    for ref in (f_rim, u_rim):
        ref[...] = jnp.zeros(ref.shape, BF16)
    beside("gy", y_near, y_far, place, lambda: clear(low), lambda: clear(high))


def place_planes(x_near, x_far, around):
    def place(below, above):
        around[0] = below[...]
        around[1] = above[...]

    def clear(k):
        around[k] = jnp.zeros(around.shape[1:], BF16)

    beside("gx", x_near, x_far, place, lambda: clear(0), lambda: clear(1))


def rims_kernel(ends, near_ref, far_ref):
    rows = ends.shape[1] // 2

    def hand(tail, head):
        tail[...] = ends[:, rows:, :]
        head[...] = ends[:, :rows, :]

    oriented(far_ref, near_ref, lax.axis_index("gy") % 2, hand)


def planes_kernel(f_ref, y_near, y_far, near_ref, far_ref=None):
    size_x, size_y, width = f_ref.shape
    low = slice(size_y + RIM - THIN, size_y + RIM)
    high = slice(size_y + RIM, size_y + RIM + THIN)

    def fill(out, x):
        out[:size_y] = f_ref[x]
        out[size_y:] = jnp.zeros((2 * RIM, width), BF16)

        def place(left, right):
            out[low] = left[x, :THIN]
            out[high] = right[x, :THIN]

        def clear(rows):
            out[rows] = jnp.zeros((THIN, width), BF16)

        beside("gy", y_near, y_far, place, lambda: clear(low), lambda: clear(high))

    def hand(last, first):
        if last is not None:
            fill(last, size_x - 1)
        if first is not None:
            fill(first, 0)

    oriented(far_ref, near_ref, lax.axis_index("gx") % 2, hand)


def front_kernel(
    f_ref, kernel_ref, offsets, pre_ref, turned, narrow_ref, bias_ref, w_ref, taps
):
    size_x, size_y, width = f_ref.shape
    inner = size_x - 2
    build_front(kernel_ref, w_ref, narrow_ref)
    bias = offsets[...].reshape(1, width // 2)
    bias = jnp.concatenate([bias, bias], axis=1)
    bias_ref[...] = bias
    blank = jnp.zeros((3, inner, RIM, width), F32)
    taps[:, :, PAD - RIM : PAD, :] = blank
    taps[:, :, PAD + size_y : PAD + size_y + RIM, :] = blank
    for p in range(0, inner, 2):
        plane_taps(taps, (p, p + 1), [f_ref[p + j] for j in range(4)], w_ref[...])
        for x in range(0 if p == 0 else p + 2, p + 4):
            turned[x] = f_ref[x].T
        for q in (p, p + 1):
            for y in range(0, size_y, CHUNK):
                pre_ref[q, y : y + CHUNK, :] = shifted_sum(taps, q, PAD + y, CHUNK) + bias


def gradient(preact, cotangent):
    sigma = 0.5 * jnp.tanh(0.5 * preact) + 0.5
    rounded = (
        cotangent.astype(F32) * sigma * (1.0 + preact * (1.0 - sigma))
    ).astype(BF16)
    return preact * sigma, rounded, rounded.astype(F32)


def inner_kernel(
    f_ref, u_ref, y_near, y_far, pre_ref, turned, w_ref, bias_ref,
    act, grad_ref, rim_ref, acc_ref, sums_ref, part_ref,
    f_rim, u_rim, wide, acc,
):
    size_x, size_y, width = f_ref.shape
    inner = size_x - 2
    gap = RIM - 2 * THIN

    place_rims(y_near, y_far, f_rim, u_rim, gap)
    f_rim[:, gap + THIN : RIM, :] = f_ref[:, :THIN, :]
    f_rim[:, RIM : RIM + THIN, :] = f_ref[:, size_y - THIN :, :]
    for p, (x, row) in enumerate(((0, width), (size_x - 2, 0))):
        part_ref[p] = jnp.dot(
            jnp.concatenate([f_ref[x], f_ref[x + 1]], axis=1),
            w_ref[row : row + 2 * width, :],
            preferred_element_type=F32,
        )
    bias = bias_ref[...]
    rows = 2 * RIM
    tall = [
        jnp.concatenate([f_rim[x + j] for x in range(inner)], axis=0) for j in range(3)
    ]
    strips = jnp.dot(
        jnp.concatenate(tall, axis=1), w_ref[...], preferred_element_type=F32
    )
    row = lax.broadcasted_iota(jnp.int32, (RIM, width), 0)
    sums = jnp.zeros((8, width), F32)
    for p in range(0, inner, 2):
        for q in (p, p + 1):
            strip = [
                strips[q * rows : (q + 1) * rows, b * width : (b + 1) * width] for b in range(3)
            ]
            for side in range(2):
                part = [tap[side * RIM : (side + 1) * RIM] for tap in strip]
                preact = (
                    pltpu.roll(part[0], 1, 0) + part[1] + pltpu.roll(part[2], RIM - 1, 0) + bias
                )
                _, rounded, exact = gradient(
                    preact, u_rim[q + 1, side * RIM : (side + 1) * RIM, :]
                )
                turn = THIN if side == 0 else RIM - THIN
                exact = pltpu.roll(exact, turn, 0)
                start = PAD - RIM if side == 0 else PAD + size_y
                wide[q, start : start + RIM, :] = exact
                rim_ref[q, side * RIM : (side + 1) * RIM, :] = exact.astype(BF16)
            low = jnp.where(row == 0, pltpu.roll(strip[0][:RIM], RIM - gap - THIN + 1, 0), 0.0)
            high = jnp.where(
                row == RIM - 1, pltpu.roll(strip[2][RIM:], RIM - 1 - THIN, 0), 0.0
            )
            for y in range(0, size_y, CHUNK):
                preact = pre_ref[q, y : y + CHUNK, :]
                if y == 0:
                    preact = jnp.concatenate([preact[:RIM] + low, preact[RIM:]], axis=0)
                if y + CHUNK == size_y:
                    preact = jnp.concatenate([preact[:-RIM], preact[-RIM:] + high], axis=0)
                value, rounded, exact = gradient(preact, u_ref[q + 1, y : y + CHUNK, :])
                wide[q, PAD + y : PAD + y + CHUNK, :] = exact
                act[q, y : y + CHUNK, :] = value.astype(BF16)
                grad_ref[q, y : y + CHUNK, :] = rounded
        grads = [shifted_grads(wide, q) for q in (p, p + 1)]
        sums = sums + body_sum(wide, p) + body_sum(wide, p + 1)
        if p < inner - 2:
            term = outer([[turned[q + j] for j in range(3)] for q in (p, p + 1)], grads)
            if p == 0:
                acc[...] = term
            else:
                acc[...] += term
        if p == inner - 4:
            for a in range(3):
                for b in range(3):
                    here, there = slice(a * width, (a + 1) * width), slice(b * width, (b + 1) * width)
                    acc_ref[there, here] = acc[here, there].T
        if p == inner - 2:
            acc_ref[...] += outer_turned(
                [[f_ref[q + j] for j in range(3)] for q in (p, p + 1)], grads
            )
    sums_ref[...] = sums


def emit_half(acc, sums, which, away, stay):
    outs = [out for out in (away, stay) if out is not None]
    blocks, count, share, width = outs[0].shape
    half = width // 2

    def block(t):
        a, b = t // 3, t % 3
        return acc[b * width : (b + 1) * width, a * width : (a + 1) * width]

    def lower(rows):
        return lax.broadcasted_iota(jnp.int32, (rows, width), 1) < half

    def middle(t):
        whole = block(t)
        rolled = pltpu.roll(whole[half:], half, 1)
        return whole[:half] + jnp.where(lower(half), rolled, 0.0)

    def low_pair(t):
        low = block(t)[half:]
        if t + 1 < 9:
            return jnp.where(lower(half), low, pltpu.roll(block(t + 1)[half:], half, 1))
        both = jnp.sum(sums, axis=0, keepdims=True)
        both = jnp.broadcast_to(both + pltpu.roll(both, half, 1), (share, width))
        turned = [
            pltpu.roll(both, (half - d * share) % width, 1) for d in range(2 * blocks)
        ]
        return jnp.where(lower(half), low, jnp.concatenate(turned, axis=0))

    def write(bit):
        def put(s, value):
            for k in range(blocks):
                for out, d in ((away, 2 * k + 1 - bit), (stay, 2 * k + bit)):
                    if out is not None:
                        out[k, s] = value[d * share : (d + 1) * share].astype(out.dtype)

        @pl.when(which == 0)
        def _():
            for s in range(count):
                put(s, middle(s))

        @pl.when(which == 1)
        def _():
            for t in range(count, 9):
                put(t - count, middle(t))
            for t in range(0, 9, 2):
                put(9 + t // 2 - count, low_pair(t))

    place = lax.axis_index("dp") % 2
    pl.when(place == 0)(lambda: write(0))
    pl.when(place == 1)(lambda: write(1))


def rest_kernel(acc, sums, send_stay, keep_away, keep_stay):
    kept = half_kept()
    emit_half(acc, sums[...], 1 - kept, None, send_stay)
    emit_half(acc, sums[...], kept, keep_away, keep_stay)


def edge_kernel(
    f_ref, u_ref, y_near, y_far, x_near, x_far, w_ref, bias_ref, acc_ref, sums_ref,
    part_ref, act, first_ref, last_ref, acc, bias_sums, send_ref, near_ref, *refs
):
    far_ref = refs[0] if len(refs) > 5 else None
    f_rim, u_rim, around, taps, wide = refs[-5:]
    size_x, size_y, width = f_ref.shape
    x_side = lax.axis_index("gx") % 2
    place_rims(y_near, y_far, f_rim, u_rim, RIM - THIN)
    place_planes(x_near, x_far, around)
    bias = bias_ref[...]
    weights = w_ref[...]
    tall = size_y + 2 * RIM
    bodies = [
        [around[0, :size_y], f_ref[0], f_ref[1]],
        [f_ref[size_x - 2], f_ref[size_x - 1], around[1, :size_y]],
    ]
    rims = [
        [around[0, size_y:tall], f_rim[0], f_rim[1]],
        [f_rim[size_x - 2], f_rim[size_x - 1], around[1, size_y:tall]],
    ]
    rim_taps(taps, (0, 1), rims, weights)
    for p in range(2):
        row = 2 * p * width
        result = part_ref[p] + jnp.dot(
            around[p, :size_y], weights[row : row + width], preferred_element_type=F32
        )
        for b in range(3):
            taps[b, p, PAD : PAD + size_y, :] = result[:, b * width : (b + 1) * width]
    outs = (first_ref, last_ref)
    places = (0, size_x - 1)
    for p in range(2):
        x = places[p]
        activate(
            taps, wide, p, bias, u_ref.at[x], u_rim.at[x], act.at[p],
            outs[p].at[pl.ds(0, size_y)], outs[p].at[pl.ds(size_y, 2 * RIM)],
        )
    acc[...] = acc_ref[...] + outer_turned(bodies, [shifted_grads(wide, p) for p in range(2)])
    sums = sums_ref[...] + body_sum(wide, 0) + body_sum(wide, 1)

    def hand(last, first):
        if last is not None:
            last[...] = last_ref[...]
        if first is not None:
            first[...] = first_ref[...]

    oriented(far_ref, near_ref, x_side, hand)

    bias_sums[...] = sums
    emit_half(acc, sums, 1 - half_kept(), send_ref, None)


def store_activation(act_inner, act_edges, act_hbm, sems):
    size_x = act_hbm.shape[0]
    copies = [
        pltpu.make_async_copy(act_edges.at[0], act_hbm.at[0], sems.at[0]),
        pltpu.make_async_copy(act_edges.at[1], act_hbm.at[size_x - 1], sems.at[1]),
        pltpu.make_async_copy(act_inner, act_hbm.at[pl.ds(1, size_x - 2)], sems.at[2]),
    ]
    for copy in copies:
        copy.start()
    return copies


def back_kernel(pairs, edges, stored, grad_ref, rim_ref, first_ref, last_ref, *refs):
    x_near, x_far = refs[:2] if edges else (None, None)
    w_ref = refs[2 * edges]
    out_hbm, *act_hbm, out, taps, around, sems = refs[-5 - stored :]
    copies = []
    if stored:
        copies = store_activation(*refs[1:3], act_hbm[0], sems.at[pl.ds(out.shape[0], 3)])
    size_y, width = grad_ref.shape[1:]
    size_x = grad_ref.shape[0] + 2
    tall = size_y + 2 * RIM

    def body(x):
        if x == 0:
            return first_ref[:size_y]
        if x == size_x - 1:
            return last_ref[:size_y]
        if x < 0 or x >= size_x:
            return around[int(x > 0), :size_y]
        return grad_ref[x - 1]

    def rim(x):
        if x == 0:
            return first_ref[size_y:tall]
        if x == size_x - 1:
            return last_ref[size_y:tall]
        if x < 0 or x >= size_x:
            return around[int(x > 0), size_y:tall]
        return rim_ref[x - 1]

    if edges:
        place_planes(x_near, x_far, around)
    narrow = w_ref[: 3 * width, : 3 * width]
    planes = [x for first in pairs for x in (first, first + 1)]
    planes += [0, size_x - 1] if edges else []
    rim_taps(taps, range(len(planes)), [[rim(x + j) for j in (-1, 0, 1)] for x in planes], narrow)
    stores = []

    def multiply(k):
        x = planes[k]
        if planes[k + 1] == x + 1:
            plane_taps(taps, (k, k + 1), [body(x + j) for j in (-1, 0, 1, 2)], w_ref[...])
        else:
            for i in (k, k + 1):
                plane_taps(taps, (i,), [body(planes[i] + j) for j in (-1, 0, 1)], narrow)

    multiply(0)
    for k in range(0, len(planes), 2):
        if k + 2 < len(planes):
            multiply(k + 2)
        for i in (k, k + 1):
            for y in range(0, size_y, CHUNK):
                out[i, y : y + CHUNK, :] = shifted_sum(taps, i, PAD + y, CHUNK).astype(BF16)
            stores.append(
                pltpu.make_async_copy(out.at[i], out_hbm.at[planes[i]], sems.at[i])
            )
            stores[-1].start()
    for copy in stores + copies:
        copy.wait()


def split_kernel(step, *refs):
    *terms, keep_ref, send_ref = refs
    total = sum_refs(terms)
    bit = (lax.axis_index("dp") // step) % 2

    def place(first, second):
        for k in range(keep_ref.shape[0]):
            keep_ref[k] = total[2 * k + first]
            send_ref[k] = total[2 * k + second].astype(BF16)

    pl.when(bit == 0)(lambda: place(0, 1))
    pl.when(bit == 1)(lambda: place(1, 0))


def sum_refs(terms):
    total = terms[0][...].astype(F32)
    for term in terms[1:]:
        total = total + term[...].astype(F32)
    return total


def add_kernel(*refs):
    *terms, total_ref = refs
    total_ref[...] = sum_refs(terms).astype(total_ref.dtype)


def finish_kernel(own, other, scale_ref, grad_ref, bias_ref):
    share, half = grad_ref.shape[1:]

    def emit(first, second):
        for s in range(SLOTS):
            block = (first if s < SLOTS // 2 else second)[s % (SLOTS // 2)] * scale_ref[s, :1]
            low, high = block[:, :half], pltpu.roll(block, half, 1)[:, :half]
            t = 2 * (s - 9)
            grad_ref[3 * s + 1 if s < 9 else 3 * t] = low.astype(BF16)
            if s < SLOTS - 1:
                grad_ref[3 * s + 2 if s < 9 else 3 * t + 3] = high.astype(BF16)
            else:
                bias_ref[...] = high[:1, :share]

    kept = half_kept()

    @pl.when(kept == 0)
    def _():
        emit(own, other)

    @pl.when(kept == 1)
    def _():
        emit(other, own)


def shape(*dims, dtype=BF16):
    return jax.ShapeDtypeStruct(dims, dtype)


def grant(mebibytes):
    return pltpu.CompilerParams(vmem_limit_bytes=mebibytes * 2**20)


def cost(microseconds):
    return pl.CostEstimate(
        flops=int(1.1e9 * microseconds), bytes_accessed=0, transcendentals=0
    )


def local(features, kernel, offsets, upstream, grad_exponents):
    cells, cotangent = features[0], upstream[0]
    size_x, size_y, width = cells.shape
    half = width // 2
    tall, rows = size_y + 2 * RIM, size_y + 2 * PAD
    parts = lax.axis_size("dp")
    share = half // parts
    sources = (cells, cotangent)
    ends = jnp.concatenate(
        [source[:, :THIN] for source in sources] + [source[:, size_y - THIN :] for source in sources],
        axis=1,
    )
    rim_near, rim_far = pl.pallas_call(
        rims_kernel,
        out_shape=(shape(size_x, 2 * THIN, width),) * 2,
        in_specs=[VMEM],
        out_specs=(VMEM, VMEM),
        compiler_params=grant(1),
        cost_estimate=cost(3.0),
        name="pack_rims",
    )(ends)
    y_near = swap(rim_near, "gy", 0)
    y_far = swap(rim_far, "gy", 1)

    voxels = (
        features.shape[0] * parts * size_x * lax.axis_size("gx") * size_y * lax.axis_size("gy") * 2
    )
    def back_weights(taps):
        return pl.pallas_call(
            lambda *refs: back_weights_kernel(1.0 / math.sqrt(voxels), *refs),
            out_shape=(shape(4 * width, 6 * width), shape(SLOTS, 8, width, dtype=F32)),
            in_specs=[VMEM, SMEM],
            out_specs=(VMEM, VMEM),
            compiler_params=grant(4),
            cost_estimate=cost(1.0),
            name="back_weights",
        )(taps, grad_exponents)

    inner = size_x - 2
    preact, turned, forward_weights, bias = pl.pallas_call(
        front_kernel,
        out_shape=(
            shape(inner, size_y, width, dtype=F32),
            shape(size_x, width, size_y),
            shape(3 * width, 3 * width),
            shape(1, width, dtype=F32),
        ),
        in_specs=[VMEM] * 3,
        out_specs=(VMEM,) * 4,
        scratch_shapes=[
            pltpu.VMEM((4 * width, 6 * width), BF16),
            pltpu.VMEM((3, inner, rows, width), F32),
        ],
        compiler_params=grant(16),
        cost_estimate=cost(2.0),
        name="front_planes",
    )(cells, kernel, offsets)

    many = lax.axis_size("gx") > 2
    plane_sends = pl.pallas_call(
        planes_kernel,
        out_shape=(shape(tall, width),) * (1 + many),
        in_specs=[VMEM] * 3,
        out_specs=(VMEM,) * (1 + many),
        compiler_params=grant(1),
        cost_estimate=cost(0.1),
        name="pack_planes",
    )(cells, y_near, y_far)
    x_near = swap(plane_sends[0], "gx", 0)
    x_far = swap(plane_sends[1], "gx", 1) if many else x_near

    rims = [
        pltpu.VMEM((size_x, 2 * RIM, width), BF16),
        pltpu.VMEM((size_x, 2 * RIM, width), BF16),
    ]
    act_inner, grad, grad_rim, acc, sums, part = pl.pallas_call(
        inner_kernel,
        out_shape=(
            shape(inner, size_y, width),
            shape(inner, size_y, width),
            shape(inner, 2 * RIM, width),
            shape(3 * width, 3 * width, dtype=F32),
            shape(8, width, dtype=F32),
            shape(2, size_y, 3 * width, dtype=F32),
        ),
        in_specs=[VMEM] * 8,
        out_specs=(VMEM,) * 6,
        scratch_shapes=rims + [
            pltpu.VMEM((inner, rows, width), F32),
            pltpu.VMEM((3 * width, 3 * width), F32),
        ],
        compiler_params=grant(12),
        cost_estimate=cost(3.0),
        name="inner_planes",
    )(cells, cotangent, y_near, y_far, preact, turned, forward_weights, bias)

    blocks = (parts // 2, SLOTS // 2, share, width)
    act_edges, first, final, acc, sums, send, *edges = pl.pallas_call(
        edge_kernel,
        out_shape=(
            shape(2, size_y, width),
            shape(tall, width),
            shape(tall, width),
            shape(3 * width, 3 * width, dtype=F32),
            shape(8, width, dtype=F32),
            shape(*blocks),
        )
        + (shape(tall, width),) * (1 + many),
        in_specs=[VMEM] * 11,
        out_specs=(VMEM,) * (7 + many),
        scratch_shapes=rims + [
            pltpu.VMEM((2, tall, width), BF16),
            pltpu.VMEM((3, 2, rows, width), F32),
            pltpu.VMEM((2, rows, width), F32),
        ],
        compiler_params=grant(12),
        cost_estimate=cost(2.0),
        name="edge_planes",
    )(
        cells, cotangent, y_near, y_far, x_near, x_far, forward_weights, bias, acc, sums, part,
    )

    def back(pairs, previous, after, beyond=(), acts=()):
        edges, stored = len(beyond) > 0, len(acts) > 0
        operands = [grad, grad_rim, first, final, *beyond, backward_weights, *acts]
        specs = [VMEM] * len(operands)
        aliases = {}
        if previous is not None:
            aliases = {len(operands): 0}
            operands.append(previous)
            specs.append(ANY)
        operands.append(after)
        specs.append(ANY)
        planes = 2 * len(pairs) + 2 * edges
        results = pl.pallas_call(
            lambda *refs: back_kernel(pairs, edges, stored, *refs),
            out_shape=(shape(size_x, size_y, width),) * (1 + stored),
            in_specs=specs,
            out_specs=(ANY,) * (1 + stored),
            scratch_shapes=[
                pltpu.VMEM((planes, size_y, width), BF16),
                pltpu.VMEM((3, planes, rows, width), F32),
                pltpu.VMEM((2, tall, width), BF16),
                pltpu.SemaphoreType.DMA((planes + 3 * stored,)),
            ],
            input_output_aliases=aliases,
            compiler_params=grant(12),
            cost_estimate=cost(2.5 if planes > 4 else 1.0),
            name="input_grad",
        )(*operands)
        return results if stored else results[0]

    starts = list(range(1, size_x - 1, 2))
    cut = len(starts) - 2
    def add(terms, dtype):
        return pl.pallas_call(
            add_kernel,
            out_shape=shape(*terms[0].shape, dtype=dtype),
            in_specs=[VMEM] * len(terms),
            out_specs=VMEM,
            compiler_params=grant(2),
            cost_estimate=cost(0.1),
            name="add_sums",
        )(*terms)

    def split(terms, step):
        dims = (terms[0].shape[0] // 2,) + terms[0].shape[1:]
        return pl.pallas_call(
            lambda *refs: split_kernel(step, *refs),
            out_shape=(shape(*dims, dtype=F32), shape(*dims)),
            in_specs=[VMEM] * len(terms),
            out_specs=(VMEM, VMEM),
            compiler_params=grant(2),
            cost_estimate=cost(0.1),
            name="split_sums",
        )(*terms)

    rounds = [("dp", 1 << i) for i in range(parts.bit_length() - 1)]
    rounds += [("gy", 1 << i) for i in range(1, lax.axis_size("gy").bit_length() - 1)]
    rounds += [("gx", 1 << i) for i in range(lax.axis_size("gx").bit_length() - 1)]
    away = swap(send, "gy", 0)
    send_stay, keep_away, keep_stay = pl.pallas_call(
        rest_kernel,
        out_shape=(shape(*blocks, dtype=F32),) * 3,
        in_specs=[VMEM, VMEM],
        out_specs=(VMEM,) * 3,
        compiler_params=grant(4),
        cost_estimate=cost(0.7),
        name="rest_of_sums",
    )(acc, sums)
    terms = [keep_stay, swap(send_stay, "gy", 0)]
    input_grad = None
    for index, (axis, step) in enumerate(rounds):
        if index == 0:
            send = add([keep_away, away], BF16)
        elif axis == "dp":
            total, send = split(terms, step)
            terms = [total]
        else:
            send = add(terms, BF16)
            terms = [send]
        if index == 0:
            later, send = lax.optimization_barrier((kernel, send))
            backward_weights, scales = back_weights(later)
        received = exchange(send, axis, step)
        if index == 0:
            input_grad = back(starts[:2], None, send)
            received, input_grad = lax.optimization_barrier((received, input_grad))
            *edges, backward_weights = lax.optimization_barrier((*edges, backward_weights))
            back_near = swap(edges[0], "gx", 0)
            back_far = swap(edges[1], "gx", 1) if many else back_near
        if index == len(rounds) - 2:
            input_grad, activation = back(
                starts[2:cut], input_grad, send, acts=(act_inner, act_edges)
            )
            received, input_grad = lax.optimization_barrier((received, input_grad))
        if index == len(rounds) - 1:
            input_grad = back(starts[cut:], input_grad, send, beyond=(back_near, back_far))
            received, input_grad = lax.optimization_barrier((received, input_grad))
        terms.append(received)
    total = add(terms, F32).reshape(SLOTS // 2, share, width)
    other = swap(total, "gy", 0)

    kernel_grad, bias_grad = pl.pallas_call(
        finish_kernel,
        out_shape=(shape(27, share, half), shape(1, share, dtype=F32)),
        in_specs=[VMEM] * 3,
        out_specs=(VMEM, VMEM),
        compiler_params=grant(4),
        name="scale_weight_grad",
    )(total, other, scales)
    return (
        activation[None],
        input_grad[None],
        jnp.swapaxes(kernel_grad.reshape(3, 3, 3, share, half), 3, 4),
        bias_grad.reshape(share),
    )


def solution(mesh):
    placed = (P("dp", "gx", "gy", None), P(), P(), P("dp", "gx", "gy", None), P())
    return jax.shard_map(
        local,
        mesh=mesh,
        in_specs=placed,
        out_specs=(
            P("dp", "gx", "gy", None),
            P("dp", "gx", "gy", None),
            P(None, None, None, None, "dp"),
            P("dp"),
        ),
        check_vma=False,
    )
```
